256 devices in a mesh: op: 16 (over z, core), sec: 16 (over y, x).
Axes of the slice: x: 4, y: 4, z: 8, core: 2. Of those that a mesh axis runs over, the one named last changes fastest.
Arguments:
- wavefunction: bfloat16 [64, 2, 256, 256], P('sec'), may hold values from -6 to 6
- left_ops: bfloat16 [128, 64, 256, 256], P('op', 'sec'), may hold values from -1 to 1
- right_ops: bfloat16 [128, 64, 256, 256], P('op', 'sec'), may hold values from -1 to 1
- sources: int32 [128, 64], P('op'), may hold values from 0 to 63, as said below
- block_dims: int32 [64], P('sec'), may hold values from 128 to 256, as said below
- energies: float32 [64], P('sec'), may hold values from 1 to 4
Outputs:
- residual: float32 [256, 64, 2, 256], P('op', 'sec')
- rayleigh: float32 [2], replicated
The draws below stay inside these ranges and needn't reach their ends.
Inputs may be any that keep to these rules, and one draw needn't show every extreme that they name: `sources`: for every op index and sec index, at most 3 of the 8 x 4 pairs (operator of that op index, target sector of that sec index) have a source sector on one sec index, and exactly 3 on some sec index. `block_dims`: some sector has the full size 256.
All inputs are finite; a program needn't handle non-finite values.
Results may differ from the reference program's by a relative error of at most 0.0019.
Values may be sent and summed in bfloat16 or wider, within the bound.
No kernel may reach another device: no remote copies, remote signals or barrier semaphores. Data moves between devices by JAX's collectives and lax.ppermute only.
A program may use at most 128 MiB of HBM per device.

```python
import math
import jax
import jax.numpy as jnp
from jax import lax

TILE = 256
NV = 2
OD = 8
SD = 4
OPS = 128
SECTORS = 64


def draw_sources(key, part):
    key = jax.random.fold_in(key, 11)
    pair_count = OD * SD
    sec_count = SECTORS // SD
    group_count = OPS // OD
    average = pair_count // sec_count

    def one_block(block_key):
        first_key, second_key, third_key = jax.random.split(block_key, 3)
        order = jax.random.permutation(first_key, sec_count)
        hottest = order[0]
        coldest = order[1]
        base = jnp.repeat(jnp.arange(sec_count, dtype=jnp.int32), average)
        base = base.at[coldest * average].set(hottest)
        devices = jax.random.permutation(second_key, base)
        within = jax.random.randint(third_key, (pair_count,), 0, SD, dtype=jnp.int32)
        return devices * SD + within
    blocks = jax.vmap(one_block)(jax.random.split(key, group_count * sec_count))
    blocks = blocks.reshape(group_count, sec_count, OD, SD)
    return jnp.transpose(blocks, (0, 2, 1, 3)).reshape(OPS, SECTORS).astype(jnp.int32)


def draw_block_dims(key, part):
    key = jax.random.fold_in(key, 12)
    first_key, second_key = jax.random.split(key)
    sizes = jax.random.randint(first_key, (SECTORS,), TILE // 2, TILE + 1, dtype=jnp.int32)
    where = jax.random.randint(second_key, (), 0, SECTORS, dtype=jnp.int32)
    return sizes.at[where].set(TILE).astype(jnp.int32)


def draw_wavefunction(key, part):
    key = jax.random.fold_in(key, 13)
    base_key, own_key = jax.random.split(key, 2)
    shape = (SECTORS, NV, TILE, TILE)
    common = jax.random.normal(base_key, (1, NV, TILE, TILE), jnp.float32)
    own = jax.random.normal(own_key, shape, jnp.float32)
    values = 0.7 * common + 0.7 * own
    return jnp.clip(values, -6.0, 6.0).astype(jnp.bfloat16)


def operator_blocks(key, width, diag_lo, diag_hi):
    noise_key, diag_key = jax.random.split(key)
    shape = (OPS, SECTORS, TILE, TILE)
    noise = jnp.clip(jax.random.normal(noise_key, shape, jnp.float32), -4.0, 4.0)
    diag = jax.random.uniform(diag_key, (OPS, SECTORS, 1, 1), jnp.float32, diag_lo, diag_hi)
    index = jnp.arange(TILE, dtype=jnp.int32)
    eye = (index[:, None] == index[None, :]).astype(jnp.float32)
    return jnp.clip(noise * width + diag * eye, -1.0, 1.0).astype(jnp.bfloat16)


def draw_left_ops(key, part):
    key = jax.random.fold_in(key, 14)
    return operator_blocks(key, TILE ** (-0.5), 0.15, 0.35)


def draw_right_ops(key, part):
    key = jax.random.fold_in(key, 15)
    return operator_blocks(key, (TILE * OPS) ** (-0.5), 1.2 / OPS, 3.6 / OPS)


def levels(key, shape, cuts, least, largest):
    def one(axis_at, blocks):
        draws = jax.random.uniform(jax.random.fold_in(jax.random.fold_in(key, 6), axis_at), (blocks,), jnp.float32, least / len(cuts), largest / len(cuts))
        return jnp.repeat(jnp.exp(draws), shape[axis_at] // blocks).reshape((-1,) + (1,) * (len(shape) - axis_at - 1))

    level = one(*cuts[0])
    for cut in cuts[1:]:
        level = level * one(*cut)
    return level


def setup_inputs(seed: int = 0) -> dict:
    keys = jax.random.split(jax.random.key(seed), 7)
    return {
        "wavefunction": draw_wavefunction(jax.random.fold_in(keys[6], 71), 0),
        "left_ops": draw_left_ops(jax.random.fold_in(keys[6], 71), 0),
        "right_ops": draw_right_ops(jax.random.fold_in(keys[6], 71), 0),
        "sources": draw_sources(jax.random.fold_in(keys[6], 71), 0),
        "block_dims": draw_block_dims(jax.random.fold_in(keys[6], 71), 0),
        "energies": jnp.clip(jnp.exp(math.log(4.0) - 1.3862944 * jax.random.uniform(keys[5], (SECTORS,), jnp.float32) ** levels(keys[5], (SECTORS,), ((0, 16),), -0.2, 0.2)), 1.0, 4.0),
    }


def reference(wavefunction, left_ops, right_ops, sources, block_dims, energies):
    live = jnp.arange(TILE, dtype=jnp.int32)[None, :] < block_dims[:, None]
    window = live[:, None, :, None] & live[:, None, None, :]
    masked = wavefunction * window.astype(jnp.bfloat16)
    masked_wide = masked.astype(jnp.float32)

    def per_target(target):
        blocks = jnp.take(masked, sources[:, target], axis=0).astype(jnp.float32)
        lefts = left_ops[:, target].astype(jnp.float32)
        rights = right_ops[:, target].astype(jnp.float32)
        inner = jnp.einsum("kab,kvbc->kvac", lefts, blocks)
        inner = lax.optimization_barrier(inner.astype(jnp.bfloat16)).astype(jnp.float32)
        return jnp.einsum("kvac,kdc->vad", inner, rights)

    sums = lax.map(per_target, jnp.arange(SECTORS, dtype=jnp.int32))
    sigma = (sums + energies[:, None, None, None] * masked_wide) * window.astype(jnp.float32)
    numer = jnp.sum(masked_wide * sigma, axis=(0, 2, 3))
    denom = jnp.sum(masked_wide * masked_wide, axis=(0, 2, 3))
    rayleigh = numer / denom
    residual = sigma - rayleigh[None, :, None, None] * masked_wide
    return jnp.transpose(residual, (2, 0, 1, 3)), rayleigh
```

```python
import jax
import jax.numpy as jnp
from jax import lax
from jax.experimental import pallas as pl
from jax.experimental.pallas import tpu as pltpu
from jax.sharding import PartitionSpec as P


def sigma_kernel(src, vec, own, left_a, left_b, right_a, right_b, out, dots, acc):
    t = pl.program_id(0)
    half = left_a.shape[0]
    tile = vec.shape[-1]
    for k in range(2 * half):
        left = left_a if k < half else left_b
        right = right_a if k < half else right_b
        block = vec[src[t * 2 * half + k]]
        inner = jnp.dot(
            left[k % half, 0], block, preferred_element_type=jnp.float32
        ).astype(jnp.bfloat16)
        term = lax.dot_general(
            inner, right[k % half, 0], (((1,), (1,)), ((), ())),
            preferred_element_type=jnp.float32,
        )
        if k == 0:
            acc[...] = term
        else:
            acc[...] += term
    total = acc[...]
    out[...] = total.reshape(out.shape).astype(out.dtype)
    mine = own[0].astype(jnp.float32) * total
    dots[0] = jnp.sum(mine.reshape(tile // 8, 8, tile), axis=0)


def partial_sums(src, vec, own, left_a, left_b, right_a, right_b, op_count):
    half, sec_dev, tile, _ = left_a.shape
    share = tile // op_count
    ops = pl.BlockSpec((half, 1, tile, tile), lambda t, s: (0, t, 0, 0))
    flops = 2 * 2 * sec_dev * 2 * half * tile**3
    return pl.pallas_call(
        sigma_kernel,
        grid_spec=pltpu.PrefetchScalarGridSpec(
            num_scalar_prefetch=1,
            grid=(sec_dev,),
            in_specs=[
                pl.BlockSpec(vec.shape, lambda t, s: (0, 0, 0)),
                pl.BlockSpec((1, tile, tile), lambda t, s: (t, 0, 0)),
                ops, ops, ops, ops,
            ],
            out_specs=[
                pl.BlockSpec((op_count, 1, share, tile), lambda t, s: (0, t, 0, 0)),
                pl.BlockSpec((1, 8, tile), lambda t, s: (t, 0, 0)),
            ],
            scratch_shapes=[pltpu.VMEM((tile, tile), jnp.float32)],
        ),
        out_shape=[
            jax.ShapeDtypeStruct((op_count, sec_dev, share, tile), jnp.bfloat16),
            jax.ShapeDtypeStruct((sec_dev, 8, tile), jnp.float32),
        ],
        compiler_params=pltpu.CompilerParams(vmem_limit_bytes=40 * 2**20),
        cost_estimate=pl.CostEstimate(
            flops=flops, bytes_accessed=2 * (vec.size + 4 * left_a.size), transcendentals=0
        ),
    )(src, vec, own, left_a, left_b, right_a, right_b)


def swap(x, axis, mask):
    count = lax.axis_size(axis)
    return lax.ppermute(x, axis, [(i, i ^ mask) for i in range(count)])


def sum_over(x, axis):
    step = 1
    while step < lax.axis_size(axis):
        one, two, three = (swap(x, axis, step * m) for m in (1, 2, 3))
        x = (x + one) + (two + three)
        step *= 4
    return x


def body(wavefunction, left_ops, right_ops, sources, block_dims, energies):
    op_count = lax.axis_size("op")
    my_sec = lax.axis_index("sec")
    my_op = lax.axis_index("op")
    sec_dev, vectors, tile, _ = wavefunction.shape
    share = tile // op_count
    chips = op_count // vectors
    mine = my_op % vectors
    live = jnp.arange(tile, dtype=jnp.int32)[None, :] < block_dims[:, None]
    window = live[:, :, None] & live[:, None, :]

    own = lax.dynamic_index_in_dim(wavefunction, mine, 1, keepdims=False)
    own = jnp.where(window, own, jnp.zeros_like(own))
    gathered = lax.all_gather(own, "sec", axis=0, tiled=True)

    left_other = swap(left_ops, "op", 1)
    right_other = swap(right_ops, "op", 1)
    table = lax.dynamic_slice_in_dim(sources, my_sec * sec_dev, sec_dev, 1)
    table = jnp.concatenate([table, swap(table, "op", 1)], axis=0)
    table = jnp.transpose(table).reshape(-1)

    wide = jnp.where(window[:, None], wavefunction, 0).astype(jnp.float32)
    norms = jnp.sum(wide * wide, axis=(2, 3))
    denom = sum_over(jnp.sum(norms, axis=0), "sec")

    partial, dots = partial_sums(
        table, gathered, own, left_ops, left_other, right_ops, right_other, op_count
    )
    numer = jnp.where(jnp.arange(vectors) == mine, jnp.sum(dots), 0.0)
    numer = numer + jnp.sum(energies[:, None] * norms, axis=0) / op_count
    numer = sum_over(sum_over(numer, "op"), "sec")
    rayleigh = numer / denom

    pieces = lax.all_to_all(partial, "op", split_axis=0, concat_axis=0, tiled=True)
    pieces = pieces.reshape(chips, vectors, sec_dev, share, tile).astype(jnp.float32)
    summed = jnp.transpose(jnp.sum(pieces, axis=0), (2, 1, 0, 3))

    rows = lax.dynamic_slice_in_dim(wavefunction, my_op * share, share, 2)
    live_rows = lax.dynamic_slice_in_dim(live, my_op * share, share, 1)
    row_window = jnp.transpose(live_rows)[:, :, None, None] & live[None, :, None, :]
    rows = jnp.where(row_window, jnp.transpose(rows, (2, 0, 1, 3)).astype(jnp.float32), 0.0)
    sigma = jnp.where(row_window, summed + energies[None, :, None, None] * rows, 0.0)
    residual = sigma - rayleigh[None, None, :, None] * rows
    return (residual, rayleigh)


def solution(mesh):
    in_specs = (
        P("sec", None, None, None),
        P("op", "sec", None, None),
        P("op", "sec", None, None),
        P("op", None),
        P("sec"),
        P("sec"),
    )
    out_specs = (P("op", "sec", None, None), P())
    return jax.shard_map(body, mesh=mesh, in_specs=in_specs, out_specs=out_specs, check_vma=False)
```

```python
import jax
import jax.numpy as jnp
from jax import lax
from jax.experimental import pallas as pl
from jax.experimental.pallas import tpu as pltpu
from jax.sharding import PartitionSpec as P

GROUP = 4


def sigma_kernel(slots, own, left_a, left_b, right_a, right_b, *rest):
    pieces, (out, vec, acc, dots, sems) = rest[:-5], rest[-5:]
    t = pl.program_id(0)
    last = pl.num_programs(0) - 1
    half, _, tile, _ = left_a.shape
    share = out.shape[2]

    @pl.when(t == 0)
    def _():
        copies = []
        at = 0
        for i, piece in enumerate(pieces):
            count = piece.shape[0]
            copies.append(
                pltpu.make_async_copy(piece, vec.at[pl.ds(at, count)], sems.at[i])
            )
            at += count
        for copy in copies:
            copy.start()
        dots[...] = jnp.zeros_like(dots)
        for copy in copies:
            copy.wait()

    for first in range(0, 2 * half, GROUP):
        inners, rights = [], []
        for k in range(first, first + GROUP):
            left = left_a if k < half else left_b
            right = right_a if k < half else right_b
            block = vec[slots[t * 2 * half + k]]
            inner = jnp.dot(left[k % half, 0], block, preferred_element_type=jnp.float32)
            inners.append(inner.astype(jnp.bfloat16))
            rights.append(right[k % half, 0])
        term = lax.dot_general(
            jnp.concatenate(inners, axis=1), jnp.concatenate(rights, axis=1),
            (((1,), (1,)), ((), ())), preferred_element_type=jnp.float32,
        )
        if first == 0:
            acc[...] = term
        else:
            acc[...] += term
    total = acc[...]
    out[:, t] = total.reshape(out.shape[0], share, tile).astype(out.dtype)
    mine = own[0].astype(jnp.float32) * total
    dots[...] += jnp.sum(mine.reshape(tile // 8, 8, tile), axis=0)

    @pl.when(t == last)
    def _():
        row = jnp.sum(dots[...], axis=0, keepdims=True)
        high = row.astype(jnp.bfloat16)
        rest1 = row - high.astype(jnp.float32)
        mid = rest1.astype(jnp.bfloat16)
        low = (rest1 - mid.astype(jnp.float32)).astype(jnp.bfloat16)
        at = lax.broadcasted_iota(jnp.int32, (share, tile), 0)
        slab = jnp.where(
            at == 0, high.astype(jnp.float32),
            jnp.where(
                at == 1, mid.astype(jnp.float32),
                jnp.where(at == 2, low.astype(jnp.float32), 0.0),
            ),
        )
        out[:, last + 1] = jnp.broadcast_to(slab[None], (out.shape[0], share, tile)).astype(
            out.dtype
        )


def partial_sums(slots, own, left_a, left_b, right_a, right_b, pieces, op_count):
    half, sec_dev, tile, _ = left_a.shape
    share = tile // op_count
    total = sum(p.shape[0] for p in pieces)
    ops = pl.BlockSpec((half, 1, tile, tile), lambda t, s: (0, t, 0, 0))
    out_shape = (op_count, sec_dev + 1, share, tile)
    return pl.pallas_call(
        sigma_kernel,
        grid_spec=pltpu.PrefetchScalarGridSpec(
            num_scalar_prefetch=1,
            grid=(sec_dev,),
            in_specs=[pl.BlockSpec((1, tile, tile), lambda t, s: (t, 0, 0)), ops, ops, ops, ops]
            + [pl.BlockSpec(memory_space=pl.ANY)] * len(pieces),
            out_specs=pl.BlockSpec(out_shape, lambda t, s: (0, 0, 0, 0)),
            scratch_shapes=[
                pltpu.VMEM((total, tile, tile), jnp.bfloat16),
                pltpu.VMEM((tile, tile), jnp.float32),
                pltpu.VMEM((8, tile), jnp.float32),
                pltpu.SemaphoreType.DMA((len(pieces),)),
            ],
        ),
        out_shape=jax.ShapeDtypeStruct(out_shape, jnp.bfloat16),
        compiler_params=pltpu.CompilerParams(vmem_limit_bytes=60 * 2**20),
        cost_estimate=pl.CostEstimate(
            flops=2 * 2 * sec_dev * 2 * half * tile**3,
            bytes_accessed=2 * tile * tile * (total + 8 * half * sec_dev),
            transcendentals=0,
        ),
    )(slots, own, left_a, left_b, right_a, right_b, *pieces)


def swap(x, axis, mask):
    count = lax.axis_size(axis)
    return lax.ppermute(x, axis, [(i, i ^ mask) for i in range(count)])


def move(x, side, dy, dx):
    perm = [
        (y * side + x_, (y + dy) % side * side + (x_ + dx) % side)
        for y in range(side) for x_ in range(side)
    ]
    return lax.ppermute(x, "sec", perm)


def ring(block, send):
    n = block.shape[0] // 2
    behind = send(block, 1)
    ahead = send(block, -1)
    far_a = send(behind[:n], 1)
    far_b = send(ahead[n:], -1)
    return [block, behind, ahead, far_a, far_b]


def ring_place(source, mine, side):
    away = (source - mine) % side
    return jnp.where(away == 0, 0, jnp.where(away == side - 1, 1, away + 1))


def body(wavefunction, left_ops, right_ops, sources, block_dims, energies):
    op_count = lax.axis_size("op")
    sec_count = lax.axis_size("sec")
    my_sec = lax.axis_index("sec")
    my_op = lax.axis_index("op")
    sec_dev, vectors, tile, _ = wavefunction.shape
    share = tile // op_count
    chips = op_count // vectors
    mine = my_op % vectors
    side = 4
    live = jnp.arange(tile, dtype=jnp.int32)[None, :] < block_dims[:, None]
    window = live[:, :, None] & live[:, None, :]

    own = lax.dynamic_index_in_dim(wavefunction, mine, 1, keepdims=False)
    own = jnp.where(window, own, jnp.zeros_like(own))

    gathered = lax.all_gather(own[:2], "sec", axis=0, tiled=True)
    along_x = lambda b, d: move(b, side, 0, d)
    along_y = lambda b, d: move(b, side, d, 0)
    pieces = [gathered]
    for sector, first, second in ((2, along_x, along_y), (3, along_y, along_x)):
        block = own[sector].reshape(2, tile // 2, tile)
        block = jnp.concatenate(ring(block, first), axis=0)
        pieces += [p.reshape(-1, tile, tile) for p in ring(block, second)]

    left_other = swap(left_ops, "op", 1)
    right_other = swap(right_ops, "op", 1)
    table = lax.dynamic_slice_in_dim(sources, my_sec * sec_dev, sec_dev, 1)
    table = jnp.concatenate([table, swap(table, "op", 1)], axis=0)
    table = jnp.transpose(table).reshape(-1)
    device, local = table // sec_dev, table % sec_dev
    in_y = ring_place(device // side, my_sec // side, side)
    in_x = ring_place(device % side, my_sec % side, side)
    slots = jnp.where(
        local < 2, device * 2 + local,
        jnp.where(local == 2, 2 * sec_count + in_y * side + in_x, 3 * sec_count + in_x * side + in_y),
    )

    wide = jnp.where(window[:, None], wavefunction, 0).astype(jnp.float32)
    norms = jnp.sum(wide * wide, axis=(2, 3))

    partial = partial_sums(
        slots, own, left_ops, left_other, right_ops, right_other, pieces, op_count
    )
    parts = lax.all_to_all(partial, "op", split_axis=0, concat_axis=0, tiled=True)
    parts = parts.reshape(chips, vectors, sec_dev + 1, share, tile)
    numer = jnp.sum(parts[:, :, sec_dev].astype(jnp.float32), axis=(0, 2, 3))
    numer = numer + jnp.sum(energies[:, None] * norms, axis=0)
    scalars = jnp.concatenate([numer, jnp.sum(norms, axis=0)])
    scalars = jnp.pad(scalars[None, None, :], ((0, 0), (0, 7), (0, 128 - 2 * vectors)))
    scalars = jnp.broadcast_to(scalars, (sec_count, 8, 128))
    scalars = lax.all_to_all(scalars, "sec", split_axis=0, concat_axis=0, tiled=True)
    scalars = jnp.sum(scalars[:, 0, : 2 * vectors], axis=0)
    rayleigh = scalars[:vectors] / scalars[vectors:]

    summed = jnp.sum(parts[:, :, :sec_dev].astype(jnp.float32), axis=0)
    summed = jnp.transpose(summed, (2, 1, 0, 3))
    rows = lax.dynamic_slice_in_dim(wavefunction, my_op * share, share, 2)
    live_rows = lax.dynamic_slice_in_dim(live, my_op * share, share, 1)
    row_window = jnp.transpose(live_rows)[:, :, None, None] & live[None, :, None, :]
    rows = jnp.where(row_window, jnp.transpose(rows, (2, 0, 1, 3)).astype(jnp.float32), 0.0)
    sigma = jnp.where(row_window, summed + energies[None, :, None, None] * rows, 0.0)
    residual = sigma - rayleigh[None, None, :, None] * rows
    return (residual, rayleigh)


def solution(mesh):
    in_specs = (
        P("sec", None, None, None),
        P("op", "sec", None, None),
        P("op", "sec", None, None),
        P("op", None),
        P("sec"),
        P("sec"),
    )
    out_specs = (P("op", "sec", None, None), P())
    return jax.shard_map(body, mesh=mesh, in_specs=in_specs, out_specs=out_specs, check_vma=False)
```

```python
import jax
import jax.numpy as jnp
from jax import lax
from jax.experimental import pallas as pl
from jax.experimental.pallas import tpu as pltpu
from jax.sharding import PartitionSpec as P

GROUP = 4


def sigma_kernel(
    table, own, extra, left_a, left_b, right_a, right_b, gathered, out, scalars, vec, acc, dots, sems
):
    t = pl.program_id(0)
    half, _, tile, _ = left_a.shape
    chips, _, height, _ = gathered.shape
    sec_dev = vec.shape[1]
    cuts = tile // height

    @pl.when(t == 0)
    def _():
        copies = [
            pltpu.make_async_copy(
                gathered.at[z],
                vec.at[:, z // cuts, pl.ds(z % cuts * height, height)],
                sems.at[z],
            )
            for z in range(chips)
        ]
        for copy in copies:
            copy.start()
        dots[...] = jnp.zeros_like(dots)
        for copy in copies:
            copy.wait()

    for first in range(0, 2 * half, GROUP):
        inners, rights = [], []
        for k in range(first, first + GROUP):
            left = left_a if k < half else left_b
            right = right_a if k < half else right_b
            source = table[t * 2 * half + k]
            block = vec[lax.div(source, sec_dev), lax.rem(source, sec_dev)]
            inner = jnp.dot(left[k % half, 0], block, preferred_element_type=jnp.float32)
            inners.append(inner.astype(jnp.bfloat16))
            rights.append(right[k % half, 0])
        term = lax.dot_general(
            jnp.concatenate(inners, axis=1), jnp.concatenate(rights, axis=1),
            (((1,), (1,)), ((), ())), preferred_element_type=jnp.float32,
        )
        if first == 0:
            acc[...] = term
        else:
            acc[...] += term
    total = acc[...]
    out[...] = total.reshape(out.shape).astype(out.dtype)
    mine = own[0].astype(jnp.float32) * total
    dots[...] += jnp.sum(mine.reshape(tile // 8, 8, tile), axis=0)

    @pl.when(t == pl.num_programs(0) - 1)
    def _():
        lane = lax.broadcasted_iota(jnp.int32, scalars.shape, 1)
        numer = jnp.sum(dots[...])
        scalars[...] = extra[...] + jnp.where(lane == table[sec_dev * 2 * half], numer, 0.0)


def partial_sums(table, own, extra, left_a, left_b, right_a, right_b, gathered, op_count):
    half, sec_dev, tile, _ = left_a.shape
    chips, sec_count = gathered.shape[:2]
    share = tile // op_count
    ops = pl.BlockSpec((half, 1, tile, tile), lambda t, s: (0, t, 0, 0))
    small = pl.BlockSpec(extra.shape, lambda t, s: (0, 0))
    return pl.pallas_call(
        sigma_kernel,
        grid_spec=pltpu.PrefetchScalarGridSpec(
            num_scalar_prefetch=1,
            grid=(sec_dev,),
            in_specs=[
                pl.BlockSpec((1, tile, tile), lambda t, s: (t, 0, 0)),
                small, ops, ops, ops, ops,
                pl.BlockSpec(memory_space=pl.ANY),
            ],
            out_specs=[
                pl.BlockSpec((op_count, 1, share, tile), lambda t, s: (0, t, 0, 0)),
                small,
            ],
            scratch_shapes=[
                pltpu.VMEM((sec_count, sec_dev, tile, tile), jnp.bfloat16),
                pltpu.VMEM((tile, tile), jnp.float32),
                pltpu.VMEM((8, tile), jnp.float32),
                pltpu.SemaphoreType.DMA((chips,)),
            ],
        ),
        out_shape=[
            jax.ShapeDtypeStruct((op_count, sec_dev, share, tile), jnp.bfloat16),
            jax.ShapeDtypeStruct(extra.shape, jnp.float32),
        ],
        compiler_params=pltpu.CompilerParams(vmem_limit_bytes=60 * 2**20),
        cost_estimate=pl.CostEstimate(
            flops=2 * 2 * sec_dev * 2 * half * tile**3,
            bytes_accessed=2 * (gathered.size + 4 * left_a.size),
            transcendentals=0,
        ),
    )(table, own, extra, left_a, left_b, right_a, right_b, gathered)


def swap(x, axis, mask):
    count = lax.axis_size(axis)
    return lax.ppermute(x, axis, [(i, i ^ mask) for i in range(count)])


def body(wavefunction, left_ops, right_ops, sources, block_dims, energies):
    op_count = lax.axis_size("op")
    sec_count = lax.axis_size("sec")
    my_sec = lax.axis_index("sec")
    my_op = lax.axis_index("op")
    sec_dev, vectors, tile, _ = wavefunction.shape
    share = tile // op_count
    chips = op_count // vectors
    cuts = chips // sec_dev
    height = tile // cuts
    core = my_op % vectors
    chip = my_op // vectors

    sector, first = chip // cuts, chip % cuts * height
    piece = lax.dynamic_slice(
        wavefunction, (sector, core, first, 0), (1, 1, height, tile)
    ).reshape(height, tile)
    size = lax.dynamic_index_in_dim(block_dims, sector, 0, keepdims=False)
    inside = (first + jnp.arange(height, dtype=jnp.int32) < size)[:, None] & (
        jnp.arange(tile, dtype=jnp.int32) < size
    )[None, :]
    piece = jnp.where(inside, piece, jnp.zeros_like(piece))
    groups = [
        [o * sec_count + s for o in range(c, op_count, vectors) for s in range(sec_count)]
        for c in range(vectors)
    ]
    gathered = lax.all_gather(
        piece, ("op", "sec"), axis=0, tiled=True, axis_index_groups=groups
    ).reshape(chips, sec_count, height, tile)

    left_other = swap(left_ops, "op", 1)
    right_other = swap(right_ops, "op", 1)
    table = lax.dynamic_slice_in_dim(sources, my_sec * sec_dev, sec_dev, 1)
    table = jnp.concatenate([table, swap(table, "op", 1)], axis=0)
    table = jnp.concatenate([jnp.transpose(table).reshape(-1), core[None].astype(jnp.int32)])

    live = jnp.arange(tile, dtype=jnp.int32)[None, :] < block_dims[:, None]
    window = live[:, :, None] & live[:, None, :]
    own = lax.dynamic_index_in_dim(wavefunction, core, 1, keepdims=False)
    own = jnp.where(window, own, jnp.zeros_like(own))
    norms = jnp.sum(jnp.square(own.astype(jnp.float32)), axis=(1, 2)) / chips
    lane = jnp.arange(128, dtype=jnp.int32)
    extra = jnp.where(lane == core, jnp.sum(energies * norms), 0.0)
    extra = jnp.where(lane == vectors + core, jnp.sum(norms), extra)
    extra = jnp.broadcast_to(extra[None, :], (8, 128))

    partial, scalars = partial_sums(
        table, own, extra, left_ops, left_other, right_ops, right_other, gathered, op_count
    )
    scalars = lax.all_gather(scalars, ("op", "sec"), axis=0, tiled=True)
    scalars = scalars.reshape(op_count * sec_count, 8, 128)[:, 0, : 2 * vectors]
    scalars = jnp.sum(scalars, axis=0)
    rayleigh = scalars[:vectors] / scalars[vectors:]

    parts = lax.all_to_all(partial, "op", split_axis=0, concat_axis=0, tiled=True)
    parts = parts.reshape(chips, vectors, sec_dev, share, tile)
    summed = jnp.transpose(jnp.sum(parts.astype(jnp.float32), axis=0), (2, 1, 0, 3))
    rows = lax.dynamic_slice_in_dim(wavefunction, my_op * share, share, 2)
    live_rows = lax.dynamic_slice_in_dim(live, my_op * share, share, 1)
    row_window = jnp.transpose(live_rows)[:, :, None, None] & live[None, :, None, :]
    rows = jnp.where(row_window, jnp.transpose(rows, (2, 0, 1, 3)).astype(jnp.float32), 0.0)
    sigma = jnp.where(row_window, summed + energies[None, :, None, None] * rows, 0.0)
    residual = sigma - rayleigh[None, None, :, None] * rows
    return (residual, rayleigh)


def solution(mesh):
    in_specs = (
        P("sec", None, None, None),
        P("op", "sec", None, None),
        P("op", "sec", None, None),
        P("op", None),
        P("sec"),
        P("sec"),
    )
    out_specs = (P("op", "sec", None, None), P())
    return jax.shard_map(body, mesh=mesh, in_specs=in_specs, out_specs=out_specs, check_vma=False)
```

```python
import jax
import jax.numpy as jnp
from jax import lax
from jax.experimental import pallas as pl
from jax.experimental.pallas import tpu as pltpu
from jax.sharding import PartitionSpec as P

GROUP = 4


def sigma_kernel(
    slots, own, extra, left_a, left_b, right_a, right_b, *rest
):
    pieces, (out, scalars, vec, acc, dots, sems) = rest[:-6], rest[-6:]
    t = pl.program_id(0)
    half, _, tile, _ = left_a.shape

    @pl.when(t == 0)
    def _():
        copies = []
        at = 0
        for i, piece in enumerate(pieces):
            count = piece.shape[0]
            copies.append(pltpu.make_async_copy(piece, vec.at[pl.ds(at, count)], sems.at[i]))
            at += count
        for copy in copies:
            copy.start()
        dots[...] = jnp.zeros_like(dots)
        for copy in copies:
            copy.wait()

    for first in range(0, 2 * half, GROUP):
        inners, rights = [], []
        for k in range(first, first + GROUP):
            left = left_a if k < half else left_b
            right = right_a if k < half else right_b
            block = vec[slots[t * 2 * half + k]]
            inner = jnp.dot(left[k % half, 0], block, preferred_element_type=jnp.float32)
            inners.append(inner.astype(jnp.bfloat16))
            rights.append(right[k % half, 0])
        term = lax.dot_general(
            jnp.concatenate(inners, axis=1), jnp.concatenate(rights, axis=1),
            (((1,), (1,)), ((), ())), preferred_element_type=jnp.float32,
        )
        if first == 0:
            acc[...] = term
        else:
            acc[...] += term
    total = acc[...]
    out[...] = total.reshape(out.shape).astype(out.dtype)
    mine = own[0].astype(jnp.float32) * total
    dots[...] += jnp.sum(mine.reshape(tile // 8, 8, tile), axis=0)

    @pl.when(t == pl.num_programs(0) - 1)
    def _():
        lane = lax.broadcasted_iota(jnp.int32, scalars.shape, 1)
        numer = jnp.sum(dots[...])
        scalars[...] = extra[...] + jnp.where(lane == slots[pl.num_programs(0) * 2 * half], numer, 0.0)


def partial_sums(slots, own, extra, left_a, left_b, right_a, right_b, pieces, op_count):
    half, sec_dev, tile, _ = left_a.shape
    total = sum(p.shape[0] for p in pieces)
    share = tile // op_count
    ops = pl.BlockSpec((half, 1, tile, tile), lambda t, s: (0, t, 0, 0))
    small = pl.BlockSpec(extra.shape, lambda t, s: (0, 0))
    return pl.pallas_call(
        sigma_kernel,
        grid_spec=pltpu.PrefetchScalarGridSpec(
            num_scalar_prefetch=1,
            grid=(sec_dev,),
            in_specs=[
                pl.BlockSpec((1, tile, tile), lambda t, s: (t, 0, 0)),
                small, ops, ops, ops, ops,
            ]
            + [pl.BlockSpec(memory_space=pl.ANY)] * len(pieces),
            out_specs=[
                pl.BlockSpec((op_count, 1, share, tile), lambda t, s: (0, t, 0, 0)),
                small,
            ],
            scratch_shapes=[
                pltpu.VMEM((total, tile, tile), jnp.bfloat16),
                pltpu.VMEM((tile, tile), jnp.float32),
                pltpu.VMEM((8, tile), jnp.float32),
                pltpu.SemaphoreType.DMA((len(pieces),)),
            ],
        ),
        out_shape=[
            jax.ShapeDtypeStruct((op_count, sec_dev, share, tile), jnp.bfloat16),
            jax.ShapeDtypeStruct(extra.shape, jnp.float32),
        ],
        compiler_params=pltpu.CompilerParams(vmem_limit_bytes=60 * 2**20),
        cost_estimate=pl.CostEstimate(
            flops=2 * 2 * sec_dev * 2 * half * tile**3,
            bytes_accessed=2 * (total * tile * tile + 4 * left_a.size),
            transcendentals=0,
        ),
    )(slots, own, extra, left_a, left_b, right_a, right_b, *pieces)


def swap(x, axis, mask):
    count = lax.axis_size(axis)
    return lax.ppermute(x, axis, [(i, i ^ mask) for i in range(count)])


def move(x, side, dy, dx):
    perm = [
        (y * side + x_, (y + dy) % side * side + (x_ + dx) % side)
        for y in range(side) for x_ in range(side)
    ]
    return lax.ppermute(x, "sec", perm)


def join_kernel(*refs):
    parts, joined, sems = refs[:-2], refs[-2], refs[-1]
    at = 0
    copies = []
    for i, part in enumerate(parts):
        count = part.shape[0]
        copies.append(pltpu.make_async_copy(part, joined.at[pl.ds(at, count)], sems.at[i]))
        at += count
    for copy in copies:
        copy.start()
    for copy in copies:
        copy.wait()


def join(*parts):
    total = sum(p.shape[0] for p in parts)
    return pl.pallas_call(
        join_kernel,
        in_specs=[pl.BlockSpec(memory_space=pl.ANY)] * len(parts),
        out_specs=pl.BlockSpec(memory_space=pl.ANY),
        out_shape=jax.ShapeDtypeStruct((total,) + parts[0].shape[1:], parts[0].dtype),
        scratch_shapes=[pltpu.SemaphoreType.DMA((len(parts),))],
    )(*parts)


def ring_near(block, send):
    return [block, send(block, 1), send(block, -1)]


def ring_far(near, send):
    n = near[0].shape[0] // 2
    return [send(near[1][:n], 1), send(near[2][n:], -1)]


def ring_place(source, mine, side):
    away = (source - mine) % side
    return jnp.where(away == 0, 0, jnp.where(away == side - 1, 1, away + 1))


def body(wavefunction, left_ops, right_ops, sources, block_dims, energies):
    op_count = lax.axis_size("op")
    sec_count = lax.axis_size("sec")
    my_sec = lax.axis_index("sec")
    my_op = lax.axis_index("op")
    sec_dev, vectors, tile, _ = wavefunction.shape
    share = tile // op_count
    chips = op_count // vectors
    core = my_op % vectors
    side = 4
    flow = sec_dev // 2

    live = jnp.arange(tile, dtype=jnp.int32)[None, :] < block_dims[:, None]
    window = live[:, :, None] & live[:, None, :]
    own = lax.dynamic_index_in_dim(wavefunction, core, 1, keepdims=False)
    own = jnp.where(window, own, jnp.zeros_like(own))

    along_x = lambda b, d: move(b, side, 0, d)
    along_y = lambda b, d: move(b, side, d, 0)
    left_other = swap(left_ops, "op", 1)
    right_other = swap(right_ops, "op", 1)
    near_x = ring_near(own[:flow], along_x)
    near_y = ring_near(own[flow:], along_y)
    line_x = join(*near_x, *ring_far(near_x, along_x))
    line_y = join(*near_y, *ring_far(near_y, along_y))
    line_x, line_y, left_other, right_other = lax.optimization_barrier(
        (line_x, line_y, left_other, right_other)
    )
    near_x = ring_near(line_x, along_y)
    near_y = ring_near(line_y, along_x)
    pieces = near_x + ring_far(near_x, along_y) + near_y + ring_far(near_y, along_x)

    table = lax.dynamic_slice_in_dim(sources, my_sec * sec_dev, sec_dev, 1)
    table = jnp.concatenate([table, swap(table, "op", 1)], axis=0)
    table = jnp.transpose(table).reshape(-1)
    device, local = table // sec_dev, table % sec_dev
    in_y = ring_place(device // side, my_sec // side, side)
    in_x = ring_place(device % side, my_sec % side, side)
    slots = jnp.where(
        local < flow, in_y * side + in_x, sec_count + in_x * side + in_y
    ) * flow + local % flow
    slots = jnp.concatenate([slots, core[None].astype(jnp.int32)])

    norms = jnp.sum(jnp.square(own.astype(jnp.float32)), axis=(1, 2)) / chips
    lane = jnp.arange(128, dtype=jnp.int32)
    extra = jnp.where(lane == core, jnp.sum(energies * norms), 0.0)
    extra = jnp.where(lane == vectors + core, jnp.sum(norms), extra)
    extra = jnp.broadcast_to(extra[None, :], (8, 128))

    partial, scalars = partial_sums(
        slots, own, extra, left_ops, left_other, right_ops, right_other, pieces, op_count
    )
    for axis in ("sec", "op"):
        scalars = jnp.broadcast_to(scalars[None], (lax.axis_size(axis),) + scalars.shape)
        scalars = lax.all_to_all(scalars, axis, split_axis=0, concat_axis=0, tiled=True)
        scalars = jnp.sum(scalars, axis=0)
    scalars = scalars[0, : 2 * vectors]
    rayleigh = scalars[:vectors] / scalars[vectors:]

    parts = lax.all_to_all(partial, "op", split_axis=0, concat_axis=0, tiled=True)
    parts = parts.reshape(chips, vectors, sec_dev, share, tile)
    summed = jnp.transpose(jnp.sum(parts.astype(jnp.float32), axis=0), (2, 1, 0, 3))
    rows = lax.dynamic_slice_in_dim(wavefunction, my_op * share, share, 2)
    live_rows = lax.dynamic_slice_in_dim(live, my_op * share, share, 1)
    row_window = jnp.transpose(live_rows)[:, :, None, None] & live[None, :, None, :]
    rows = jnp.where(row_window, jnp.transpose(rows, (2, 0, 1, 3)).astype(jnp.float32), 0.0)
    sigma = jnp.where(row_window, summed + energies[None, :, None, None] * rows, 0.0)
    residual = sigma - rayleigh[None, None, :, None] * rows
    return (residual, rayleigh)


def solution(mesh):
    in_specs = (
        P("sec", None, None, None),
        P("op", "sec", None, None),
        P("op", "sec", None, None),
        P("op", None),
        P("sec"),
        P("sec"),
    )
    out_specs = (P("op", "sec", None, None), P())
    return jax.shard_map(body, mesh=mesh, in_specs=in_specs, out_specs=out_specs, check_vma=False)
```

```python
import jax
import jax.numpy as jnp
from jax import lax
from jax.experimental import pallas as pl
from jax.experimental.pallas import tpu as pltpu
from jax.sharding import PartitionSpec as P

GROUP = 4


def sigma_kernel(
    slots, own, extra, left_a, left_b, right_a, right_b, *rest
):
    pieces, (out, scalars, vec, acc, dots, sems) = rest[:-6], rest[-6:]
    t = pl.program_id(0)
    half, _, tile, _ = left_a.shape

    @pl.when(t == 0)
    def _():
        copies = []
        at = 0
        for i, piece in enumerate(pieces):
            count = piece.shape[0]
            copies.append(pltpu.make_async_copy(piece, vec.at[pl.ds(at, count)], sems.at[i]))
            at += count
        for copy in copies:
            copy.start()
        dots[...] = jnp.zeros_like(dots)
        for copy in copies:
            copy.wait()

    for first in range(0, 2 * half, GROUP):
        inners, rights = [], []
        for k in range(first, first + GROUP):
            left = left_a if k < half else left_b
            right = right_a if k < half else right_b
            block = vec[slots[t * 2 * half + k]]
            inner = jnp.dot(left[k % half, 0], block, preferred_element_type=jnp.float32)
            inners.append(inner.astype(jnp.bfloat16))
            rights.append(right[k % half, 0])
        term = lax.dot_general(
            jnp.concatenate(inners, axis=1), jnp.concatenate(rights, axis=1),
            (((1,), (1,)), ((), ())), preferred_element_type=jnp.float32,
        )
        if first == 0:
            acc[...] = term
        else:
            acc[...] += term
    total = acc[...]
    out[...] = total.reshape(out.shape).astype(out.dtype)
    mine = own[0].astype(jnp.float32) * total
    dots[...] += jnp.sum(mine.reshape(tile // 8, 8, tile), axis=0)

    @pl.when(t == pl.num_programs(0) - 1)
    def _():
        lane = lax.broadcasted_iota(jnp.int32, scalars.shape, 1)
        numer = jnp.sum(dots[...])
        scalars[...] = extra[...] + jnp.where(lane == slots[pl.num_programs(0) * 2 * half], numer, 0.0)


def partial_sums(slots, own, extra, left_a, left_b, right_a, right_b, pieces, op_count):
    half, sec_dev, tile, _ = left_a.shape
    total = sum(p.shape[0] for p in pieces)
    share = tile // op_count
    ops = pl.BlockSpec((half, 1, tile, tile), lambda t, s: (0, t, 0, 0))
    small = pl.BlockSpec(extra.shape, lambda t, s: (0, 0))
    return pl.pallas_call(
        sigma_kernel,
        grid_spec=pltpu.PrefetchScalarGridSpec(
            num_scalar_prefetch=1,
            grid=(sec_dev,),
            in_specs=[
                pl.BlockSpec((1, tile, tile), lambda t, s: (t, 0, 0)),
                small, ops, ops, ops, ops,
            ]
            + [pl.BlockSpec(memory_space=pl.ANY)] * len(pieces),
            out_specs=[
                pl.BlockSpec((op_count, 1, share, tile), lambda t, s: (0, t, 0, 0)),
                small,
            ],
            scratch_shapes=[
                pltpu.VMEM((total, tile, tile), jnp.bfloat16),
                pltpu.VMEM((tile, tile), jnp.float32),
                pltpu.VMEM((8, tile), jnp.float32),
                pltpu.SemaphoreType.DMA((len(pieces),)),
            ],
        ),
        out_shape=[
            jax.ShapeDtypeStruct((op_count, sec_dev, share, tile), jnp.bfloat16),
            jax.ShapeDtypeStruct(extra.shape, jnp.float32),
        ],
        compiler_params=pltpu.CompilerParams(vmem_limit_bytes=60 * 2**20),
        cost_estimate=pl.CostEstimate(
            flops=2 * 2 * sec_dev * 2 * half * tile**3,
            bytes_accessed=2 * (total * tile * tile + 4 * left_a.size),
            transcendentals=0,
        ),
    )(slots, own, extra, left_a, left_b, right_a, right_b, *pieces)


def swap(x, axis, mask):
    count = lax.axis_size(axis)
    return lax.ppermute(x, axis, [(i, i ^ mask) for i in range(count)])


def sum_over(x, axis):
    step = 1
    while step < lax.axis_size(axis):
        x = x + swap(x, axis, step)
        step *= 2
    return x


def move(x, side, dy, dx):
    perm = [
        (y * side + x_, (y + dy) % side * side + (x_ + dx) % side)
        for y in range(side) for x_ in range(side)
    ]
    return lax.ppermute(x, "sec", perm)


def join_kernel(*refs):
    parts, joined = refs[:-1], refs[-1]
    at = 0
    for part in parts:
        count = part.shape[0]
        joined[pl.ds(at, count)] = part[...]
        at += count


def join(*parts):
    total = sum(p.shape[0] for p in parts)
    return pl.pallas_call(
        join_kernel,
        in_specs=[pl.BlockSpec(memory_space=pltpu.VMEM)] * len(parts),
        out_specs=pl.BlockSpec(memory_space=pltpu.VMEM),
        out_shape=jax.ShapeDtypeStruct((total,) + parts[0].shape[1:], parts[0].dtype),
    )(*parts)


def ring_near(block, send):
    return [block, send(block, 1), send(block, -1)]


def ring_far(near, send):
    n = near[0].shape[0] // 2
    return [send(near[1][:n], 1), send(near[2][n:], -1)]


def ring_halves(low, high, send):
    return [low, high, send(low, 1), send(high, 1), send(low, -1), send(high, -1)]


def ring_last(near, send):
    return [send(near[2], 1), send(near[5], -1)]


def ring_place(source, mine, side):
    away = (source - mine) % side
    return jnp.where(away == 0, 0, jnp.where(away == side - 1, 1, away + 1))


def body(wavefunction, left_ops, right_ops, sources, block_dims, energies):
    op_count = lax.axis_size("op")
    sec_count = lax.axis_size("sec")
    my_sec = lax.axis_index("sec")
    my_op = lax.axis_index("op")
    sec_dev, vectors, tile, _ = wavefunction.shape
    share = tile // op_count
    chips = op_count // vectors
    core = my_op % vectors
    side = 4
    flow = sec_dev // 2

    live = jnp.arange(tile, dtype=jnp.int32)[None, :] < block_dims[:, None]
    window = live[:, :, None] & live[:, None, :]
    own = lax.dynamic_index_in_dim(wavefunction, core, 1, keepdims=False)
    own = jnp.where(window, own, jnp.zeros_like(own))

    along_x = lambda b, d: move(b, side, 0, d)
    along_y = lambda b, d: move(b, side, d, 0)
    left_other = swap(left_ops, "op", 1)
    near_x = ring_near(own[:flow], along_x)
    near_y = ring_near(own[flow:], along_y)
    near_x, near_y, left_other, right = lax.optimization_barrier(
        (near_x, near_y, left_other, right_ops)
    )
    right_other = swap(right, "op", 1)
    far_x = ring_far(near_x, along_x)
    far_y = ring_far(near_y, along_y)
    pieces_x = ring_halves(join(near_x[0], near_x[1]), join(near_x[2], *far_x), along_y)
    pieces_y = ring_halves(join(near_y[0], near_y[1]), join(near_y[2], *far_y), along_x)
    pieces_x, pieces_y, right_other = lax.optimization_barrier((pieces_x, pieces_y, right_other))
    pieces = pieces_x + ring_last(pieces_x, along_y) + pieces_y + ring_last(pieces_y, along_x)

    table = lax.dynamic_slice_in_dim(sources, my_sec * sec_dev, sec_dev, 1)
    table = jnp.concatenate([table, swap(table, "op", 1)], axis=0)
    table = jnp.transpose(table).reshape(-1)
    device, local = table // sec_dev, table % sec_dev
    in_y = ring_place(device // side, my_sec // side, side)
    in_x = ring_place(device % side, my_sec % side, side)
    slots = jnp.where(
        local < flow, in_y * side + in_x, sec_count + in_x * side + in_y
    ) * flow + local % flow
    slots = jnp.concatenate([slots, core[None].astype(jnp.int32)])

    norms = jnp.sum(jnp.square(own.astype(jnp.float32)), axis=(1, 2)) / chips
    lane = jnp.arange(128, dtype=jnp.int32)
    extra = jnp.where(lane == core, jnp.sum(energies * norms), 0.0)
    extra = jnp.where(lane == vectors + core, jnp.sum(norms), extra)
    extra = jnp.broadcast_to(extra[None, :], (8, 128))

    partial, scalars = partial_sums(
        slots, own, extra, left_ops, left_other, right_ops, right_other, pieces, op_count
    )
    parts = lax.all_to_all(partial, "op", split_axis=0, concat_axis=0, tiled=True)
    scalars = sum_over(scalars, "sec")
    scalars, parts = lax.optimization_barrier((scalars, parts))
    scalars = sum_over(scalars, "op")[0, : 2 * vectors]
    rayleigh = scalars[:vectors] / scalars[vectors:]

    parts = parts.reshape(chips, vectors, sec_dev, share, tile)
    summed = jnp.transpose(jnp.sum(parts.astype(jnp.float32), axis=0), (2, 1, 0, 3))
    rows = lax.dynamic_slice_in_dim(wavefunction, my_op * share, share, 2)
    live_rows = lax.dynamic_slice_in_dim(live, my_op * share, share, 1)
    row_window = jnp.transpose(live_rows)[:, :, None, None] & live[None, :, None, :]
    rows = jnp.where(row_window, jnp.transpose(rows, (2, 0, 1, 3)).astype(jnp.float32), 0.0)
    sigma = jnp.where(row_window, summed + energies[None, :, None, None] * rows, 0.0)
    residual = sigma - rayleigh[None, None, :, None] * rows
    return (residual, rayleigh)


def solution(mesh):
    in_specs = (
        P("sec", None, None, None),
        P("op", "sec", None, None),
        P("op", "sec", None, None),
        P("op", None),
        P("sec"),
        P("sec"),
    )
    out_specs = (P("op", "sec", None, None), P())
    return jax.shard_map(body, mesh=mesh, in_specs=in_specs, out_specs=out_specs, check_vma=False)
```

```python
import functools

import jax
import jax.numpy as jnp
from jax import lax
from jax.experimental import pallas as pl
from jax.experimental.pallas import tpu as pltpu
from jax.sharding import PartitionSpec as P

GROUP = 4


def sigma_kernel(places, slots, own, left_a, left_b, right_a, right_b, *rest):
    arrays, (out, vec, acc, dots, sems) = rest[:-5], rest[-5:]
    t = pl.program_id(0)
    last = pl.num_programs(0) - 1
    half, _, tile, _ = left_a.shape
    op_count, _, lanes = out.shape
    share = tile // op_count

    @pl.when(t == 0)
    def _():
        copies = []
        at = 0
        for i, (array, first, count) in enumerate(places):
            copies.append(
                pltpu.make_async_copy(
                    arrays[array].at[pl.ds(first, count)], vec.at[pl.ds(at, count)], sems.at[i]
                )
            )
            at += count
        for copy in copies:
            copy.start()
        dots[...] = jnp.zeros_like(dots)
        for copy in copies:
            copy.wait()

    for first in range(0, 2 * half, GROUP):
        inners, rights = [], []
        for k in range(first, first + GROUP):
            left = left_a if k < half else left_b
            right = right_a if k < half else right_b
            block = vec[slots[t * 2 * half + k]]
            inner = jnp.dot(left[k % half, 0], block, preferred_element_type=jnp.float32)
            inners.append(inner.astype(jnp.bfloat16))
            rights.append(right[k % half, 0])
        term = lax.dot_general(
            jnp.concatenate(inners, axis=1), jnp.concatenate(rights, axis=1),
            (((1,), (1,)), ((), ())), preferred_element_type=jnp.float32,
        )
        if first == 0:
            acc[...] = term
        else:
            acc[...] += term
    total = acc[...]
    cuts = tile // lanes
    for cut in range(cuts):
        part = total[:, cut * lanes : (cut + 1) * lanes].reshape(op_count, share, lanes)
        row = pl.multiple_of((t * cuts + cut) * share, share)
        out[:, pl.ds(row, share), :] = part.astype(out.dtype)
    mine = own[0].astype(jnp.float32) * total
    dots[...] += jnp.sum(mine.reshape(tile // 8, 8, tile), axis=0)

    @pl.when(t == last)
    def _():
        row = jnp.sum(dots[...], axis=0, keepdims=True)
        row = sum(row[:, cut * lanes : (cut + 1) * lanes] for cut in range(cuts))
        high = row.astype(jnp.bfloat16).astype(jnp.float32)
        mid = (row - high).astype(jnp.bfloat16).astype(jnp.float32)
        low = row - high - mid
        at = lax.broadcasted_iota(jnp.int32, (share, lanes), 0)
        slab = jnp.where(at == 0, high, jnp.where(at == 1, mid, jnp.where(at == 2, low, 0.0)))
        slab = slab.astype(out.dtype)
        out[:, (last + 1) * cuts * share :, :] = jnp.broadcast_to(
            slab[None], (op_count, share, lanes)
        )


def partial_sums(slots, own, left_a, left_b, right_a, right_b, arrays, places, op_count):
    half, sec_dev, tile, _ = left_a.shape
    share = tile // op_count
    lanes = 128
    total = sum(count for _, _, count in places)
    ops = pl.BlockSpec((half, 1, tile, tile), lambda t, s: (0, t, 0, 0))
    out_shape = (op_count, (sec_dev * (tile // lanes) + 1) * share, lanes)
    return pl.pallas_call(
        functools.partial(sigma_kernel, places),
        grid_spec=pltpu.PrefetchScalarGridSpec(
            num_scalar_prefetch=1,
            grid=(sec_dev,),
            in_specs=[pl.BlockSpec((1, tile, tile), lambda t, s: (t, 0, 0)), ops, ops, ops, ops]
            + [pl.BlockSpec(memory_space=pl.ANY)] * len(arrays),
            out_specs=pl.BlockSpec(out_shape, lambda t, s: (0, 0, 0)),
            scratch_shapes=[
                pltpu.VMEM((total, tile, tile), jnp.bfloat16),
                pltpu.VMEM((tile, tile), jnp.float32),
                pltpu.VMEM((8, tile), jnp.float32),
                pltpu.SemaphoreType.DMA((len(places),)),
            ],
        ),
        out_shape=jax.ShapeDtypeStruct(out_shape, jnp.bfloat16),
        compiler_params=pltpu.CompilerParams(vmem_limit_bytes=60 * 2**20),
        cost_estimate=pl.CostEstimate(
            flops=2 * 2 * sec_dev * 2 * half * tile**3,
            bytes_accessed=2 * tile * tile * (total + 8 * half * sec_dev),
            transcendentals=0,
        ),
    )(slots, own, left_a, left_b, right_a, right_b, *arrays)


def swap(x, axis, mask):
    count = lax.axis_size(axis)
    return lax.ppermute(x, axis, [(i, i ^ mask) for i in range(count)])


def move(x, side, dy, dx):
    perm = [
        (y * side + x_, (y + dy) % side * side + (x_ + dx) % side)
        for y in range(side) for x_ in range(side)
    ]
    return lax.ppermute(x, "sec", perm)


def cut_kernel(plan, count, *refs):
    arrays, outs = refs[:count], refs[count:]
    for out, parts in zip(outs, plan):
        at = 0
        for array, first, size in parts:
            out[pl.ds(at, size)] = arrays[array][pl.ds(first, size)]
            at += size


def cut(plan, *arrays):
    block, dtype = arrays[0].shape[1:], arrays[0].dtype
    sizes = [sum(size for _, _, size in parts) for parts in plan]
    return pl.pallas_call(
        functools.partial(cut_kernel, plan, len(arrays)),
        in_specs=[pl.BlockSpec(memory_space=pltpu.VMEM)] * len(arrays),
        out_specs=[pl.BlockSpec(memory_space=pltpu.VMEM)] * len(plan),
        out_shape=[jax.ShapeDtypeStruct((size,) + block, dtype) for size in sizes],
    )(*arrays)


def gather_blocks(own, along_x, along_y, left_ops, right_ops):
    left_other = swap(left_ops, "op", 1)
    west, east = along_x(own, 1), along_x(own, -1)
    north, south = along_y(own, 1), along_y(own, -1)
    west, east, north, south, left_other, right = lax.optimization_barrier(
        (west, east, north, south, left_other, right_ops)
    )
    right_other = swap(right, "op", 1)
    far_w, far_e, far_n, far_s, mid_x, mid_y, more_x, more_y = cut(
        [
            [(0, 0, 1)], [(1, 1, 1)], [(2, 2, 1)], [(3, 3, 1)],
            [(0, 0, 2), (1, 0, 2)], [(2, 2, 2), (3, 2, 2)],
            [(0, 0, 2), (1, 0, 2), (2, 0, 2)], [(2, 2, 2), (3, 2, 2), (0, 2, 2)],
        ],
        west, east, north, south,
    )
    far_w, far_e = along_x(far_w, 1), along_x(far_e, -1)
    far_n, far_s = along_y(far_n, 1), along_y(far_s, -1)
    far_w, far_e, far_n, far_s, mid_x, mid_y, more_x, more_y, right_other = (
        lax.optimization_barrier(
            (far_w, far_e, far_n, far_s, mid_x, mid_y, more_x, more_y, right_other)
        )
    )
    more_xb, mid_xa = along_y(more_x, 1), along_y(mid_x, -1)
    more_yb, mid_ya = along_x(more_y, 1), along_x(mid_y, -1)
    far_x, far_y = cut(
        [[(0, 0, 1), (1, 0, 1)], [(2, 0, 1), (3, 0, 1)]], far_w, far_e, far_n, far_s
    )
    mid_xf, mid_yf = along_y(mid_xa, -1), along_x(mid_ya, -1)
    far_xb, far_xa = along_y(far_x, 1), along_y(far_x, -1)
    far_yb, far_ya = along_x(far_y, 1), along_x(far_y, -1)
    far_xf, far_yf = along_y(far_xb, 1), along_x(far_yb, 1)
    pieces = [
        (own, 0, 2), (mid_x, 0, 4), (far_x, 0, 2),
        (north, 0, 2), (more_xb, 0, 4), (far_xb, 0, 2),
        (south, 0, 2), (mid_xa, 0, 4), (far_xa, 0, 2),
        (more_xb, 4, 2), (mid_xf, 0, 4), (far_xf, 0, 2),
        (own, 2, 2), (mid_y, 0, 4), (far_y, 0, 2),
        (west, 2, 2), (more_yb, 0, 4), (far_yb, 0, 2),
        (east, 2, 2), (mid_ya, 0, 4), (far_ya, 0, 2),
        (more_yb, 4, 2), (mid_yf, 0, 4), (far_yf, 0, 2),
    ]
    arrays = []
    for array, _, _ in pieces:
        if not any(a is array for a in arrays):
            arrays.append(array)
    places = [
        (next(i for i, a in enumerate(arrays) if a is p[0]), p[1], p[2]) for p in pieces
    ]
    return arrays, places, left_other, right_other


def ring_place(source, mine, side):
    away = (source - mine) % side
    return jnp.where(away == 0, 0, jnp.where(away == side - 1, 1, away + 1))


def body(wavefunction, left_ops, right_ops, sources, block_dims, energies):
    op_count = lax.axis_size("op")
    sec_count = lax.axis_size("sec")
    my_sec = lax.axis_index("sec")
    my_op = lax.axis_index("op")
    sec_dev, vectors, tile, _ = wavefunction.shape
    share = tile // op_count
    chips = op_count // vectors
    core = my_op % vectors
    side = 4
    flow = sec_dev // 2

    live = jnp.arange(tile, dtype=jnp.int32)[None, :] < block_dims[:, None]
    window = live[:, :, None] & live[:, None, :]
    own = lax.dynamic_index_in_dim(wavefunction, core, 1, keepdims=False)
    own = jnp.where(window, own, jnp.zeros_like(own))

    along_x = lambda b, d: move(b, side, 0, d)
    along_y = lambda b, d: move(b, side, d, 0)
    arrays, places, left_other, right_other = gather_blocks(
        own, along_x, along_y, left_ops, right_ops
    )

    table = lax.dynamic_slice_in_dim(sources, my_sec * sec_dev, sec_dev, 1)
    table = jnp.concatenate([table, swap(table, "op", 1)], axis=0)
    table = jnp.transpose(table).reshape(-1)
    device, local = table // sec_dev, table % sec_dev
    in_y = ring_place(device // side, my_sec // side, side)
    in_x = ring_place(device % side, my_sec % side, side)
    slots = jnp.where(
        local < flow, in_y * side + in_x, sec_count + in_x * side + in_y
    ) * flow + local % flow

    wide = jnp.where(window[:, None], wavefunction, 0).astype(jnp.float32)
    norms = jnp.sum(wide * wide, axis=(2, 3))

    partial = partial_sums(
        slots, own, left_ops, left_other, right_ops, right_other, arrays, places, op_count
    )
    parts = lax.all_to_all(partial, "op", split_axis=0, concat_axis=0, tiled=True)
    lanes = parts.shape[2]
    parts = parts.reshape(chips, vectors, -1, share, lanes)
    numer = jnp.sum(parts[:, :, -1].astype(jnp.float32), axis=(0, 2, 3))
    numer = numer + jnp.sum(energies[:, None] * norms, axis=0)
    scalars = jnp.concatenate([numer, jnp.sum(norms, axis=0)])
    scalars = jnp.pad(scalars[None, None, :], ((0, 0), (0, 7), (0, 128 - 2 * vectors)))
    scalars = jnp.broadcast_to(scalars, (sec_count, 8, 128))
    scalars = lax.all_to_all(scalars, "sec", split_axis=0, concat_axis=0, tiled=True)
    scalars = jnp.sum(scalars[:, 0, : 2 * vectors], axis=0)
    rayleigh = scalars[:vectors] / scalars[vectors:]

    parts = parts[:, :, :-1].reshape(chips, vectors, sec_dev, tile // lanes, share, lanes)
    summed = jnp.sum(parts.astype(jnp.float32), axis=0)
    summed = jnp.concatenate([summed[:, :, cut] for cut in range(tile // lanes)], axis=3)
    summed = jnp.transpose(summed, (2, 1, 0, 3))
    rows = lax.dynamic_slice_in_dim(wavefunction, my_op * share, share, 2)
    live_rows = lax.dynamic_slice_in_dim(live, my_op * share, share, 1)
    row_window = jnp.transpose(live_rows)[:, :, None, None] & live[None, :, None, :]
    rows = jnp.where(row_window, jnp.transpose(rows, (2, 0, 1, 3)).astype(jnp.float32), 0.0)
    sigma = jnp.where(row_window, summed + energies[None, :, None, None] * rows, 0.0)
    residual = sigma - rayleigh[None, None, :, None] * rows
    return (residual, rayleigh)


def solution(mesh):
    in_specs = (
        P("sec", None, None, None),
        P("op", "sec", None, None),
        P("op", "sec", None, None),
        P("op", None),
        P("sec"),
        P("sec"),
    )
    out_specs = (P("op", "sec", None, None), P())
    return jax.shard_map(body, mesh=mesh, in_specs=in_specs, out_specs=out_specs, check_vma=False)
```

```python
import functools

import jax
import jax.numpy as jnp
from jax import lax
from jax.experimental import pallas as pl
from jax.experimental.pallas import tpu as pltpu
from jax.sharding import PartitionSpec as P

GROUP = 4


def sigma_kernel(places, slots, own, left_a, left_b, right_a, right_b, *rest):
    arrays, (out, vec, acc, dots, sems) = rest[:-5], rest[-5:]
    t = pl.program_id(0)
    last = pl.num_programs(0) - 1
    half, _, tile, _ = left_a.shape
    op_count, _, lanes = out.shape
    share = tile // op_count

    @pl.when(t == 0)
    def _():
        copies = []
        at = 0
        for i, (array, first, count) in enumerate(places):
            copies.append(
                pltpu.make_async_copy(
                    arrays[array].at[pl.ds(first, count)], vec.at[pl.ds(at, count)], sems.at[i]
                )
            )
            at += count
        for copy in copies:
            copy.start()
        dots[...] = jnp.zeros_like(dots)
        for copy in copies:
            copy.wait()

    for first in range(0, 2 * half, GROUP):
        inners, rights = [], []
        for k in range(first, first + GROUP):
            left = left_a if k < half else left_b
            right = right_a if k < half else right_b
            block = vec[slots[t * 2 * half + k]]
            inner = jnp.dot(left[k % half, 0], block, preferred_element_type=jnp.float32)
            inners.append(inner.astype(jnp.bfloat16))
            rights.append(right[k % half, 0])
        term = lax.dot_general(
            jnp.concatenate(inners, axis=1), jnp.concatenate(rights, axis=1),
            (((1,), (1,)), ((), ())), preferred_element_type=jnp.float32,
        )
        if first == 0:
            acc[...] = term
        else:
            acc[...] += term
    total = acc[...]
    cuts = tile // lanes
    for cut in range(cuts):
        part = total[:, cut * lanes : (cut + 1) * lanes].reshape(op_count, share, lanes)
        row = pl.multiple_of((t * cuts + cut) * share, share)
        out[:, pl.ds(row, share), :] = part.astype(out.dtype)
    mine = own[0].astype(jnp.float32) * total
    dots[...] += jnp.sum(mine.reshape(tile // 8, 8, tile), axis=0)

    @pl.when(t == last)
    def _():
        row = jnp.sum(dots[...], axis=0, keepdims=True)
        row = sum(row[:, cut * lanes : (cut + 1) * lanes] for cut in range(cuts))
        high = row.astype(jnp.bfloat16).astype(jnp.float32)
        mid = (row - high).astype(jnp.bfloat16).astype(jnp.float32)
        low = row - high - mid
        at = lax.broadcasted_iota(jnp.int32, (share, lanes), 0)
        slab = jnp.where(at == 0, high, jnp.where(at == 1, mid, jnp.where(at == 2, low, 0.0)))
        slab = slab.astype(out.dtype)
        out[:, (last + 1) * cuts * share :, :] = jnp.broadcast_to(
            slab[None], (op_count, share, lanes)
        )


def partial_sums(slots, own, left_a, left_b, right_a, right_b, arrays, places, op_count):
    half, sec_dev, tile, _ = left_a.shape
    share = tile // op_count
    lanes = 128
    total = sum(count for _, _, count in places)
    ops = pl.BlockSpec((half, 1, tile, tile), lambda t, s: (0, t, 0, 0))
    out_shape = (op_count, (sec_dev * (tile // lanes) + 1) * share, lanes)
    return pl.pallas_call(
        functools.partial(sigma_kernel, places),
        grid_spec=pltpu.PrefetchScalarGridSpec(
            num_scalar_prefetch=1,
            grid=(sec_dev,),
            in_specs=[pl.BlockSpec((1, tile, tile), lambda t, s: (t, 0, 0)), ops, ops, ops, ops]
            + [pl.BlockSpec(memory_space=pl.ANY)] * len(arrays),
            out_specs=pl.BlockSpec(out_shape, lambda t, s: (0, 0, 0)),
            scratch_shapes=[
                pltpu.VMEM((total, tile, tile), jnp.bfloat16),
                pltpu.VMEM((tile, tile), jnp.float32),
                pltpu.VMEM((8, tile), jnp.float32),
                pltpu.SemaphoreType.DMA((len(places),)),
            ],
        ),
        out_shape=jax.ShapeDtypeStruct(out_shape, jnp.bfloat16),
        compiler_params=pltpu.CompilerParams(vmem_limit_bytes=60 * 2**20),
        cost_estimate=pl.CostEstimate(
            flops=2 * 2 * sec_dev * 2 * half * tile**3,
            bytes_accessed=2 * tile * tile * (total + 8 * half * sec_dev),
            transcendentals=0,
        ),
    )(slots, own, left_a, left_b, right_a, right_b, *arrays)


def swap(x, axis, mask):
    count = lax.axis_size(axis)
    return lax.ppermute(x, axis, [(i, i ^ mask) for i in range(count)])


def step(x, side, ring, way):
    perm = []
    for op in range(lax.axis_size("op")):
        for at in range(side * side):
            y, x_ = at // side, at % side
            if (op + ring) % 2 == 0:
                x_ = (x_ + way) % side
            else:
                y = (y + way) % side
            perm.append((op * side * side + at, op * side * side + y * side + x_))
    return lax.ppermute(x, ("op", "sec"), perm)


def cut_kernel(plan, count, *refs):
    arrays, outs = refs[:count], refs[count:]
    for out, parts in zip(outs, plan):
        at = 0
        for array, first, size in parts:
            out[pl.ds(at, size)] = arrays[array][pl.ds(first, size)]
            at += size


def cut(plan, *arrays):
    block, dtype = arrays[0].shape[1:], arrays[0].dtype
    sizes = [sum(size for _, _, size in parts) for parts in plan]
    return pl.pallas_call(
        functools.partial(cut_kernel, plan, len(arrays)),
        in_specs=[pl.BlockSpec(memory_space=pltpu.VMEM)] * len(arrays),
        out_specs=[pl.BlockSpec(memory_space=pltpu.VMEM)] * len(plan),
        out_shape=[jax.ShapeDtypeStruct((size,) + block, dtype) for size in sizes],
    )(*arrays)


def gather_blocks(own, side, left_ops, right_ops):
    first = lambda b, way: step(b, side, 0, way)
    second = lambda b, way: step(b, side, 1, way)
    half = own.shape[0] // 2
    left_other = swap(left_ops, "op", 1)
    behind, ahead = first(own, 1), first(own, -1)
    own_b, own_a = second(own, 1), second(own, -1)
    behind, ahead, left_other, right = lax.optimization_barrier(
        (behind, ahead, left_other, right_ops)
    )
    right_other = swap(right, "op", 1)
    far_low, far_high = first(behind[:half], 1), first(ahead[half:], -1)
    behind_b, behind_a = second(behind, 1), second(behind, -1)
    ahead_b, ahead_a = second(ahead, 1), second(ahead, -1)
    far_low, far_high, right_other = lax.optimization_barrier((far_low, far_high, right_other))
    (far,) = cut([[(0, 0, half), (1, 0, half)]], far_low, far_high)
    far_b, far_a = second(far, 1), second(far, -1)
    own_f, behind_f = second(own_b, 1), second(behind_b, 1)
    ahead_f, far_f = second(ahead_a, -1), second(far_a, -1)
    arrays = [
        own, behind, ahead, far, own_b, behind_b, ahead_b, far_b,
        own_a, behind_a, ahead_a, far_a, own_f, behind_f, ahead_f, far_f,
    ]
    places = [(i, 0, array.shape[0]) for i, array in enumerate(arrays)]
    return arrays, places, left_other, right_other


def ring_place(source, mine, side):
    away = (source - mine) % side
    return jnp.where(away == 0, 0, jnp.where(away == side - 1, 1, away + 1))


def body(wavefunction, left_ops, right_ops, sources, block_dims, energies):
    op_count = lax.axis_size("op")
    sec_count = lax.axis_size("sec")
    my_sec = lax.axis_index("sec")
    my_op = lax.axis_index("op")
    sec_dev, vectors, tile, _ = wavefunction.shape
    share = tile // op_count
    chips = op_count // vectors
    core = my_op % vectors
    side = 4

    live = jnp.arange(tile, dtype=jnp.int32)[None, :] < block_dims[:, None]
    window = live[:, :, None] & live[:, None, :]
    own = lax.dynamic_index_in_dim(wavefunction, core, 1, keepdims=False)
    own = jnp.where(window, own, jnp.zeros_like(own))

    arrays, places, left_other, right_other = gather_blocks(own, side, left_ops, right_ops)

    table = lax.dynamic_slice_in_dim(sources, my_sec * sec_dev, sec_dev, 1)
    table = jnp.concatenate([table, swap(table, "op", 1)], axis=0)
    table = jnp.transpose(table).reshape(-1)
    device, local = table // sec_dev, table % sec_dev
    in_y = ring_place(device // side, my_sec // side, side)
    in_x = ring_place(device % side, my_sec % side, side)
    slots = jnp.where(core == 0, in_y * side + in_x, in_x * side + in_y) * sec_dev + local

    wide = jnp.where(window[:, None], wavefunction, 0).astype(jnp.float32)
    norms = jnp.sum(wide * wide, axis=(2, 3))

    partial = partial_sums(
        slots, own, left_ops, left_other, right_ops, right_other, arrays, places, op_count
    )
    parts = lax.all_to_all(partial, "op", split_axis=0, concat_axis=0, tiled=True)
    lanes = parts.shape[2]
    parts = parts.reshape(chips, vectors, -1, share, lanes)
    numer = jnp.sum(parts[:, :, -1].astype(jnp.float32), axis=(0, 2, 3))
    numer = numer + jnp.sum(energies[:, None] * norms, axis=0)
    scalars = jnp.concatenate([numer, jnp.sum(norms, axis=0)])
    scalars = jnp.pad(scalars[None, None, :], ((0, 0), (0, 7), (0, 128 - 2 * vectors)))
    scalars = jnp.broadcast_to(scalars, (sec_count, 8, 128))
    scalars = lax.all_to_all(scalars, "sec", split_axis=0, concat_axis=0, tiled=True)
    scalars = jnp.sum(scalars[:, 0, : 2 * vectors], axis=0)
    rayleigh = scalars[:vectors] / scalars[vectors:]

    parts = parts[:, :, :-1].reshape(chips, vectors, sec_dev, tile // lanes, share, lanes)
    summed = jnp.sum(parts.astype(jnp.float32), axis=0)
    summed = jnp.concatenate([summed[:, :, cut] for cut in range(tile // lanes)], axis=3)
    summed = jnp.transpose(summed, (2, 1, 0, 3))
    rows = lax.dynamic_slice_in_dim(wavefunction, my_op * share, share, 2)
    live_rows = lax.dynamic_slice_in_dim(live, my_op * share, share, 1)
    row_window = jnp.transpose(live_rows)[:, :, None, None] & live[None, :, None, :]
    rows = jnp.where(row_window, jnp.transpose(rows, (2, 0, 1, 3)).astype(jnp.float32), 0.0)
    sigma = jnp.where(row_window, summed + energies[None, :, None, None] * rows, 0.0)
    residual = sigma - rayleigh[None, None, :, None] * rows
    return (residual, rayleigh)


def solution(mesh):
    in_specs = (
        P("sec", None, None, None),
        P("op", "sec", None, None),
        P("op", "sec", None, None),
        P("op", None),
        P("sec"),
        P("sec"),
    )
    out_specs = (P("op", "sec", None, None), P())
    return jax.shard_map(body, mesh=mesh, in_specs=in_specs, out_specs=out_specs, check_vma=False)
```

```python
import functools

import jax
import jax.numpy as jnp
from jax import lax
from jax.experimental import pallas as pl
from jax.experimental.pallas import tpu as pltpu
from jax.sharding import PartitionSpec as P

GROUP = 4
LANES = 128


def start_places(arrays, vec, sems):
    copies = []
    at = 0
    for i, array in enumerate(arrays):
        count = array.shape[0]
        copies.append(pltpu.make_async_copy(array, vec.at[pl.ds(at, count)], sems.at[i]))
        at += count
    for copy in copies:
        copy.start()
    return copies


def early_kernel(slots, left_a, left_b, right_a, right_b, *rest):
    arrays, (sums, vec, sems) = rest[:-3], rest[-3:]
    t = pl.program_id(0)
    half = left_a.shape[0]
    zero = vec.shape[0] - 1

    @pl.when(t == 0)
    def _():
        copies = start_places(arrays, vec, sems)
        vec[zero] = jnp.zeros(vec.shape[1:], vec.dtype)
        for copy in copies:
            copy.wait()

    for first in range(0, 2 * half, GROUP):
        inners, rights = [], []
        for k in range(first, first + GROUP):
            left = left_a if k < half else left_b
            right = right_a if k < half else right_b
            block = vec[jnp.minimum(slots[t * 2 * half + k], zero)]
            inner = jnp.dot(left[k % half, 0], block, preferred_element_type=jnp.float32)
            inners.append(inner.astype(jnp.bfloat16))
            rights.append(right[k % half, 0])
        term = lax.dot_general(
            jnp.concatenate(inners, axis=1), jnp.concatenate(rights, axis=1),
            (((1,), (1,)), ((), ())), preferred_element_type=jnp.float32,
        )
        if first == 0:
            sums[0] = term
        else:
            sums[0] += term


def early_sums(slots, left_a, left_b, right_a, right_b, arrays):
    half, sec_dev, tile, _ = left_a.shape
    total = sum(a.shape[0] for a in arrays)
    ops = pl.BlockSpec((half, 1, tile, tile), lambda t, s: (0, t, 0, 0))
    return pl.pallas_call(
        early_kernel,
        grid_spec=pltpu.PrefetchScalarGridSpec(
            num_scalar_prefetch=1,
            grid=(sec_dev,),
            in_specs=[ops, ops, ops, ops] + [pl.BlockSpec(memory_space=pl.ANY)] * len(arrays),
            out_specs=pl.BlockSpec((1, tile, tile), lambda t, s: (t, 0, 0)),
            scratch_shapes=[
                pltpu.VMEM((total + 1, tile, tile), jnp.bfloat16),
                pltpu.SemaphoreType.DMA((len(arrays),)),
            ],
        ),
        out_shape=jax.ShapeDtypeStruct((sec_dev, tile, tile), jnp.float32),
        compiler_params=pltpu.CompilerParams(vmem_limit_bytes=48 * 2**20),
        cost_estimate=pl.CostEstimate(
            flops=2 * 2 * sec_dev * 2 * half * tile**3,
            bytes_accessed=2 * tile * tile * (total + 8 * half * sec_dev),
            transcendentals=0,
        ),
    )(slots, left_a, left_b, right_a, right_b, *arrays)


def late_kernel(
    skip, slots, own, early, left_a, left_b, right_a, right_b, *rest
):
    arrays, (out, vec, lefts, rights, acc, todo, sems, left_sems, right_sems) = rest[:-9], rest[-9:]
    half, sec_dev, tile, _ = left_a.shape
    pairs = sec_dev * 2 * half
    op_count, _, lanes = out.shape
    share = tile // op_count
    cuts = tile // lanes

    def enlist(pair, count):
        is_late = slots[pair] >= skip

        @pl.when(is_late)
        def _():
            todo[count] = pair
            t, k = lax.div(pair, 2 * half), lax.rem(pair, 2 * half)

            @pl.when(k < half)
            def _():
                pltpu.make_async_copy(left_a.at[k, t], lefts.at[count], left_sems.at[count]).start()
                pltpu.make_async_copy(right_a.at[k, t], rights.at[count], right_sems.at[count]).start()

            @pl.when(k >= half)
            def _():
                pltpu.make_async_copy(
                    left_b.at[k - half, t], lefts.at[count], left_sems.at[count]
                ).start()
                pltpu.make_async_copy(
                    right_b.at[k - half, t], rights.at[count], right_sems.at[count]
                ).start()

        return count + is_late.astype(jnp.int32)

    copies = start_places(arrays, vec, sems)
    copies.append(pltpu.make_async_copy(early, acc, sems.at[len(arrays)]))
    copies[-1].start()
    count = lax.fori_loop(0, pairs, enlist, jnp.int32(0))
    for copy in copies:
        copy.wait()

    def add(at, blocks):
        inner = jnp.dot(lefts[at], blocks, preferred_element_type=jnp.float32)
        return lax.dot_general(
            inner.astype(jnp.bfloat16), rights[at], (((1,), (1,)), ((), ())),
            preferred_element_type=jnp.float32,
        )

    def wait(at):
        pltpu.make_async_copy(left_a.at[0, 0], lefts.at[at], left_sems.at[at]).wait()
        pltpu.make_async_copy(right_a.at[0, 0], rights.at[at], right_sems.at[at]).wait()

    def group(i, carry):
        ats = [i * GROUP + j for j in range(GROUP)]
        for at in ats:
            wait(at)
        terms = []
        for at in ats:
            block = vec[slots[todo[at]] - skip]
            terms.append(add(at, block))
        for at, term in zip(ats, terms):
            acc[lax.div(todo[at], 2 * half)] += term
        return carry

    def single(at, carry):
        wait(at)
        block = vec[slots[todo[at]] - skip]
        acc[lax.div(todo[at], 2 * half)] += add(at, block)
        return carry

    groups = lax.div(count, GROUP)
    lax.fori_loop(0, groups, group, 0)
    lax.fori_loop(groups * GROUP, count, single, 0)

    dots = jnp.zeros((8, tile), jnp.float32)
    for t in range(sec_dev):
        total = acc[t]
        for cut in range(cuts):
            part = total[:, cut * lanes : (cut + 1) * lanes].reshape(op_count, share, lanes)
            row = (t * cuts + cut) * share
            out[:, row : row + share, :] = part.astype(out.dtype)
        mine = own[t].astype(jnp.float32) * total
        dots += jnp.sum(mine.reshape(tile // 8, 8, tile), axis=0)
    row = jnp.sum(dots, axis=0, keepdims=True)
    row = sum(row[:, cut * lanes : (cut + 1) * lanes] for cut in range(cuts))
    high = row.astype(jnp.bfloat16).astype(jnp.float32)
    mid = (row - high).astype(jnp.bfloat16).astype(jnp.float32)
    low = row - high - mid
    at = lax.broadcasted_iota(jnp.int32, (share, lanes), 0)
    slab = jnp.where(at == 0, high, jnp.where(at == 1, mid, jnp.where(at == 2, low, 0.0)))
    slab = slab.astype(out.dtype)
    out[:, sec_dev * cuts * share :, :] = jnp.broadcast_to(slab[None], (op_count, share, lanes))


def late_sums(slots, own, early, left_a, left_b, right_a, right_b, arrays, skip, op_count):
    half, sec_dev, tile, _ = left_a.shape
    pairs = sec_dev * 2 * half
    share = tile // op_count
    total = sum(a.shape[0] for a in arrays)
    out_shape = (op_count, (sec_dev * (tile // LANES) + 1) * share, LANES)
    whole = pl.BlockSpec(memory_space=pltpu.VMEM)
    return pl.pallas_call(
        functools.partial(late_kernel, skip),
        grid_spec=pltpu.PrefetchScalarGridSpec(
            num_scalar_prefetch=1,
            grid=(),
            in_specs=[whole] + [pl.BlockSpec(memory_space=pl.ANY)] * (5 + len(arrays)),
            out_specs=whole,
            scratch_shapes=[
                pltpu.VMEM((total, tile, tile), jnp.bfloat16),
                pltpu.VMEM((pairs, tile, tile), jnp.bfloat16),
                pltpu.VMEM((pairs, tile, tile), jnp.bfloat16),
                pltpu.VMEM((sec_dev, tile, tile), jnp.float32),
                pltpu.SMEM((pairs,), jnp.int32),
                pltpu.SemaphoreType.DMA((len(arrays) + 1,)),
                pltpu.SemaphoreType.DMA((pairs,)),
                pltpu.SemaphoreType.DMA((pairs,)),
            ],
        ),
        out_shape=jax.ShapeDtypeStruct(out_shape, jnp.bfloat16),
        compiler_params=pltpu.CompilerParams(vmem_limit_bytes=48 * 2**20),
        cost_estimate=pl.CostEstimate(
            flops=2 * sec_dev * half * tile**3,
            bytes_accessed=2 * tile * tile * (total + 2 * half * sec_dev),
            transcendentals=0,
        ),
    )(slots, own, early, left_a, left_b, right_a, right_b, *arrays)


def swap(x, axis, mask):
    count = lax.axis_size(axis)
    return lax.ppermute(x, axis, [(i, i ^ mask) for i in range(count)])


def step(x, side, ring, way):
    perm = []
    for op in range(lax.axis_size("op")):
        for at in range(side * side):
            y, x_ = at // side, at % side
            if (op + ring) % 2 == 0:
                x_ = (x_ + way) % side
            else:
                y = (y + way) % side
            perm.append((op * side * side + at, op * side * side + y * side + x_))
    return lax.ppermute(x, ("op", "sec"), perm)


def cut_kernel(plan, count, *refs):
    arrays, outs = refs[:count], refs[count:]
    for out, parts in zip(outs, plan):
        at = 0
        for array, first, size in parts:
            out[pl.ds(at, size)] = arrays[array][pl.ds(first, size)]
            at += size


def cut(plan, *arrays):
    block, dtype = arrays[0].shape[1:], arrays[0].dtype
    sizes = [sum(size for _, _, size in parts) for parts in plan]
    return pl.pallas_call(
        functools.partial(cut_kernel, plan, len(arrays)),
        in_specs=[pl.BlockSpec(memory_space=pltpu.VMEM)] * len(arrays),
        out_specs=[pl.BlockSpec(memory_space=pltpu.VMEM)] * len(plan),
        out_shape=[jax.ShapeDtypeStruct((size,) + block, dtype) for size in sizes],
    )(*arrays)


def gather_blocks(own, side, left_ops, right_ops):
    first = lambda b, way: step(b, side, 0, way)
    second = lambda b, way: step(b, side, 1, way)
    half = own.shape[0] // 2
    left_other = swap(left_ops, "op", 1)
    behind, ahead = first(own, 1), first(own, -1)
    own_b, own_a = second(own, 1), second(own, -1)
    behind, ahead, own_b, own_a, left_other, right = lax.optimization_barrier(
        (behind, ahead, own_b, own_a, left_other, right_ops)
    )
    right_other = swap(right, "op", 1)
    far_low, far_high = first(behind[:half], 1), first(ahead[half:], -1)
    behind_b, behind_a = second(behind, 1), second(behind, -1)
    ahead_b, ahead_a = second(ahead, 1), second(ahead, -1)
    far_low, far_high, right_other = lax.optimization_barrier((far_low, far_high, right_other))
    (far,) = cut([[(0, 0, half), (1, 0, half)]], far_low, far_high)
    far_b, far_a = second(far, 1), second(far, -1)
    own_f, behind_f = second(own_b, 1), second(behind_b, 1)
    ahead_f, far_f = second(ahead_a, -1), second(far_a, -1)
    early = [
        own, behind, ahead, far, own_b, behind_b, ahead_b, far_b,
        own_a, behind_a, ahead_a, far_a,
    ]
    return early, [own_f, behind_f, ahead_f, far_f], left_other, right_other


def ring_place(source, mine, side):
    away = (source - mine) % side
    return jnp.where(away == 0, 0, jnp.where(away == side - 1, 1, away + 1))


def body(wavefunction, left_ops, right_ops, sources, block_dims, energies):
    op_count = lax.axis_size("op")
    sec_count = lax.axis_size("sec")
    my_sec = lax.axis_index("sec")
    my_op = lax.axis_index("op")
    sec_dev, vectors, tile, _ = wavefunction.shape
    share = tile // op_count
    chips = op_count // vectors
    core = my_op % vectors
    side = 4

    live = jnp.arange(tile, dtype=jnp.int32)[None, :] < block_dims[:, None]
    window = live[:, :, None] & live[:, None, :]
    own = lax.dynamic_index_in_dim(wavefunction, core, 1, keepdims=False)
    own = jnp.where(window, own, jnp.zeros_like(own))

    early, late, left_other, right_other = gather_blocks(own, side, left_ops, right_ops)
    skip = sum(a.shape[0] for a in early)

    table = lax.dynamic_slice_in_dim(sources, my_sec * sec_dev, sec_dev, 1)
    table = jnp.concatenate([table, swap(table, "op", 1)], axis=0)
    table = jnp.transpose(table).reshape(-1)
    device, local = table // sec_dev, table % sec_dev
    in_y = ring_place(device // side, my_sec // side, side)
    in_x = ring_place(device % side, my_sec % side, side)
    slots = jnp.where(core == 0, in_y * side + in_x, in_x * side + in_y) * sec_dev + local

    wide = jnp.where(window[:, None], wavefunction, 0).astype(jnp.float32)
    norms = jnp.sum(wide * wide, axis=(2, 3))

    ops = (left_ops, left_other, right_ops, right_other)
    sums = early_sums(slots, *ops, early)
    partial = late_sums(slots, own, sums, *ops, late, skip, op_count)
    parts = lax.all_to_all(partial, "op", split_axis=0, concat_axis=0, tiled=True)
    lanes = LANES
    parts = parts.reshape(chips, vectors, -1, share, lanes)
    numer = jnp.sum(parts[:, :, -1].astype(jnp.float32), axis=(0, 2, 3))
    numer = numer + jnp.sum(energies[:, None] * norms, axis=0)
    scalars = jnp.concatenate([numer, jnp.sum(norms, axis=0)])
    scalars = jnp.pad(scalars[None, None, :], ((0, 0), (0, 7), (0, 128 - 2 * vectors)))
    scalars = jnp.broadcast_to(scalars, (sec_count, 8, 128))
    scalars = lax.all_to_all(scalars, "sec", split_axis=0, concat_axis=0, tiled=True)
    scalars = jnp.sum(scalars[:, 0, : 2 * vectors], axis=0)
    rayleigh = scalars[:vectors] / scalars[vectors:]

    parts = parts[:, :, :-1].reshape(chips, vectors, sec_dev, tile // lanes, share, lanes)
    summed = jnp.sum(parts.astype(jnp.float32), axis=0)
    summed = jnp.concatenate([summed[:, :, cut] for cut in range(tile // lanes)], axis=3)
    summed = jnp.transpose(summed, (2, 1, 0, 3))
    rows = lax.dynamic_slice_in_dim(wavefunction, my_op * share, share, 2)
    live_rows = lax.dynamic_slice_in_dim(live, my_op * share, share, 1)
    row_window = jnp.transpose(live_rows)[:, :, None, None] & live[None, :, None, :]
    rows = jnp.where(row_window, jnp.transpose(rows, (2, 0, 1, 3)).astype(jnp.float32), 0.0)
    sigma = jnp.where(row_window, summed + energies[None, :, None, None] * rows, 0.0)
    residual = sigma - rayleigh[None, None, :, None] * rows
    return (residual, rayleigh)


def solution(mesh):
    in_specs = (
        P("sec", None, None, None),
        P("op", "sec", None, None),
        P("op", "sec", None, None),
        P("op", None),
        P("sec"),
        P("sec"),
    )
    out_specs = (P("op", "sec", None, None), P())
    return jax.shard_map(body, mesh=mesh, in_specs=in_specs, out_specs=out_specs, check_vma=False)
```

```python
import functools

import jax
import jax.numpy as jnp
from jax import lax
from jax.experimental import pallas as pl
from jax.experimental.pallas import tpu as pltpu
from jax.sharding import PartitionSpec as P

GROUP = 4
LANES = 128


def start_places(arrays, vec, sems):
    copies = []
    at = 0
    for i, array in enumerate(arrays):
        count = array.shape[0]
        copies.append(pltpu.make_async_copy(array, vec.at[pl.ds(at, count)], sems.at[i]))
        at += count
    for copy in copies:
        copy.start()
    return copies


def early_kernel(slots, left_a, left_b, right_a, right_b, *rest):
    arrays, (sums, vec, sems) = rest[:-3], rest[-3:]
    t = pl.program_id(0)
    half = left_a.shape[0]
    zero = vec.shape[0] - 1

    @pl.when(t == 0)
    def _():
        copies = start_places(arrays, vec, sems)
        vec[zero] = jnp.zeros(vec.shape[1:], vec.dtype)
        for copy in copies:
            copy.wait()

    for first in range(0, 2 * half, GROUP):
        inners, rights = [], []
        for k in range(first, first + GROUP):
            left = left_a if k < half else left_b
            right = right_a if k < half else right_b
            block = vec[jnp.minimum(slots[t * 2 * half + k], zero)]
            inner = jnp.dot(left[k % half, 0], block, preferred_element_type=jnp.float32)
            inners.append(inner.astype(jnp.bfloat16))
            rights.append(right[k % half, 0])
        term = lax.dot_general(
            jnp.concatenate(inners, axis=1), jnp.concatenate(rights, axis=1),
            (((1,), (1,)), ((), ())), preferred_element_type=jnp.float32,
        )
        if first == 0:
            sums[0] = term
        else:
            sums[0] += term


def early_sums(slots, left_a, left_b, right_a, right_b, arrays):
    half, sec_dev, tile, _ = left_a.shape
    total = sum(a.shape[0] for a in arrays)
    ops = pl.BlockSpec((half, 1, tile, tile), lambda t, s: (0, t, 0, 0))
    return pl.pallas_call(
        early_kernel,
        grid_spec=pltpu.PrefetchScalarGridSpec(
            num_scalar_prefetch=1,
            grid=(sec_dev,),
            in_specs=[ops, ops, ops, ops] + [pl.BlockSpec(memory_space=pl.ANY)] * len(arrays),
            out_specs=pl.BlockSpec((1, tile, tile), lambda t, s: (t, 0, 0)),
            scratch_shapes=[
                pltpu.VMEM((total + 1, tile, tile), jnp.bfloat16),
                pltpu.SemaphoreType.DMA((len(arrays),)),
            ],
        ),
        out_shape=jax.ShapeDtypeStruct((sec_dev, tile, tile), jnp.float32),
        compiler_params=pltpu.CompilerParams(vmem_limit_bytes=48 * 2**20),
        cost_estimate=pl.CostEstimate(
            flops=2 * 2 * sec_dev * 2 * half * tile**3,
            bytes_accessed=2 * tile * tile * (total + 8 * half * sec_dev),
            transcendentals=0,
        ),
    )(slots, left_a, left_b, right_a, right_b, *arrays)


def late_kernel(
    skip, slots, own, early, left_a, left_b, right_a, right_b, *rest
):
    arrays, (out, vec, lefts, rights, acc, todo, sems, left_sems, right_sems) = rest[:-9], rest[-9:]
    half, sec_dev, tile, _ = left_a.shape
    pairs = sec_dev * 2 * half
    op_count, _, lanes = out.shape
    share = tile // op_count
    cuts = tile // lanes

    def enlist(pair, count):
        is_late = slots[pair] >= skip

        @pl.when(is_late)
        def _():
            todo[count] = pair
            t, k = lax.div(pair, 2 * half), lax.rem(pair, 2 * half)

            @pl.when(k < half)
            def _():
                pltpu.make_async_copy(left_a.at[k, t], lefts.at[count], left_sems.at[count]).start()
                pltpu.make_async_copy(right_a.at[k, t], rights.at[count], right_sems.at[count]).start()

            @pl.when(k >= half)
            def _():
                pltpu.make_async_copy(
                    left_b.at[k - half, t], lefts.at[count], left_sems.at[count]
                ).start()
                pltpu.make_async_copy(
                    right_b.at[k - half, t], rights.at[count], right_sems.at[count]
                ).start()

        return count + is_late.astype(jnp.int32)

    copies = start_places(arrays, vec, sems)
    copies.append(pltpu.make_async_copy(early, acc, sems.at[len(arrays)]))
    copies[-1].start()
    count = lax.fori_loop(0, pairs, enlist, jnp.int32(0))
    for copy in copies:
        copy.wait()

    def add(at, blocks):
        inner = jnp.dot(lefts[at], blocks, preferred_element_type=jnp.float32)
        return lax.dot_general(
            inner.astype(jnp.bfloat16), rights[at], (((1,), (1,)), ((), ())),
            preferred_element_type=jnp.float32,
        )

    def wait(at):
        pltpu.make_async_copy(left_a.at[0, 0], lefts.at[at], left_sems.at[at]).wait()
        pltpu.make_async_copy(right_a.at[0, 0], rights.at[at], right_sems.at[at]).wait()

    def group(i, carry):
        ats = [i * GROUP + j for j in range(GROUP)]
        for at in ats:
            wait(at)
        terms = []
        for at in ats:
            block = vec[slots[todo[at]] - skip]
            terms.append(add(at, block))
        for at, term in zip(ats, terms):
            acc[lax.div(todo[at], 2 * half)] += term
        return carry

    def single(at, carry):
        wait(at)
        block = vec[slots[todo[at]] - skip]
        acc[lax.div(todo[at], 2 * half)] += add(at, block)
        return carry

    groups = lax.div(count, GROUP)
    lax.fori_loop(0, groups, group, 0)
    lax.fori_loop(groups * GROUP, count, single, 0)

    dots = jnp.zeros((8, tile), jnp.float32)
    for t in range(sec_dev):
        total = acc[t]
        for cut in range(cuts):
            part = total[:, cut * lanes : (cut + 1) * lanes].reshape(op_count, share, lanes)
            row = (t * cuts + cut) * share
            out[:, row : row + share, :] = part.astype(out.dtype)
        mine = own[t].astype(jnp.float32) * total
        dots += jnp.sum(mine.reshape(tile // 8, 8, tile), axis=0)
    row = jnp.sum(dots, axis=0, keepdims=True)
    row = sum(row[:, cut * lanes : (cut + 1) * lanes] for cut in range(cuts))
    high = row.astype(jnp.bfloat16).astype(jnp.float32)
    mid = (row - high).astype(jnp.bfloat16).astype(jnp.float32)
    low = row - high - mid
    at = lax.broadcasted_iota(jnp.int32, (share, lanes), 0)
    slab = jnp.where(at == 0, high, jnp.where(at == 1, mid, jnp.where(at == 2, low, 0.0)))
    slab = slab.astype(out.dtype)
    out[:, sec_dev * cuts * share :, :] = jnp.broadcast_to(slab[None], (op_count, share, lanes))


def late_sums(slots, own, early, left_a, left_b, right_a, right_b, arrays, skip, op_count):
    half, sec_dev, tile, _ = left_a.shape
    pairs = sec_dev * 2 * half
    share = tile // op_count
    total = sum(a.shape[0] for a in arrays)
    out_shape = (op_count, (sec_dev * (tile // LANES) + 1) * share, LANES)
    whole = pl.BlockSpec(memory_space=pltpu.VMEM)
    return pl.pallas_call(
        functools.partial(late_kernel, skip),
        grid_spec=pltpu.PrefetchScalarGridSpec(
            num_scalar_prefetch=1,
            grid=(),
            in_specs=[whole, pl.BlockSpec(memory_space=pltpu.HBM)]
            + [pl.BlockSpec(memory_space=pl.ANY)] * (4 + len(arrays)),
            out_specs=whole,
            scratch_shapes=[
                pltpu.VMEM((total, tile, tile), jnp.bfloat16),
                pltpu.VMEM((pairs, tile, tile), jnp.bfloat16),
                pltpu.VMEM((pairs, tile, tile), jnp.bfloat16),
                pltpu.VMEM((sec_dev, tile, tile), jnp.float32),
                pltpu.SMEM((pairs,), jnp.int32),
                pltpu.SemaphoreType.DMA((len(arrays) + 1,)),
                pltpu.SemaphoreType.DMA((pairs,)),
                pltpu.SemaphoreType.DMA((pairs,)),
            ],
        ),
        out_shape=jax.ShapeDtypeStruct(out_shape, jnp.bfloat16),
        compiler_params=pltpu.CompilerParams(vmem_limit_bytes=48 * 2**20),
        cost_estimate=pl.CostEstimate(
            flops=2 * sec_dev * half * tile**3,
            bytes_accessed=2 * tile * tile * (total + 2 * half * sec_dev),
            transcendentals=0,
        ),
    )(slots, own, early, left_a, left_b, right_a, right_b, *arrays)


def swap(x, axis, mask):
    count = lax.axis_size(axis)
    return lax.ppermute(x, axis, [(i, i ^ mask) for i in range(count)])


def step(x, side, ring, way):
    perm = []
    for op in range(lax.axis_size("op")):
        for at in range(side * side):
            y, x_ = at // side, at % side
            if (op + ring) % 2 == 0:
                x_ = (x_ + way) % side
            else:
                y = (y + way) % side
            perm.append((op * side * side + at, op * side * side + y * side + x_))
    return lax.ppermute(x, ("op", "sec"), perm)


def gather_blocks(own, side, left_ops, right_ops):
    first = lambda b, way: step(b, side, 0, way)
    second = lambda b, way: step(b, side, 1, way)
    left_other = swap(left_ops, "op", 1)
    behind, ahead = first(own, 1), first(own, -1)
    own, behind, ahead, left_other, right = lax.optimization_barrier(
        (own, behind, ahead, left_other, right_ops)
    )
    right_other = swap(right, "op", 1)
    far = first(behind, 1)
    own_a, behind_a, ahead_a = second(own, -1), second(behind, -1), second(ahead, -1)
    own, behind, ahead, far, right_other = lax.optimization_barrier(
        (own, behind, ahead, far, right_other)
    )
    far_a = second(far, -1)
    own_b, behind_b = second(own, 1), second(behind, 1)
    ahead_b, far_b = second(ahead, 1), second(far, 1)
    own_f, behind_f = second(own_b, 1), second(behind_a, -1)
    ahead_f, far_f = second(ahead_a, -1), second(far_a, -1)
    early = [
        own, behind, ahead, far, own_b, behind_b, ahead_b, far_b,
        own_a, behind_a, ahead_a, far_a,
    ]
    return early, [own_f, behind_f, ahead_f, far_f], left_other, right_other


def ring_place(source, mine, side):
    away = (source - mine) % side
    return jnp.where(away == 0, 0, jnp.where(away == side - 1, 1, away + 1))


def body(wavefunction, left_ops, right_ops, sources, block_dims, energies):
    op_count = lax.axis_size("op")
    sec_count = lax.axis_size("sec")
    my_sec = lax.axis_index("sec")
    my_op = lax.axis_index("op")
    sec_dev, vectors, tile, _ = wavefunction.shape
    share = tile // op_count
    chips = op_count // vectors
    core = my_op % vectors
    side = 4

    live = jnp.arange(tile, dtype=jnp.int32)[None, :] < block_dims[:, None]
    window = live[:, :, None] & live[:, None, :]
    own = lax.dynamic_index_in_dim(wavefunction, core, 1, keepdims=False)
    own = jnp.where(window, own, jnp.zeros_like(own))

    early, late, left_other, right_other = gather_blocks(own, side, left_ops, right_ops)
    skip = sum(a.shape[0] for a in early)

    table = lax.dynamic_slice_in_dim(sources, my_sec * sec_dev, sec_dev, 1)
    table = jnp.concatenate([table, swap(table, "op", 1)], axis=0)
    table = jnp.transpose(table).reshape(-1)
    device, local = table // sec_dev, table % sec_dev
    in_y = ring_place(device // side, my_sec // side, side)
    in_x = ring_place(device % side, my_sec % side, side)
    slots = jnp.where(core == 0, in_y * side + in_x, in_x * side + in_y) * sec_dev + local

    wide = jnp.where(window[:, None], wavefunction, 0).astype(jnp.float32)
    norms = jnp.sum(wide * wide, axis=(2, 3))

    ops = (left_ops, left_other, right_ops, right_other)
    sums = early_sums(slots, *ops, early)
    partial = late_sums(slots, own, sums, *ops, late, skip, op_count)
    parts = lax.all_to_all(partial, "op", split_axis=0, concat_axis=0, tiled=True)
    lanes = LANES
    parts = parts.reshape(chips, vectors, -1, share, lanes)
    numer = jnp.sum(parts[:, :, -1].astype(jnp.float32), axis=(0, 2, 3))
    numer = numer + jnp.sum(energies[:, None] * norms, axis=0)
    scalars = jnp.concatenate([numer, jnp.sum(norms, axis=0)])
    scalars = jnp.pad(scalars[None, None, :], ((0, 0), (0, 7), (0, 128 - 2 * vectors)))
    scalars = jnp.broadcast_to(scalars, (sec_count, 8, 128))
    scalars = lax.all_to_all(scalars, "sec", split_axis=0, concat_axis=0, tiled=True)
    scalars = jnp.sum(scalars[:, 0, : 2 * vectors], axis=0)
    rayleigh = scalars[:vectors] / scalars[vectors:]

    parts = parts[:, :, :-1].reshape(chips, vectors, sec_dev, tile // lanes, share, lanes)
    summed = jnp.sum(parts.astype(jnp.float32), axis=0)
    summed = jnp.concatenate([summed[:, :, cut] for cut in range(tile // lanes)], axis=3)
    summed = jnp.transpose(summed, (2, 1, 0, 3))
    rows = lax.dynamic_slice_in_dim(wavefunction, my_op * share, share, 2)
    live_rows = lax.dynamic_slice_in_dim(live, my_op * share, share, 1)
    row_window = jnp.transpose(live_rows)[:, :, None, None] & live[None, :, None, :]
    rows = jnp.where(row_window, jnp.transpose(rows, (2, 0, 1, 3)).astype(jnp.float32), 0.0)
    sigma = jnp.where(row_window, summed + energies[None, :, None, None] * rows, 0.0)
    residual = sigma - rayleigh[None, None, :, None] * rows
    return (residual, rayleigh)


def solution(mesh):
    in_specs = (
        P("sec", None, None, None),
        P("op", "sec", None, None),
        P("op", "sec", None, None),
        P("op", None),
        P("sec"),
        P("sec"),
    )
    out_specs = (P("op", "sec", None, None), P())
    return jax.shard_map(body, mesh=mesh, in_specs=in_specs, out_specs=out_specs, check_vma=False)
```

```python
import functools

import jax
import jax.numpy as jnp
from jax import lax
from jax.experimental import pallas as pl
from jax.experimental.pallas import tpu as pltpu
from jax.sharding import PartitionSpec as P

GROUP = 4
LANES = 128


def start_places(arrays, vec, sems):
    copies = []
    at = 0
    for i, array in enumerate(arrays):
        count = array.shape[0]
        copies.append(pltpu.make_async_copy(array, vec.at[pl.ds(at, count)], sems.at[i]))
        at += count
    for copy in copies:
        copy.start()
    return copies


def early_kernel(slots, left_a, left_b, right_a, right_b, *rest):
    arrays, (sums, vec, sems) = rest[:-3], rest[-3:]
    t = pl.program_id(0)
    half = left_a.shape[0]
    zero = vec.shape[0] - 1

    @pl.when(t == 0)
    def _():
        copies = start_places(arrays, vec, sems)
        vec[zero] = jnp.zeros(vec.shape[1:], vec.dtype)
        for copy in copies:
            copy.wait()

    for first in range(0, 2 * half, GROUP):
        inners, rights = [], []
        for k in range(first, first + GROUP):
            left = left_a if k < half else left_b
            right = right_a if k < half else right_b
            block = vec[jnp.minimum(slots[t * 2 * half + k], zero)]
            inner = jnp.dot(left[k % half, 0], block, preferred_element_type=jnp.float32)
            inners.append(inner.astype(jnp.bfloat16))
            rights.append(right[k % half, 0])
        term = lax.dot_general(
            jnp.concatenate(inners, axis=1), jnp.concatenate(rights, axis=1),
            (((1,), (1,)), ((), ())), preferred_element_type=jnp.float32,
        )
        if first == 0:
            sums[0] = term
        else:
            sums[0] += term


def early_sums(slots, left_a, left_b, right_a, right_b, arrays):
    half, sec_dev, tile, _ = left_a.shape
    total = sum(a.shape[0] for a in arrays)
    ops = pl.BlockSpec((half, 1, tile, tile), lambda t, s: (0, t, 0, 0))
    return pl.pallas_call(
        early_kernel,
        grid_spec=pltpu.PrefetchScalarGridSpec(
            num_scalar_prefetch=1,
            grid=(sec_dev,),
            in_specs=[ops, ops, ops, ops] + [pl.BlockSpec(memory_space=pl.ANY)] * len(arrays),
            out_specs=pl.BlockSpec((1, tile, tile), lambda t, s: (t, 0, 0)),
            scratch_shapes=[
                pltpu.VMEM((total + 1, tile, tile), jnp.bfloat16),
                pltpu.SemaphoreType.DMA((len(arrays),)),
            ],
        ),
        out_shape=jax.ShapeDtypeStruct((sec_dev, tile, tile), jnp.float32),
        compiler_params=pltpu.CompilerParams(vmem_limit_bytes=48 * 2**20),
        cost_estimate=pl.CostEstimate(
            flops=2 * 2 * sec_dev * 2 * half * tile**3,
            bytes_accessed=2 * tile * tile * (total + 8 * half * sec_dev),
            transcendentals=0,
        ),
    )(slots, left_a, left_b, right_a, right_b, *arrays)


def late_kernel(
    skip, slots, own, early, left_a, left_b, right_a, right_b, *rest
):
    arrays, (out, vec, lefts, rights, acc, todo, sems, left_sems, right_sems) = rest[:-9], rest[-9:]
    half, sec_dev, tile, _ = left_a.shape
    pairs = sec_dev * 2 * half
    op_count, _, lanes = out.shape
    share = tile // op_count
    cuts = tile // lanes

    def enlist(pair, count):
        is_late = slots[pair] >= skip

        @pl.when(is_late)
        def _():
            todo[count] = pair
            t, k = lax.div(pair, 2 * half), lax.rem(pair, 2 * half)

            @pl.when(k < half)
            def _():
                pltpu.make_async_copy(left_a.at[k, t], lefts.at[count], left_sems.at[count]).start()
                pltpu.make_async_copy(right_a.at[k, t], rights.at[count], right_sems.at[count]).start()

            @pl.when(k >= half)
            def _():
                pltpu.make_async_copy(
                    left_b.at[k - half, t], lefts.at[count], left_sems.at[count]
                ).start()
                pltpu.make_async_copy(
                    right_b.at[k - half, t], rights.at[count], right_sems.at[count]
                ).start()

        return count + is_late.astype(jnp.int32)

    copies = start_places(arrays, vec, sems)
    copies.append(pltpu.make_async_copy(early, acc, sems.at[len(arrays)]))
    copies[-1].start()
    count = lax.fori_loop(0, pairs, enlist, jnp.int32(0))
    for copy in copies:
        copy.wait()

    def add(at, blocks):
        inner = jnp.dot(lefts[at], blocks, preferred_element_type=jnp.float32)
        return lax.dot_general(
            inner.astype(jnp.bfloat16), rights[at], (((1,), (1,)), ((), ())),
            preferred_element_type=jnp.float32,
        )

    def wait(at):
        pltpu.make_async_copy(left_a.at[0, 0], lefts.at[at], left_sems.at[at]).wait()
        pltpu.make_async_copy(right_a.at[0, 0], rights.at[at], right_sems.at[at]).wait()

    def group(i, carry):
        ats = [i * GROUP + j for j in range(GROUP)]
        for at in ats:
            wait(at)
        terms = []
        for at in ats:
            block = vec[slots[todo[at]] - skip]
            terms.append(add(at, block))
        for at, term in zip(ats, terms):
            acc[lax.div(todo[at], 2 * half)] += term
        return carry

    def single(at, carry):
        wait(at)
        block = vec[slots[todo[at]] - skip]
        acc[lax.div(todo[at], 2 * half)] += add(at, block)
        return carry

    groups = lax.div(count, GROUP)
    lax.fori_loop(0, groups, group, 0)
    lax.fori_loop(groups * GROUP, count, single, 0)

    dots = jnp.zeros((8, tile), jnp.float32)
    for t in range(sec_dev):
        total = acc[t]
        for cut in range(cuts):
            part = total[:, cut * lanes : (cut + 1) * lanes].reshape(op_count, share, lanes)
            row = (t * cuts + cut) * share
            out[:, row : row + share, :] = part.astype(out.dtype)
        mine = own[t].astype(jnp.float32) * total
        dots += jnp.sum(mine.reshape(tile // 8, 8, tile), axis=0)
    row = jnp.sum(dots, axis=0, keepdims=True)
    row = sum(row[:, cut * lanes : (cut + 1) * lanes] for cut in range(cuts))
    high = row.astype(jnp.bfloat16).astype(jnp.float32)
    mid = (row - high).astype(jnp.bfloat16).astype(jnp.float32)
    low = row - high - mid
    at = lax.broadcasted_iota(jnp.int32, (share, lanes), 0)
    slab = jnp.where(at == 0, high, jnp.where(at == 1, mid, jnp.where(at == 2, low, 0.0)))
    slab = slab.astype(out.dtype)
    out[:, sec_dev * cuts * share :, :] = jnp.broadcast_to(slab[None], (op_count, share, lanes))


def late_sums(slots, own, early, left_a, left_b, right_a, right_b, arrays, skip, op_count):
    half, sec_dev, tile, _ = left_a.shape
    pairs = sec_dev * 2 * half
    share = tile // op_count
    total = sum(a.shape[0] for a in arrays)
    out_shape = (op_count, (sec_dev * (tile // LANES) + 1) * share, LANES)
    whole = pl.BlockSpec(memory_space=pltpu.VMEM)
    return pl.pallas_call(
        functools.partial(late_kernel, skip),
        grid_spec=pltpu.PrefetchScalarGridSpec(
            num_scalar_prefetch=1,
            grid=(),
            in_specs=[whole, pl.BlockSpec(memory_space=pltpu.HBM)]
            + [pl.BlockSpec(memory_space=pl.ANY)] * (4 + len(arrays)),
            out_specs=whole,
            scratch_shapes=[
                pltpu.VMEM((total, tile, tile), jnp.bfloat16),
                pltpu.VMEM((pairs, tile, tile), jnp.bfloat16),
                pltpu.VMEM((pairs, tile, tile), jnp.bfloat16),
                pltpu.VMEM((sec_dev, tile, tile), jnp.float32),
                pltpu.SMEM((pairs,), jnp.int32),
                pltpu.SemaphoreType.DMA((len(arrays) + 1,)),
                pltpu.SemaphoreType.DMA((pairs,)),
                pltpu.SemaphoreType.DMA((pairs,)),
            ],
        ),
        out_shape=jax.ShapeDtypeStruct(out_shape, jnp.bfloat16),
        compiler_params=pltpu.CompilerParams(vmem_limit_bytes=48 * 2**20),
        cost_estimate=pl.CostEstimate(
            flops=2 * sec_dev * half * tile**3,
            bytes_accessed=2 * tile * tile * (total + 2 * half * sec_dev),
            transcendentals=0,
        ),
    )(slots, own, early, left_a, left_b, right_a, right_b, *arrays)


def swap(x, axis, mask):
    count = lax.axis_size(axis)
    return lax.ppermute(x, axis, [(i, i ^ mask) for i in range(count)])


def step(x, side, ring, way):
    perm = []
    for op in range(lax.axis_size("op")):
        for at in range(side * side):
            y, x_ = at // side, at % side
            if (op + ring) % 2 == 0:
                x_ = (x_ + way) % side
            else:
                y = (y + way) % side
            perm.append((op * side * side + at, op * side * side + y * side + x_))
    return lax.ppermute(x, ("op", "sec"), perm)


def gather_blocks(own, side, left_ops, right_ops):
    first = lambda b, way: step(b, side, 0, way)
    second = lambda b, way: step(b, side, 1, way)
    left_other = swap(left_ops, "op", 1)
    behind, ahead = first(own, 1), first(own, -1)
    own, behind, ahead, left_other, right = lax.optimization_barrier(
        (own, behind, ahead, left_other, right_ops)
    )
    right_other = swap(right, "op", 1)
    far = first(behind, 1)
    own_a, behind_a, ahead_a = second(own, -1), second(behind, -1), second(ahead, -1)
    own, behind, ahead, far, right_other = lax.optimization_barrier(
        (own, behind, ahead, far, right_other)
    )
    far_a, far_b = second(far, -1), second(far, 1)
    own_b, behind_b, ahead_b = second(own, 1), second(behind, 1), second(ahead, 1)
    own_f, behind_f = second(own_b, 1), second(behind_a, -1)
    ahead_f, far_f = second(ahead_a, -1), second(far_a, -1)
    early = [
        own, behind, ahead, far, own_b, behind_b, ahead_b, own_a, behind_a, ahead_a, far_a,
    ]
    late = [far_b, own_f, behind_f, ahead_f, far_f]
    return early, late, left_other, right_other


def array_place(place):
    return jnp.where(place == 7, 11, jnp.where((place > 7) & (place < 12), place - 1, place))


def ring_place(source, mine, side):
    away = (source - mine) % side
    return jnp.where(away == 0, 0, jnp.where(away == side - 1, 1, away + 1))


def body(wavefunction, left_ops, right_ops, sources, block_dims, energies):
    op_count = lax.axis_size("op")
    sec_count = lax.axis_size("sec")
    my_sec = lax.axis_index("sec")
    my_op = lax.axis_index("op")
    sec_dev, vectors, tile, _ = wavefunction.shape
    share = tile // op_count
    chips = op_count // vectors
    core = my_op % vectors
    side = 4

    own = lax.dynamic_index_in_dim(wavefunction, core, 1, keepdims=False)
    row = lax.broadcasted_iota(jnp.int32, own.shape, 1)
    column = lax.broadcasted_iota(jnp.int32, own.shape, 2)
    inside = jnp.maximum(row, column) < block_dims[:, None, None]
    own = jnp.where(inside, own, jnp.zeros_like(own))

    early, late, left_other, right_other = gather_blocks(own, side, left_ops, right_ops)
    skip = sum(a.shape[0] for a in early)

    table = lax.dynamic_slice_in_dim(sources, my_sec * sec_dev, sec_dev, 1)
    table = jnp.concatenate([table, swap(table, "op", 1)], axis=0)
    table = jnp.transpose(table).reshape(-1)
    device, local = table // sec_dev, table % sec_dev
    in_y = ring_place(device // side, my_sec // side, side)
    in_x = ring_place(device % side, my_sec % side, side)
    place = jnp.where(core == 0, in_y * side + in_x, in_x * side + in_y)
    slots = array_place(place) * sec_dev + local

    live = jnp.arange(tile, dtype=jnp.int32)[None, :] < block_dims[:, None]
    window = live[:, :, None] & live[:, None, :]
    wide = jnp.where(window[:, None], wavefunction, 0).astype(jnp.float32)
    norms = jnp.sum(wide * wide, axis=(2, 3))

    ops = (left_ops, left_other, right_ops, right_other)
    sums = early_sums(slots, *ops, early)
    partial = late_sums(slots, own, sums, *ops, late, skip, op_count)
    parts = lax.all_to_all(partial, "op", split_axis=0, concat_axis=0, tiled=True)
    lanes = LANES
    parts = parts.reshape(chips, vectors, -1, share, lanes)
    numer = jnp.sum(parts[:, :, -1].astype(jnp.float32), axis=(0, 2, 3))
    numer = numer + jnp.sum(energies[:, None] * norms, axis=0)
    scalars = jnp.concatenate([numer, jnp.sum(norms, axis=0)])
    scalars = jnp.pad(scalars[None, None, :], ((0, 0), (0, 7), (0, 128 - 2 * vectors)))
    scalars = jnp.broadcast_to(scalars, (sec_count, 8, 128))
    scalars = lax.all_to_all(scalars, "sec", split_axis=0, concat_axis=0, tiled=True)
    scalars = jnp.sum(scalars[:, 0, : 2 * vectors], axis=0)
    rayleigh = scalars[:vectors] / scalars[vectors:]

    parts = parts[:, :, :-1].reshape(chips, vectors, sec_dev, tile // lanes, share, lanes)
    summed = jnp.sum(parts.astype(jnp.float32), axis=0)
    summed = jnp.concatenate([summed[:, :, cut] for cut in range(tile // lanes)], axis=3)
    summed = jnp.transpose(summed, (2, 1, 0, 3))
    rows = lax.dynamic_slice_in_dim(wavefunction, my_op * share, share, 2)
    live_rows = lax.dynamic_slice_in_dim(live, my_op * share, share, 1)
    row_window = jnp.transpose(live_rows)[:, :, None, None] & live[None, :, None, :]
    rows = jnp.where(row_window, jnp.transpose(rows, (2, 0, 1, 3)).astype(jnp.float32), 0.0)
    sigma = jnp.where(row_window, summed + energies[None, :, None, None] * rows, 0.0)
    residual = sigma - rayleigh[None, None, :, None] * rows
    return (residual, rayleigh)


def solution(mesh):
    in_specs = (
        P("sec", None, None, None),
        P("op", "sec", None, None),
        P("op", "sec", None, None),
        P("op", None),
        P("sec"),
        P("sec"),
    )
    out_specs = (P("op", "sec", None, None), P())
    return jax.shard_map(body, mesh=mesh, in_specs=in_specs, out_specs=out_specs, check_vma=False)
```

```python
import functools

import jax
import jax.numpy as jnp
from jax import lax
from jax.experimental import pallas as pl
from jax.experimental.pallas import tpu as pltpu
from jax.sharding import PartitionSpec as P

GROUP = 4
LANES = 128


def stage_kernel(low, high, given, last, *refs):
    refs = list(refs)
    slots = refs.pop(0)
    own = refs.pop(0) if last else None
    sums = refs.pop(0) if given else None
    left_a, left_b, right_a, right_b = (refs.pop(0) for _ in range(4))
    vec, lefts, rights, acc, todo, sems, left_sems, right_sems = refs[-8:]
    arrays, out = refs[:-9], refs[-9]
    half, sec_dev, tile, _ = left_a.shape
    acc = acc if last else out

    copies = []
    at = 0
    for i, array in enumerate(arrays):
        copies.append(
            pltpu.make_async_copy(array, vec.at[pl.ds(at, array.shape[0])], sems.at[i])
        )
        at += array.shape[0]
    for copy in copies:
        copy.start()

    def enlist(pair, count):
        slot = slots[pair]
        is_mine = jnp.logical_and(slot >= low, slot < high)

        @pl.when(is_mine)
        def _():
            todo[count] = pair
            t, k = lax.div(pair, 2 * half), lax.rem(pair, 2 * half)

            @pl.when(k < half)
            def _():
                pltpu.make_async_copy(left_a.at[k, t], lefts.at[count], left_sems.at[count]).start()
                pltpu.make_async_copy(right_a.at[k, t], rights.at[count], right_sems.at[count]).start()

            @pl.when(k >= half)
            def _():
                pltpu.make_async_copy(
                    left_b.at[k - half, t], lefts.at[count], left_sems.at[count]
                ).start()
                pltpu.make_async_copy(
                    right_b.at[k - half, t], rights.at[count], right_sems.at[count]
                ).start()

        return count + is_mine.astype(jnp.int32)

    count = lax.fori_loop(0, sec_dev * 2 * half, enlist, jnp.int32(0))
    acc[...] = sums[...] if given else jnp.zeros(acc.shape, acc.dtype)
    for copy in copies:
        copy.wait()

    def wait(at):
        pltpu.make_async_copy(left_a.at[0, 0], lefts.at[at], left_sems.at[at]).wait()
        pltpu.make_async_copy(right_a.at[0, 0], rights.at[at], right_sems.at[at]).wait()

    def product(at):
        block = vec[slots[todo[at]] - low]
        inner = jnp.dot(lefts[at], block, preferred_element_type=jnp.float32)
        return lax.dot_general(
            inner.astype(jnp.bfloat16), rights[at], (((1,), (1,)), ((), ())),
            preferred_element_type=jnp.float32,
        )

    def several(i, carry):
        ats = [i * GROUP + j for j in range(GROUP)]
        for at in ats:
            wait(at)
        terms = [product(at) for at in ats]
        for at, term in zip(ats, terms):
            acc[lax.div(todo[at], 2 * half)] += term
        return carry

    def single(at, carry):
        wait(at)
        acc[lax.div(todo[at], 2 * half)] += product(at)
        return carry

    groups = lax.div(count, GROUP)
    lax.fori_loop(0, groups, several, 0)
    lax.fori_loop(groups * GROUP, count, single, 0)
    if last:
        lay_out(acc, own, out)


def lay_out(acc, own, out):
    sec_dev, tile, _ = acc.shape
    op_count, _, lanes = out.shape
    share = tile // op_count
    cuts = tile // lanes
    dots = jnp.zeros((8, tile), jnp.float32)
    for t in range(sec_dev):
        total = acc[t]
        for cut in range(cuts):
            part = total[:, cut * lanes : (cut + 1) * lanes].reshape(op_count, share, lanes)
            row = (t * cuts + cut) * share
            out[:, row : row + share, :] = part.astype(out.dtype)
        mine = own[t].astype(jnp.float32) * total
        dots += jnp.sum(mine.reshape(tile // 8, 8, tile), axis=0)
    row = jnp.sum(dots, axis=0, keepdims=True)
    row = sum(row[:, cut * lanes : (cut + 1) * lanes] for cut in range(cuts))
    high = row.astype(jnp.bfloat16).astype(jnp.float32)
    mid = (row - high).astype(jnp.bfloat16).astype(jnp.float32)
    low = row - high - mid
    at = lax.broadcasted_iota(jnp.int32, (share, lanes), 0)
    slab = jnp.where(at == 0, high, jnp.where(at == 1, mid, jnp.where(at == 2, low, 0.0)))
    slab = slab.astype(out.dtype)
    out[:, sec_dev * cuts * share :, :] = jnp.broadcast_to(slab[None], (op_count, share, lanes))


def stage(slots, ops, arrays, low, sums=None, own=None, op_count=0):
    half, sec_dev, tile, _ = ops[0].shape
    pairs = sec_dev * 2 * half
    total = sum(a.shape[0] for a in arrays)
    last = own is not None
    out_shape = jax.ShapeDtypeStruct((sec_dev, tile, tile), jnp.float32)
    if last:
        rows = (sec_dev * (tile // LANES) + 1) * (tile // op_count)
        out_shape = jax.ShapeDtypeStruct((op_count, rows, LANES), jnp.bfloat16)
    whole = pl.BlockSpec(memory_space=pltpu.VMEM)
    held = ([own] if last else []) + ([sums] if sums is not None else [])
    return pl.pallas_call(
        functools.partial(stage_kernel, low, low + total, sums is not None, last),
        grid_spec=pltpu.PrefetchScalarGridSpec(
            num_scalar_prefetch=1,
            grid=(),
            in_specs=[whole] * len(held)
            + [pl.BlockSpec(memory_space=pl.ANY)] * (4 + len(arrays)),
            out_specs=whole,
            scratch_shapes=[
                pltpu.VMEM((total, tile, tile), jnp.bfloat16),
                pltpu.VMEM((pairs, tile, tile), jnp.bfloat16),
                pltpu.VMEM((pairs, tile, tile), jnp.bfloat16),
                pltpu.VMEM((sec_dev, tile, tile) if last else (1, 8, LANES), jnp.float32),
                pltpu.SMEM((pairs,), jnp.int32),
                pltpu.SemaphoreType.DMA((len(arrays),)),
                pltpu.SemaphoreType.DMA((pairs,)),
                pltpu.SemaphoreType.DMA((pairs,)),
            ],
        ),
        out_shape=out_shape,
        compiler_params=pltpu.CompilerParams(vmem_limit_bytes=40 * 2**20),
        cost_estimate=pl.CostEstimate(
            flops=2 * 2 * total * tile**3,
            bytes_accessed=2 * tile * tile * 3 * total,
            transcendentals=0,
        ),
    )(slots, *held, *ops, *arrays)


def swap(x, axis, mask):
    count = lax.axis_size(axis)
    return lax.ppermute(x, axis, [(i, i ^ mask) for i in range(count)])


def step(x, side, ring, way):
    perm = []
    for op in range(lax.axis_size("op")):
        for at in range(side * side):
            y, x_ = at // side, at % side
            if (op + ring) % 2 == 0:
                x_ = (x_ + way) % side
            else:
                y = (y + way) % side
            perm.append((op * side * side + at, op * side * side + y * side + x_))
    return lax.ppermute(x, ("op", "sec"), perm)


def partial_sums(own, slots, side, left_ops, right_ops, op_count):
    first = lambda b, way: step(b, side, 0, way)
    second = lambda b, way: step(b, side, 1, way)
    left_other = swap(left_ops, "op", 1)
    behind, ahead = first(own, 1), first(own, -1)
    own, behind, ahead, left_other, right = lax.optimization_barrier(
        (own, behind, ahead, left_other, right_ops)
    )
    right_other = swap(right, "op", 1)
    far = first(behind, 1)
    own_a, behind_a, ahead_a = second(own, -1), second(behind, -1), second(ahead, -1)
    own, behind, ahead, far, right_other = lax.optimization_barrier(
        (own, behind, ahead, far, right_other)
    )
    far_a, far_b = second(far, -1), second(far, 1)
    own_b, behind_b, ahead_b = second(own, 1), second(behind, 1), second(ahead, 1)
    ops = (left_ops, left_other, right_ops, right_other)
    first_arrays = [own, behind, ahead, far, behind_a, ahead_a]
    sums = stage(slots, ops, first_arrays, 0)
    sums, behind_a = lax.optimization_barrier((sums, behind_a))
    own_f, behind_f = second(own_b, 1), second(behind_a, -1)
    ahead_f, far_f = second(ahead_a, -1), second(far_a, -1)
    next_arrays = [own_b, behind_b, ahead_b, own_a, far_a]
    last_arrays = [far_b, own_f, behind_f, ahead_f, far_f]
    low = sum(a.shape[0] for a in first_arrays)
    sums = stage(slots, ops, next_arrays, low, sums)
    low += sum(a.shape[0] for a in next_arrays)
    return stage(slots, ops, last_arrays, low, sums, own, op_count)


def array_place(place):
    order = [0, 1, 2, 3, 9, 10, 4, 5, 6, 8, 11, 7, 12, 13, 14, 15]
    return sum(jnp.where(place == at, i, 0) for i, at in enumerate(order))


def ring_place(source, mine, side):
    away = (source - mine) % side
    return jnp.where(away == 0, 0, jnp.where(away == side - 1, 1, away + 1))


def body(wavefunction, left_ops, right_ops, sources, block_dims, energies):
    op_count = lax.axis_size("op")
    sec_count = lax.axis_size("sec")
    my_sec = lax.axis_index("sec")
    my_op = lax.axis_index("op")
    sec_dev, vectors, tile, _ = wavefunction.shape
    share = tile // op_count
    chips = op_count // vectors
    core = my_op % vectors
    side = 4

    own = lax.dynamic_index_in_dim(wavefunction, core, 1, keepdims=False)
    row = lax.broadcasted_iota(jnp.int32, own.shape, 1)
    column = lax.broadcasted_iota(jnp.int32, own.shape, 2)
    inside = jnp.maximum(row, column) < block_dims[:, None, None]
    own = jnp.where(inside, own, jnp.zeros_like(own))

    table = lax.dynamic_slice_in_dim(sources, my_sec * sec_dev, sec_dev, 1)
    table = jnp.concatenate([table, swap(table, "op", 1)], axis=0)
    table = jnp.transpose(table).reshape(-1)
    device, local = table // sec_dev, table % sec_dev
    in_y = ring_place(device // side, my_sec // side, side)
    in_x = ring_place(device % side, my_sec % side, side)
    place = jnp.where(core == 0, in_y * side + in_x, in_x * side + in_y)
    slots = array_place(place) * sec_dev + local

    live = jnp.arange(tile, dtype=jnp.int32)[None, :] < block_dims[:, None]
    window = live[:, :, None] & live[:, None, :]
    wide = jnp.where(window[:, None], wavefunction, 0).astype(jnp.float32)
    norms = jnp.sum(wide * wide, axis=(2, 3))

    partial = partial_sums(own, slots, side, left_ops, right_ops, op_count)
    parts = lax.all_to_all(partial, "op", split_axis=0, concat_axis=0, tiled=True)
    lanes = LANES
    parts = parts.reshape(chips, vectors, -1, share, lanes)
    numer = jnp.sum(parts[:, :, -1].astype(jnp.float32), axis=(0, 2, 3))
    numer = numer + jnp.sum(energies[:, None] * norms, axis=0)
    scalars = jnp.concatenate([numer, jnp.sum(norms, axis=0)])
    scalars = jnp.pad(scalars[None, None, :], ((0, 0), (0, 7), (0, 128 - 2 * vectors)))
    scalars = jnp.broadcast_to(scalars, (sec_count, 8, 128))
    scalars = lax.all_to_all(scalars, "sec", split_axis=0, concat_axis=0, tiled=True)
    scalars = jnp.sum(scalars[:, 0, : 2 * vectors], axis=0)
    rayleigh = scalars[:vectors] / scalars[vectors:]

    parts = parts[:, :, :-1].reshape(chips, vectors, sec_dev, tile // lanes, share, lanes)
    summed = jnp.sum(parts.astype(jnp.float32), axis=0)
    summed = jnp.concatenate([summed[:, :, cut] for cut in range(tile // lanes)], axis=3)
    summed = jnp.transpose(summed, (2, 1, 0, 3))
    rows = lax.dynamic_slice_in_dim(wavefunction, my_op * share, share, 2)
    live_rows = lax.dynamic_slice_in_dim(live, my_op * share, share, 1)
    row_window = jnp.transpose(live_rows)[:, :, None, None] & live[None, :, None, :]
    rows = jnp.where(row_window, jnp.transpose(rows, (2, 0, 1, 3)).astype(jnp.float32), 0.0)
    sigma = jnp.where(row_window, summed + energies[None, :, None, None] * rows, 0.0)
    residual = sigma - rayleigh[None, None, :, None] * rows
    return (residual, rayleigh)


def solution(mesh):
    in_specs = (
        P("sec", None, None, None),
        P("op", "sec", None, None),
        P("op", "sec", None, None),
        P("op", None),
        P("sec"),
        P("sec"),
    )
    out_specs = (P("op", "sec", None, None), P())
    return jax.shard_map(body, mesh=mesh, in_specs=in_specs, out_specs=out_specs, check_vma=False)
```

```python
import functools

import jax
import jax.numpy as jnp
from jax import lax
from jax.experimental import pallas as pl
from jax.experimental.pallas import tpu as pltpu
from jax.sharding import PartitionSpec as P

GROUP = 4
LANES = 128


def start_blocks(arrays, vec, sems):
    copies = []
    at = 0
    for i, array in enumerate(arrays):
        count = array.shape[0]
        copies.append(pltpu.make_async_copy(array, vec.at[pl.ds(at, count)], sems.at[i]))
        copies[-1].start()
        at += count
    vec[at] = jnp.zeros(vec.shape[1:], vec.dtype)
    return copies


def enlist(slots, blocks, places, t, size, low, high, found):
    base = t * (size + GROUP)
    count = jnp.int32(0)
    for k in range(size):
        slot = slots[t * size + k]
        mine = jnp.logical_and(slot >= low, slot < high)

        @pl.when(mine)
        def _():
            blocks[base + count] = slot - low
            places[base + count] = found(k, count)

        count = count + mine.astype(jnp.int32)
    for i in range(GROUP):
        blocks[base + count + i] = high - low
        places[base + count + i] = t * size
    return count


def add_groups(acc, vec, lefts, rights, blocks, places, t, size, count):
    base = t * (size + GROUP)

    def group(i, carry):
        inners, terms = [], []
        for j in range(GROUP):
            at = base + i * GROUP + j
            place = places[at]
            inner = jnp.dot(lefts[place], vec[blocks[at]], preferred_element_type=jnp.float32)
            inners.append(inner.astype(jnp.bfloat16))
            terms.append(rights[place])
        acc[t] += lax.dot_general(
            jnp.concatenate(inners, axis=1), jnp.concatenate(terms, axis=1),
            (((1,), (1,)), ((), ())), preferred_element_type=jnp.float32,
        )
        return carry

    lax.fori_loop(0, lax.div(count + GROUP - 1, GROUP), group, 0)


def early_kernel(slots, left_a, left_b, right_a, right_b, *rest):
    arrays, (sums, vec, lefts, rights, blocks, places, sems, op_sems) = rest[:-8], rest[-8:]
    half, sec_dev, tile, _ = left_a.shape
    size = 2 * half
    total = vec.shape[0] - 1
    block_copies = start_blocks(arrays, vec, sems)
    op_copies = []
    for t in range(sec_dev):
        mine = []
        for i, (ops, held, first) in enumerate(
            ((left_a, lefts, 0), (left_b, lefts, half), (right_a, rights, 0), (right_b, rights, half))
        ):
            mine.append(
                pltpu.make_async_copy(
                    ops.at[:, t], held.at[pl.ds(t * size + first, half)], op_sems.at[t, i]
                )
            )
            mine[-1].start()
        op_copies.append(mine)
    sums[...] = jnp.zeros(sums.shape, sums.dtype)
    counts = [
        enlist(slots, blocks, places, t, size, 0, total, lambda k, count, t=t: t * size + k)
        for t in range(sec_dev)
    ]
    for copy in block_copies:
        copy.wait()
    for t in range(sec_dev):
        for copy in op_copies[t]:
            copy.wait()
        add_groups(sums, vec, lefts, rights, blocks, places, t, size, counts[t])


def early_sums(slots, left_a, left_b, right_a, right_b, arrays):
    half, sec_dev, tile, _ = left_a.shape
    size = 2 * half
    total = sum(a.shape[0] for a in arrays)
    return pl.pallas_call(
        early_kernel,
        grid_spec=pltpu.PrefetchScalarGridSpec(
            num_scalar_prefetch=1,
            grid=(),
            in_specs=[pl.BlockSpec(memory_space=pl.ANY)] * (4 + len(arrays)),
            out_specs=pl.BlockSpec(memory_space=pltpu.VMEM),
            scratch_shapes=[
                pltpu.VMEM((total + 1, tile, tile), jnp.bfloat16),
                pltpu.VMEM((sec_dev * size, tile, tile), jnp.bfloat16),
                pltpu.VMEM((sec_dev * size, tile, tile), jnp.bfloat16),
                pltpu.SMEM((sec_dev * (size + GROUP),), jnp.int32),
                pltpu.SMEM((sec_dev * (size + GROUP),), jnp.int32),
                pltpu.SemaphoreType.DMA((len(arrays),)),
                pltpu.SemaphoreType.DMA((sec_dev, 4)),
            ],
        ),
        out_shape=jax.ShapeDtypeStruct((sec_dev, tile, tile), jnp.float32),
        compiler_params=pltpu.CompilerParams(vmem_limit_bytes=48 * 2**20),
        cost_estimate=pl.CostEstimate(
            flops=2 * 2 * sec_dev * size * tile**3,
            bytes_accessed=2 * tile * tile * (total + 2 * size * sec_dev),
            transcendentals=0,
        ),
    )(slots, left_a, left_b, right_a, right_b, *arrays)


def late_kernel(skip, slots, own, early, left_a, left_b, right_a, right_b, *rest):
    arrays, scratch = rest[:-10], rest[-10:]
    out, vec, lefts, rights, acc, blocks, places, sems, left_sems, right_sems = scratch
    half, sec_dev, tile, _ = left_a.shape
    size = 2 * half
    total = vec.shape[0] - 1
    block_copies = start_blocks(arrays, vec, sems)

    def fetch(t):
        def found(k, count):
            at = t * size + count
            left, right = (left_a, right_a) if k < half else (left_b, right_b)
            pltpu.make_async_copy(left.at[k % half, t], lefts.at[at], left_sems.at[at]).start()
            pltpu.make_async_copy(right.at[k % half, t], rights.at[at], right_sems.at[at]).start()
            return at

        return found

    counts = [
        enlist(slots, blocks, places, t, size, skip, skip + total, fetch(t))
        for t in range(sec_dev)
    ]
    acc[...] = early[...]
    for copy in block_copies:
        copy.wait()
    for t in range(sec_dev):

        def wait(i, carry, t=t):
            at = t * size + i
            pltpu.make_async_copy(left_a.at[0, 0], lefts.at[at], left_sems.at[at]).wait()
            pltpu.make_async_copy(right_a.at[0, 0], rights.at[at], right_sems.at[at]).wait()
            return carry

        lax.fori_loop(0, counts[t], wait, 0)
        add_groups(acc, vec, lefts, rights, blocks, places, t, size, counts[t])
    lay_out(acc, own, out)


def lay_out(acc, own, out):
    sec_dev, tile, _ = acc.shape
    op_count, _, lanes = out.shape
    share = tile // op_count
    cuts = tile // lanes
    dots = jnp.zeros((8, tile), jnp.float32)
    for t in range(sec_dev):
        total = acc[t]
        for cut in range(cuts):
            part = total[:, cut * lanes : (cut + 1) * lanes].reshape(op_count, share, lanes)
            row = (t * cuts + cut) * share
            out[:, row : row + share, :] = part.astype(out.dtype)
        mine = own[t].astype(jnp.float32) * total
        dots += jnp.sum(mine.reshape(tile // 8, 8, tile), axis=0)
    row = jnp.sum(dots, axis=0, keepdims=True)
    row = sum(row[:, cut * lanes : (cut + 1) * lanes] for cut in range(cuts))
    high = row.astype(jnp.bfloat16).astype(jnp.float32)
    mid = (row - high).astype(jnp.bfloat16).astype(jnp.float32)
    low = row - high - mid
    at = lax.broadcasted_iota(jnp.int32, (share, lanes), 0)
    slab = jnp.where(at == 0, high, jnp.where(at == 1, mid, jnp.where(at == 2, low, 0.0)))
    slab = slab.astype(out.dtype)
    out[:, sec_dev * cuts * share :, :] = jnp.broadcast_to(slab[None], (op_count, share, lanes))


def late_sums(slots, own, early, left_a, left_b, right_a, right_b, arrays, skip, op_count):
    half, sec_dev, tile, _ = left_a.shape
    size = 2 * half
    share = tile // op_count
    total = sum(a.shape[0] for a in arrays)
    out_shape = (op_count, (sec_dev * (tile // LANES) + 1) * share, LANES)
    whole = pl.BlockSpec(memory_space=pltpu.VMEM)
    return pl.pallas_call(
        functools.partial(late_kernel, skip),
        grid_spec=pltpu.PrefetchScalarGridSpec(
            num_scalar_prefetch=1,
            grid=(),
            in_specs=[whole, whole] + [pl.BlockSpec(memory_space=pl.ANY)] * (4 + len(arrays)),
            out_specs=whole,
            scratch_shapes=[
                pltpu.VMEM((total + 1, tile, tile), jnp.bfloat16),
                pltpu.VMEM((sec_dev * size, tile, tile), jnp.bfloat16),
                pltpu.VMEM((sec_dev * size, tile, tile), jnp.bfloat16),
                pltpu.VMEM((sec_dev, tile, tile), jnp.float32),
                pltpu.SMEM((sec_dev * (size + GROUP),), jnp.int32),
                pltpu.SMEM((sec_dev * (size + GROUP),), jnp.int32),
                pltpu.SemaphoreType.DMA((len(arrays),)),
                pltpu.SemaphoreType.DMA((sec_dev * size,)),
                pltpu.SemaphoreType.DMA((sec_dev * size,)),
            ],
        ),
        out_shape=jax.ShapeDtypeStruct(out_shape, jnp.bfloat16),
        compiler_params=pltpu.CompilerParams(vmem_limit_bytes=48 * 2**20),
        cost_estimate=pl.CostEstimate(
            flops=2 * sec_dev * half * tile**3,
            bytes_accessed=2 * tile * tile * (total + 2 * half * sec_dev),
            transcendentals=0,
        ),
    )(slots, own, early, left_a, left_b, right_a, right_b, *arrays)


def swap(x, axis, mask):
    count = lax.axis_size(axis)
    return lax.ppermute(x, axis, [(i, i ^ mask) for i in range(count)])


def step(x, side, ring, way):
    perm = []
    for op in range(lax.axis_size("op")):
        for at in range(side * side):
            y, x_ = at // side, at % side
            if (op + ring) % 2 == 0:
                x_ = (x_ + way) % side
            else:
                y = (y + way) % side
            perm.append((op * side * side + at, op * side * side + y * side + x_))
    return lax.ppermute(x, ("op", "sec"), perm)


def gather_blocks(own, side, left_ops, right_ops):
    first = lambda b, way: step(b, side, 0, way)
    second = lambda b, way: step(b, side, 1, way)
    left_other = swap(left_ops, "op", 1)
    behind, ahead = first(own, 1), first(own, -1)
    own, behind, ahead, left_other, right = lax.optimization_barrier(
        (own, behind, ahead, left_other, right_ops)
    )
    right_other = swap(right, "op", 1)
    far = first(behind, 1)
    own_a, behind_a, ahead_a = second(own, -1), second(behind, -1), second(ahead, -1)
    own, behind, ahead, far, right_other = lax.optimization_barrier(
        (own, behind, ahead, far, right_other)
    )
    far_a, far_b = second(far, -1), second(far, 1)
    own_b, behind_b, ahead_b = second(own, 1), second(behind, 1), second(ahead, 1)
    own_f, behind_f = second(own_b, 1), second(behind_a, -1)
    ahead_f, far_f = second(ahead_a, -1), second(far_a, -1)
    early = [
        own, behind, ahead, far, own_b, behind_b, ahead_b, own_a, behind_a, ahead_a, far_a,
    ]
    late = [far_b, own_f, behind_f, ahead_f, far_f]
    return early, late, left_other, right_other


def array_place(place):
    return jnp.where(place == 7, 11, jnp.where((place > 7) & (place < 12), place - 1, place))


def ring_place(source, mine, side):
    away = (source - mine) % side
    return jnp.where(away == 0, 0, jnp.where(away == side - 1, 1, away + 1))


def body(wavefunction, left_ops, right_ops, sources, block_dims, energies):
    op_count = lax.axis_size("op")
    sec_count = lax.axis_size("sec")
    my_sec = lax.axis_index("sec")
    my_op = lax.axis_index("op")
    sec_dev, vectors, tile, _ = wavefunction.shape
    share = tile // op_count
    chips = op_count // vectors
    core = my_op % vectors
    side = 4

    own = lax.dynamic_index_in_dim(wavefunction, core, 1, keepdims=False)
    row = lax.broadcasted_iota(jnp.int32, own.shape, 1)
    column = lax.broadcasted_iota(jnp.int32, own.shape, 2)
    inside = jnp.maximum(row, column) < block_dims[:, None, None]
    own = jnp.where(inside, own, jnp.zeros_like(own))

    early, late, left_other, right_other = gather_blocks(own, side, left_ops, right_ops)
    skip = sum(a.shape[0] for a in early)

    table = lax.dynamic_slice_in_dim(sources, my_sec * sec_dev, sec_dev, 1)
    table = jnp.concatenate([table, swap(table, "op", 1)], axis=0)
    table = jnp.transpose(table).reshape(-1)
    device, local = table // sec_dev, table % sec_dev
    in_y = ring_place(device // side, my_sec // side, side)
    in_x = ring_place(device % side, my_sec % side, side)
    place = jnp.where(core == 0, in_y * side + in_x, in_x * side + in_y)
    slots = array_place(place) * sec_dev + local

    live = jnp.arange(tile, dtype=jnp.int32)[None, :] < block_dims[:, None]
    window = live[:, :, None] & live[:, None, :]
    wide = jnp.where(window[:, None], wavefunction, 0).astype(jnp.float32)
    norms = jnp.sum(wide * wide, axis=(2, 3))

    ops = (left_ops, left_other, right_ops, right_other)
    sums = early_sums(slots, *ops, early)
    partial = late_sums(slots, own, sums, *ops, late, skip, op_count)
    parts = lax.all_to_all(partial, "op", split_axis=0, concat_axis=0, tiled=True)
    lanes = LANES
    parts = parts.reshape(chips, vectors, -1, share, lanes)
    numer = jnp.sum(parts[:, :, -1].astype(jnp.float32), axis=(0, 2, 3))
    numer = numer + jnp.sum(energies[:, None] * norms, axis=0)
    scalars = jnp.concatenate([numer, jnp.sum(norms, axis=0)])
    scalars = jnp.pad(scalars[None, None, :], ((0, 0), (0, 7), (0, 128 - 2 * vectors)))
    scalars = jnp.broadcast_to(scalars, (sec_count, 8, 128))
    scalars = lax.all_to_all(scalars, "sec", split_axis=0, concat_axis=0, tiled=True)
    scalars = jnp.sum(scalars[:, 0, : 2 * vectors], axis=0)
    rayleigh = scalars[:vectors] / scalars[vectors:]

    parts = parts[:, :, :-1].reshape(chips, vectors, sec_dev, tile // lanes, share, lanes)
    summed = jnp.sum(parts.astype(jnp.float32), axis=0)
    summed = jnp.concatenate([summed[:, :, cut] for cut in range(tile // lanes)], axis=3)
    summed = jnp.transpose(summed, (2, 1, 0, 3))
    rows = lax.dynamic_slice_in_dim(wavefunction, my_op * share, share, 2)
    live_rows = lax.dynamic_slice_in_dim(live, my_op * share, share, 1)
    row_window = jnp.transpose(live_rows)[:, :, None, None] & live[None, :, None, :]
    rows = jnp.where(row_window, jnp.transpose(rows, (2, 0, 1, 3)).astype(jnp.float32), 0.0)
    sigma = jnp.where(row_window, summed + energies[None, :, None, None] * rows, 0.0)
    residual = sigma - rayleigh[None, None, :, None] * rows
    return (residual, rayleigh)


def solution(mesh):
    in_specs = (
        P("sec", None, None, None),
        P("op", "sec", None, None),
        P("op", "sec", None, None),
        P("op", None),
        P("sec"),
        P("sec"),
    )
    out_specs = (P("op", "sec", None, None), P())
    return jax.shard_map(body, mesh=mesh, in_specs=in_specs, out_specs=out_specs, check_vma=False)
```

```python
import functools

import jax
import jax.numpy as jnp
from jax import lax
from jax.experimental import pallas as pl
from jax.experimental.pallas import tpu as pltpu
from jax.sharding import PartitionSpec as P

GROUP = 4
LATE_GROUP = 8
LANES = 128


def start_blocks(arrays, vec, sems):
    copies = []
    at = 0
    for i, array in enumerate(arrays):
        count = array.shape[0]
        copies.append(pltpu.make_async_copy(array, vec.at[pl.ds(at, count)], sems.at[i]))
        copies[-1].start()
        at += count
    vec[at] = jnp.zeros(vec.shape[1:], vec.dtype)
    return copies


def early_kernel(slots, left_a, left_b, right_a, right_b, *rest):
    arrays, (sums, vec, lefts, rights, sems, op_sems) = rest[:-6], rest[-6:]
    half, sec_dev, tile, _ = left_a.shape
    size = 2 * half
    total = vec.shape[0] - 1
    block_copies = start_blocks(arrays, vec, sems)

    def op_copies(t):
        held = (
            (left_a, lefts, 0), (left_b, lefts, half), (right_a, rights, 0), (right_b, rights, half)
        )
        return [
            pltpu.make_async_copy(
                ops.at[:, t], to.at[pl.ds(t * size + first, half)], op_sems.at[t, i]
            )
            for i, (ops, to, first) in enumerate(held)
        ]

    for t in range(sec_dev):
        for copy in op_copies(t):
            copy.start()
    for copy in block_copies:
        copy.wait()

    def target(t, carry):
        for copy in op_copies(t):
            copy.wait()
        for first in range(0, size, GROUP):
            inners, terms = [], []
            for k in range(first, first + GROUP):
                block = vec[jnp.minimum(slots[t * size + k], total)]
                inner = jnp.dot(
                    lefts[t * size + k], block, preferred_element_type=jnp.float32
                )
                inners.append(inner.astype(jnp.bfloat16))
                terms.append(rights[t * size + k])
            term = lax.dot_general(
                jnp.concatenate(inners, axis=1), jnp.concatenate(terms, axis=1),
                (((1,), (1,)), ((), ())), preferred_element_type=jnp.float32,
            )
            if first == 0:
                sums[t] = term
            else:
                sums[t] += term
        return carry

    lax.fori_loop(0, sec_dev, target, 0)


def early_sums(slots, left_a, left_b, right_a, right_b, arrays):
    half, sec_dev, tile, _ = left_a.shape
    size = 2 * half
    total = sum(a.shape[0] for a in arrays)
    return pl.pallas_call(
        early_kernel,
        grid_spec=pltpu.PrefetchScalarGridSpec(
            num_scalar_prefetch=1,
            grid=(),
            in_specs=[pl.BlockSpec(memory_space=pl.ANY)] * (4 + len(arrays)),
            out_specs=pl.BlockSpec(memory_space=pltpu.VMEM),
            scratch_shapes=[
                pltpu.VMEM((total + 1, tile, tile), jnp.bfloat16),
                pltpu.VMEM((sec_dev * size, tile, tile), jnp.bfloat16),
                pltpu.VMEM((sec_dev * size, tile, tile), jnp.bfloat16),
                pltpu.SemaphoreType.DMA((len(arrays),)),
                pltpu.SemaphoreType.DMA((sec_dev, 4)),
            ],
        ),
        out_shape=jax.ShapeDtypeStruct((sec_dev, tile, tile), jnp.float32),
        compiler_params=pltpu.CompilerParams(vmem_limit_bytes=48 * 2**20),
        cost_estimate=pl.CostEstimate(
            flops=2 * 2 * sec_dev * size * tile**3,
            bytes_accessed=2 * tile * tile * (total + 2 * size * sec_dev),
            transcendentals=0,
        ),
    )(slots, left_a, left_b, right_a, right_b, *arrays)


def late_kernel(skip, slots, own, early, left_a, left_b, right_a, right_b, *rest):
    arrays, scratch = rest[:-10], rest[-10:]
    out, vec, lefts, rights, acc, blocks, targets, sems, left_sems, right_sems = scratch
    half, sec_dev, tile, _ = left_a.shape
    size = 2 * half
    total = vec.shape[0] - 1
    block_copies = start_blocks(arrays, vec, sems)

    def enlist(pair, count):
        slot = slots[pair]
        mine = slot >= skip

        @pl.when(mine)
        def _():
            t, k = lax.div(pair, size), lax.rem(pair, size)
            blocks[count] = slot - skip
            targets[count] = t

            @pl.when(k < half)
            def _():
                pltpu.make_async_copy(left_a.at[k, t], lefts.at[count], left_sems.at[count]).start()
                pltpu.make_async_copy(right_a.at[k, t], rights.at[count], right_sems.at[count]).start()

            @pl.when(k >= half)
            def _():
                pltpu.make_async_copy(
                    left_b.at[k - half, t], lefts.at[count], left_sems.at[count]
                ).start()
                pltpu.make_async_copy(
                    right_b.at[k - half, t], rights.at[count], right_sems.at[count]
                ).start()

        return count + mine.astype(jnp.int32)

    count = lax.fori_loop(0, sec_dev * size, enlist, jnp.int32(0))
    for i in range(LATE_GROUP):
        blocks[count + i] = total
        targets[count + i] = 0
    acc[...] = early[...]
    for copy in block_copies:
        copy.wait()

    def group(i, carry):
        ats = [i * LATE_GROUP + j for j in range(LATE_GROUP)]
        for at in ats:

            @pl.when(at < count)
            def _():
                pltpu.make_async_copy(left_a.at[0, 0], lefts.at[at], left_sems.at[at]).wait()
                pltpu.make_async_copy(right_a.at[0, 0], rights.at[at], right_sems.at[at]).wait()

        terms = []
        for at in ats:
            place = jnp.where(at < count, at, 0)
            inner = jnp.dot(lefts[place], vec[blocks[at]], preferred_element_type=jnp.float32)
            terms.append(
                lax.dot_general(
                    inner.astype(jnp.bfloat16), rights[place], (((1,), (1,)), ((), ())),
                    preferred_element_type=jnp.float32,
                )
            )
        for at, term in zip(ats, terms):
            acc[targets[at]] += term
        return carry

    lax.fori_loop(0, lax.div(count + LATE_GROUP - 1, LATE_GROUP), group, 0)
    lay_out(acc, own, out)


def lay_out(acc, own, out):
    sec_dev, tile, _ = acc.shape
    op_count, _, lanes = out.shape
    share = tile // op_count
    cuts = tile // lanes
    dots = jnp.zeros((8, tile), jnp.float32)
    for t in range(sec_dev):
        total = acc[t]
        for cut in range(cuts):
            part = total[:, cut * lanes : (cut + 1) * lanes].reshape(op_count, share, lanes)
            row = (t * cuts + cut) * share
            out[:, row : row + share, :] = part.astype(out.dtype)
        mine = own[t].astype(jnp.float32) * total
        dots += jnp.sum(mine.reshape(tile // 8, 8, tile), axis=0)
    row = jnp.sum(dots, axis=0, keepdims=True)
    row = sum(row[:, cut * lanes : (cut + 1) * lanes] for cut in range(cuts))
    high = row.astype(jnp.bfloat16).astype(jnp.float32)
    mid = (row - high).astype(jnp.bfloat16).astype(jnp.float32)
    low = row - high - mid
    at = lax.broadcasted_iota(jnp.int32, (share, lanes), 0)
    slab = jnp.where(at == 0, high, jnp.where(at == 1, mid, jnp.where(at == 2, low, 0.0)))
    slab = slab.astype(out.dtype)
    out[:, sec_dev * cuts * share :, :] = jnp.broadcast_to(slab[None], (op_count, share, lanes))


def late_sums(slots, own, early, left_a, left_b, right_a, right_b, arrays, skip, op_count):
    half, sec_dev, tile, _ = left_a.shape
    size = 2 * half
    share = tile // op_count
    total = sum(a.shape[0] for a in arrays)
    out_shape = (op_count, (sec_dev * (tile // LANES) + 1) * share, LANES)
    whole = pl.BlockSpec(memory_space=pltpu.VMEM)
    return pl.pallas_call(
        functools.partial(late_kernel, skip),
        grid_spec=pltpu.PrefetchScalarGridSpec(
            num_scalar_prefetch=1,
            grid=(),
            in_specs=[whole, whole] + [pl.BlockSpec(memory_space=pl.ANY)] * (4 + len(arrays)),
            out_specs=whole,
            scratch_shapes=[
                pltpu.VMEM((total + 1, tile, tile), jnp.bfloat16),
                pltpu.VMEM((sec_dev * size, tile, tile), jnp.bfloat16),
                pltpu.VMEM((sec_dev * size, tile, tile), jnp.bfloat16),
                pltpu.VMEM((sec_dev, tile, tile), jnp.float32),
                pltpu.SMEM((sec_dev * size + LATE_GROUP,), jnp.int32),
                pltpu.SMEM((sec_dev * size + LATE_GROUP,), jnp.int32),
                pltpu.SemaphoreType.DMA((len(arrays),)),
                pltpu.SemaphoreType.DMA((sec_dev * size,)),
                pltpu.SemaphoreType.DMA((sec_dev * size,)),
            ],
        ),
        out_shape=jax.ShapeDtypeStruct(out_shape, jnp.bfloat16),
        compiler_params=pltpu.CompilerParams(vmem_limit_bytes=48 * 2**20),
        cost_estimate=pl.CostEstimate(
            flops=2 * sec_dev * half * tile**3,
            bytes_accessed=2 * tile * tile * (total + 2 * half * sec_dev),
            transcendentals=0,
        ),
    )(slots, own, early, left_a, left_b, right_a, right_b, *arrays)


def swap(x, axis, mask):
    count = lax.axis_size(axis)
    return lax.ppermute(x, axis, [(i, i ^ mask) for i in range(count)])


def step(x, side, ring, way):
    perm = []
    for op in range(lax.axis_size("op")):
        for at in range(side * side):
            y, x_ = at // side, at % side
            if (op + ring) % 2 == 0:
                x_ = (x_ + way) % side
            else:
                y = (y + way) % side
            perm.append((op * side * side + at, op * side * side + y * side + x_))
    return lax.ppermute(x, ("op", "sec"), perm)


def gather_blocks(own, side, left_ops, right_ops):
    first = lambda b, way: step(b, side, 0, way)
    second = lambda b, way: step(b, side, 1, way)
    left_other = swap(left_ops, "op", 1)
    behind, ahead = first(own, 1), first(own, -1)
    own, behind, ahead, left_other, right = lax.optimization_barrier(
        (own, behind, ahead, left_other, right_ops)
    )
    right_other = swap(right, "op", 1)
    far = first(behind, 1)
    own_a, behind_a, ahead_a = second(own, -1), second(behind, -1), second(ahead, -1)
    own, behind, ahead, far, right_other = lax.optimization_barrier(
        (own, behind, ahead, far, right_other)
    )
    far_a, far_b = second(far, -1), second(far, 1)
    own_b, behind_b, ahead_b = second(own, 1), second(behind, 1), second(ahead, 1)
    own_f, behind_f = second(own_b, 1), second(behind_a, -1)
    ahead_f, far_f = second(ahead_a, -1), second(far_a, -1)
    early = [
        own, behind, ahead, far, own_b, behind_b, ahead_b, own_a, behind_a, ahead_a, far_a,
    ]
    late = [far_b, own_f, behind_f, ahead_f, far_f]
    return early, late, left_other, right_other


def array_place(place):
    return jnp.where(place == 7, 11, jnp.where((place > 7) & (place < 12), place - 1, place))


def ring_place(source, mine, side):
    away = (source - mine) % side
    return jnp.where(away == 0, 0, jnp.where(away == side - 1, 1, away + 1))


def body(wavefunction, left_ops, right_ops, sources, block_dims, energies):
    op_count = lax.axis_size("op")
    sec_count = lax.axis_size("sec")
    my_sec = lax.axis_index("sec")
    my_op = lax.axis_index("op")
    sec_dev, vectors, tile, _ = wavefunction.shape
    share = tile // op_count
    chips = op_count // vectors
    core = my_op % vectors
    side = 4

    own = lax.dynamic_index_in_dim(wavefunction, core, 1, keepdims=False)
    row = lax.broadcasted_iota(jnp.int32, own.shape, 1)
    column = lax.broadcasted_iota(jnp.int32, own.shape, 2)
    inside = jnp.maximum(row, column) < block_dims[:, None, None]
    own = jnp.where(inside, own, jnp.zeros_like(own))

    early, late, left_other, right_other = gather_blocks(own, side, left_ops, right_ops)
    skip = sum(a.shape[0] for a in early)

    table = lax.dynamic_slice_in_dim(sources, my_sec * sec_dev, sec_dev, 1)
    table = jnp.concatenate([table, swap(table, "op", 1)], axis=0)
    table = jnp.transpose(table).reshape(-1)
    device, local = table // sec_dev, table % sec_dev
    in_y = ring_place(device // side, my_sec // side, side)
    in_x = ring_place(device % side, my_sec % side, side)
    place = jnp.where(core == 0, in_y * side + in_x, in_x * side + in_y)
    slots = array_place(place) * sec_dev + local

    live = jnp.arange(tile, dtype=jnp.int32)[None, :] < block_dims[:, None]
    window = live[:, :, None] & live[:, None, :]
    wide = jnp.where(window[:, None], wavefunction, 0).astype(jnp.float32)
    norms = jnp.sum(wide * wide, axis=(2, 3))

    ops = (left_ops, left_other, right_ops, right_other)
    sums = early_sums(slots, *ops, early)
    partial = late_sums(slots, own, sums, *ops, late, skip, op_count)
    parts = lax.all_to_all(partial, "op", split_axis=0, concat_axis=0, tiled=True)
    lanes = LANES
    parts = parts.reshape(chips, vectors, -1, share, lanes)
    numer = jnp.sum(parts[:, :, -1].astype(jnp.float32), axis=(0, 2, 3))
    numer = numer + jnp.sum(energies[:, None] * norms, axis=0)
    scalars = jnp.concatenate([numer, jnp.sum(norms, axis=0)])
    scalars = jnp.pad(scalars[None, None, :], ((0, 0), (0, 7), (0, 128 - 2 * vectors)))
    scalars = jnp.broadcast_to(scalars, (sec_count, 8, 128))
    scalars = lax.all_to_all(scalars, "sec", split_axis=0, concat_axis=0, tiled=True)
    scalars = jnp.sum(scalars[:, 0, : 2 * vectors], axis=0)
    rayleigh = scalars[:vectors] / scalars[vectors:]

    parts = parts[:, :, :-1].reshape(chips, vectors, sec_dev, tile // lanes, share, lanes)
    summed = jnp.sum(parts.astype(jnp.float32), axis=0)
    summed = jnp.concatenate([summed[:, :, cut] for cut in range(tile // lanes)], axis=3)
    summed = jnp.transpose(summed, (2, 1, 0, 3))
    rows = lax.dynamic_slice_in_dim(wavefunction, my_op * share, share, 2)
    live_rows = lax.dynamic_slice_in_dim(live, my_op * share, share, 1)
    row_window = jnp.transpose(live_rows)[:, :, None, None] & live[None, :, None, :]
    rows = jnp.where(row_window, jnp.transpose(rows, (2, 0, 1, 3)).astype(jnp.float32), 0.0)
    sigma = jnp.where(row_window, summed + energies[None, :, None, None] * rows, 0.0)
    residual = sigma - rayleigh[None, None, :, None] * rows
    return (residual, rayleigh)


def solution(mesh):
    in_specs = (
        P("sec", None, None, None),
        P("op", "sec", None, None),
        P("op", "sec", None, None),
        P("op", None),
        P("sec"),
        P("sec"),
    )
    out_specs = (P("op", "sec", None, None), P())
    return jax.shard_map(body, mesh=mesh, in_specs=in_specs, out_specs=out_specs, check_vma=False)
```

```python
import functools

import jax
import jax.numpy as jnp
from jax import lax
from jax.experimental import pallas as pl
from jax.experimental.pallas import tpu as pltpu
from jax.sharding import PartitionSpec as P

GROUP = 4
LANES = 128


def start_blocks(arrays, vec, sems):
    copies = []
    at = 0
    for i, array in enumerate(arrays):
        count = array.shape[0]
        copies.append(pltpu.make_async_copy(array, vec.at[pl.ds(at, count)], sems.at[i]))
        copies[-1].start()
        at += count
    vec[at] = jnp.zeros(vec.shape[1:], vec.dtype)
    return copies


def early_kernel(slots, left_a, left_b, right_a, right_b, *rest):
    arrays, (sums, vec, sems) = rest[:-3], rest[-3:]
    half, sec_dev, tile, _ = left_a.shape
    size = 2 * half
    total = vec.shape[0] - 1
    for copy in start_blocks(arrays, vec, sems):
        copy.wait()

    def target(t, carry):
        for first in range(0, size, GROUP):
            inners, terms = [], []
            for k in range(first, first + GROUP):
                left, right = (left_a, right_a) if k < half else (left_b, right_b)
                block = vec[jnp.minimum(slots[t * size + k], total)]
                inner = jnp.dot(left[k % half, t], block, preferred_element_type=jnp.float32)
                inners.append(inner.astype(jnp.bfloat16))
                terms.append(right[k % half, t])
            term = lax.dot_general(
                jnp.concatenate(inners, axis=1), jnp.concatenate(terms, axis=1),
                (((1,), (1,)), ((), ())), preferred_element_type=jnp.float32,
            )
            if first == 0:
                sums[t] = term
            else:
                sums[t] += term
        return carry

    lax.fori_loop(0, sec_dev, target, 0)


def early_sums(slots, left_a, left_b, right_a, right_b, arrays):
    half, sec_dev, tile, _ = left_a.shape
    total = sum(a.shape[0] for a in arrays)
    whole = pl.BlockSpec(memory_space=pltpu.VMEM)
    return pl.pallas_call(
        early_kernel,
        grid_spec=pltpu.PrefetchScalarGridSpec(
            num_scalar_prefetch=1,
            grid=(),
            in_specs=[whole] * 4 + [pl.BlockSpec(memory_space=pl.ANY)] * len(arrays),
            out_specs=whole,
            scratch_shapes=[
                pltpu.VMEM((total + 1, tile, tile), jnp.bfloat16),
                pltpu.SemaphoreType.DMA((len(arrays),)),
            ],
        ),
        out_shape=jax.ShapeDtypeStruct((sec_dev, tile, tile), jnp.float32),
        compiler_params=pltpu.CompilerParams(vmem_limit_bytes=16 * 2**20),
        cost_estimate=pl.CostEstimate(
            flops=2 * 2 * sec_dev * 2 * half * tile**3,
            bytes_accessed=2 * tile * tile * (total + 4 * half * sec_dev),
            transcendentals=0,
        ),
    )(slots, left_a, left_b, right_a, right_b, *arrays)


def late_kernel(skip, slots, own, early, left_a, left_b, right_a, right_b, *rest):
    arrays, (out, vec, acc, pairs, sems) = rest[:-5], rest[-5:]
    half, sec_dev, tile, _ = left_a.shape
    size = 2 * half
    total = vec.shape[0] - 1
    limit = half * sec_dev + GROUP
    block_copies = start_blocks(arrays, vec, sems)

    def enlist(at, counts):
        t, k = lax.div(at, half), lax.rem(at, half)
        found = []
        for side, count in enumerate(counts):
            slot = slots[t * size + side * half + k]
            mine = slot >= skip

            @pl.when(mine)
            def _():
                pairs[side * 3 * limit + count] = slot - skip
                pairs[side * 3 * limit + limit + count] = t
                pairs[side * 3 * limit + 2 * limit + count] = k

            found.append(count + mine.astype(jnp.int32))
        return tuple(found)

    counts = lax.fori_loop(0, half * sec_dev, enlist, (jnp.int32(0), jnp.int32(0)))
    most = lax.div(jnp.maximum(*counts) + GROUP - 1, GROUP)
    for side, count in enumerate(counts):

        def fill(at, carry, side=side):
            pairs[side * 3 * limit + at] = total
            pairs[side * 3 * limit + limit + at] = 0
            pairs[side * 3 * limit + 2 * limit + at] = 0
            return carry

        lax.fori_loop(count, most * GROUP, fill, 0)
    acc[...] = early[...]
    for copy in block_copies:
        copy.wait()

    def group(i, carry):
        terms = []
        for side, (left, right) in enumerate(((left_a, right_a), (left_b, right_b))):
            for j in range(GROUP):
                at = side * 3 * limit + i * GROUP + j
                t, k = pairs[at + limit], pairs[at + 2 * limit]
                inner = jnp.dot(left[k, t], vec[pairs[at]], preferred_element_type=jnp.float32)
                term = lax.dot_general(
                    inner.astype(jnp.bfloat16), right[k, t], (((1,), (1,)), ((), ())),
                    preferred_element_type=jnp.float32,
                )
                terms.append((t, term))
        for t, term in terms:
            acc[t] += term
        return carry

    lax.fori_loop(0, most, group, 0)
    lay_out(acc, own, out)


def lay_out(acc, own, out):
    sec_dev, tile, _ = acc.shape
    op_count, _, lanes = out.shape
    share = tile // op_count
    cuts = tile // lanes
    dots = jnp.zeros((8, tile), jnp.float32)
    for t in range(sec_dev):
        total = acc[t]
        for cut in range(cuts):
            part = total[:, cut * lanes : (cut + 1) * lanes].reshape(op_count, share, lanes)
            row = (t * cuts + cut) * share
            out[:, row : row + share, :] = part.astype(out.dtype)
        mine = own[t].astype(jnp.float32) * total
        dots += jnp.sum(mine.reshape(tile // 8, 8, tile), axis=0)
    row = jnp.sum(dots, axis=0, keepdims=True)
    row = sum(row[:, cut * lanes : (cut + 1) * lanes] for cut in range(cuts))
    high = row.astype(jnp.bfloat16).astype(jnp.float32)
    mid = (row - high).astype(jnp.bfloat16).astype(jnp.float32)
    low = row - high - mid
    at = lax.broadcasted_iota(jnp.int32, (share, lanes), 0)
    slab = jnp.where(at == 0, high, jnp.where(at == 1, mid, jnp.where(at == 2, low, 0.0)))
    slab = slab.astype(out.dtype)
    out[:, sec_dev * cuts * share :, :] = jnp.broadcast_to(slab[None], (op_count, share, lanes))


def late_sums(slots, own, early, left_a, left_b, right_a, right_b, arrays, skip, op_count):
    half, sec_dev, tile, _ = left_a.shape
    share = tile // op_count
    total = sum(a.shape[0] for a in arrays)
    out_shape = (op_count, (sec_dev * (tile // LANES) + 1) * share, LANES)
    whole = pl.BlockSpec(memory_space=pltpu.VMEM)
    return pl.pallas_call(
        functools.partial(late_kernel, skip),
        grid_spec=pltpu.PrefetchScalarGridSpec(
            num_scalar_prefetch=1,
            grid=(),
            in_specs=[whole] * 6 + [pl.BlockSpec(memory_space=pl.ANY)] * len(arrays),
            out_specs=whole,
            scratch_shapes=[
                pltpu.VMEM((total + 1, tile, tile), jnp.bfloat16),
                pltpu.VMEM((sec_dev, tile, tile), jnp.float32),
                pltpu.SMEM((6 * (half * sec_dev + GROUP),), jnp.int32),
                pltpu.SemaphoreType.DMA((len(arrays),)),
            ],
        ),
        out_shape=jax.ShapeDtypeStruct(out_shape, jnp.bfloat16),
        compiler_params=pltpu.CompilerParams(vmem_limit_bytes=16 * 2**20),
        cost_estimate=pl.CostEstimate(
            flops=2 * sec_dev * half * tile**3,
            bytes_accessed=2 * tile * tile * (total + 2 * half * sec_dev),
            transcendentals=0,
        ),
    )(slots, own, early, left_a, left_b, right_a, right_b, *arrays)


def fetch_kernel(left, right, left_held, right_held, sems):
    copies = [
        pltpu.make_async_copy(left, left_held, sems.at[0]),
        pltpu.make_async_copy(right, right_held, sems.at[1]),
    ]
    for copy in copies:
        copy.start()
    for copy in copies:
        copy.wait()


def fetch(left, right):
    whole = pl.BlockSpec(memory_space=pltpu.VMEM)
    return pl.pallas_call(
        fetch_kernel,
        in_specs=[pl.BlockSpec(memory_space=pl.ANY)] * 2,
        out_specs=[whole] * 2,
        out_shape=[jax.ShapeDtypeStruct(x.shape, x.dtype) for x in (left, right)],
        scratch_shapes=[pltpu.SemaphoreType.DMA((2,))],
        compiler_params=pltpu.CompilerParams(vmem_limit_bytes=16 * 2**20),
    )(left, right)


def swap(x, axis, mask):
    count = lax.axis_size(axis)
    return lax.ppermute(x, axis, [(i, i ^ mask) for i in range(count)])


def step(x, side, ring, way):
    perm = []
    for op in range(lax.axis_size("op")):
        for at in range(side * side):
            y, x_ = at // side, at % side
            if (op + ring) % 2 == 0:
                x_ = (x_ + way) % side
            else:
                y = (y + way) % side
            perm.append((op * side * side + at, op * side * side + y * side + x_))
    return lax.ppermute(x, ("op", "sec"), perm)


def gather_blocks(own, side, left_ops, right_ops):
    first = lambda b, way: step(b, side, 0, way)
    second = lambda b, way: step(b, side, 1, way)
    left_other = swap(left_ops, "op", 1)
    behind, ahead = first(own, 1), first(own, -1)
    own, behind, ahead, left_other, right = lax.optimization_barrier(
        (own, behind, ahead, left_other, right_ops)
    )
    right_other = swap(right, "op", 1)
    far = first(behind, 1)
    own_a, behind_a, ahead_a = second(own, -1), second(behind, -1), second(ahead, -1)
    own, behind, ahead, far, right_other, left_own, right_own = lax.optimization_barrier(
        (own, behind, ahead, far, right_other, *fetch(left_ops, right))
    )
    far_a, far_b = second(far, -1), second(far, 1)
    own_b, behind_b, ahead_b = second(own, 1), second(behind, 1), second(ahead, 1)
    own_f, behind_f = second(own_b, 1), second(behind_a, -1)
    ahead_f, far_f = second(ahead_a, -1), second(far_a, -1)
    early = [
        own, behind, ahead, far, own_b, behind_b, ahead_b, own_a, behind_a, ahead_a, far_a,
    ]
    late = [far_b, own_f, behind_f, ahead_f, far_f]
    return early, late, (left_own, left_other, right_own, right_other)


def array_place(place):
    return jnp.where(place == 7, 11, jnp.where((place > 7) & (place < 12), place - 1, place))


def ring_place(source, mine, side):
    away = (source - mine) % side
    return jnp.where(away == 0, 0, jnp.where(away == side - 1, 1, away + 1))


def body(wavefunction, left_ops, right_ops, sources, block_dims, energies):
    op_count = lax.axis_size("op")
    sec_count = lax.axis_size("sec")
    my_sec = lax.axis_index("sec")
    my_op = lax.axis_index("op")
    sec_dev, vectors, tile, _ = wavefunction.shape
    share = tile // op_count
    chips = op_count // vectors
    core = my_op % vectors
    side = 4

    own = lax.dynamic_index_in_dim(wavefunction, core, 1, keepdims=False)
    row = lax.broadcasted_iota(jnp.int32, own.shape, 1)
    column = lax.broadcasted_iota(jnp.int32, own.shape, 2)
    inside = jnp.maximum(row, column) < block_dims[:, None, None]
    own = jnp.where(inside, own, jnp.zeros_like(own))

    early, late, ops = gather_blocks(own, side, left_ops, right_ops)
    skip = sum(a.shape[0] for a in early)

    table = lax.dynamic_slice_in_dim(sources, my_sec * sec_dev, sec_dev, 1)
    table = jnp.concatenate([table, swap(table, "op", 1)], axis=0)
    table = jnp.transpose(table).reshape(-1)
    device, local = table // sec_dev, table % sec_dev
    in_y = ring_place(device // side, my_sec // side, side)
    in_x = ring_place(device % side, my_sec % side, side)
    place = jnp.where(core == 0, in_y * side + in_x, in_x * side + in_y)
    slots = array_place(place) * sec_dev + local

    live = jnp.arange(tile, dtype=jnp.int32)[None, :] < block_dims[:, None]
    window = live[:, :, None] & live[:, None, :]
    wide = jnp.where(window[:, None], wavefunction, 0).astype(jnp.float32)
    norms = jnp.sum(wide * wide, axis=(2, 3))

    sums = early_sums(slots, *ops, early)
    partial = late_sums(slots, own, sums, *ops, late, skip, op_count)
    parts = lax.all_to_all(partial, "op", split_axis=0, concat_axis=0, tiled=True)
    lanes = LANES
    parts = parts.reshape(chips, vectors, -1, share, lanes)
    numer = jnp.sum(parts[:, :, -1].astype(jnp.float32), axis=(0, 2, 3))
    numer = numer + jnp.sum(energies[:, None] * norms, axis=0)
    scalars = jnp.concatenate([numer, jnp.sum(norms, axis=0)])
    scalars = jnp.pad(scalars[None, None, :], ((0, 0), (0, 7), (0, 128 - 2 * vectors)))
    scalars = jnp.broadcast_to(scalars, (sec_count, 8, 128))
    scalars = lax.all_to_all(scalars, "sec", split_axis=0, concat_axis=0, tiled=True)
    scalars = jnp.sum(scalars[:, 0, : 2 * vectors], axis=0)
    rayleigh = scalars[:vectors] / scalars[vectors:]

    parts = parts[:, :, :-1].reshape(chips, vectors, sec_dev, tile // lanes, share, lanes)
    summed = jnp.sum(parts.astype(jnp.float32), axis=0)
    summed = jnp.concatenate([summed[:, :, cut] for cut in range(tile // lanes)], axis=3)
    summed = jnp.transpose(summed, (2, 1, 0, 3))
    rows = lax.dynamic_slice_in_dim(wavefunction, my_op * share, share, 2)
    live_rows = lax.dynamic_slice_in_dim(live, my_op * share, share, 1)
    row_window = jnp.transpose(live_rows)[:, :, None, None] & live[None, :, None, :]
    rows = jnp.where(row_window, jnp.transpose(rows, (2, 0, 1, 3)).astype(jnp.float32), 0.0)
    sigma = jnp.where(row_window, summed + energies[None, :, None, None] * rows, 0.0)
    residual = sigma - rayleigh[None, None, :, None] * rows
    return (residual, rayleigh)


def solution(mesh):
    in_specs = (
        P("sec", None, None, None),
        P("op", "sec", None, None),
        P("op", "sec", None, None),
        P("op", None),
        P("sec"),
        P("sec"),
    )
    out_specs = (P("op", "sec", None, None), P())
    return jax.shard_map(body, mesh=mesh, in_specs=in_specs, out_specs=out_specs, check_vma=False)
```

```python
import functools

import jax
import jax.numpy as jnp
from jax import lax
from jax.experimental import pallas as pl
from jax.experimental.pallas import tpu as pltpu
from jax.sharding import PartitionSpec as P

LATE_GROUP = 8
LANES = 128


def start_places(arrays, vec, sems):
    copies = []
    at = 0
    for i, array in enumerate(arrays):
        count = array.shape[0]
        copies.append(pltpu.make_async_copy(array, vec.at[pl.ds(at, count)], sems.at[i]))
        at += count
    for copy in copies:
        copy.start()
    return copies


def early_kernel(slots, left_a, left_b, right_a, right_b, *rest):
    arrays, (sums, vec, sems) = rest[:-3], rest[-3:]
    t = pl.program_id(0)
    half = left_a.shape[0]
    zero = vec.shape[0] - 1

    @pl.when(t == 0)
    def _():
        copies = start_places(arrays, vec, sems)
        vec[zero] = jnp.zeros(vec.shape[1:], vec.dtype)
        for copy in copies:
            copy.wait()

    for k in range(2 * half):
        left, right = (left_a, right_a) if k < half else (left_b, right_b)
        block = vec[jnp.minimum(slots[t * 2 * half + k], zero)]
        inner = jnp.dot(left[k % half, 0], block, preferred_element_type=jnp.float32)
        term = lax.dot_general(
            inner.astype(jnp.bfloat16), right[k % half, 0], (((1,), (1,)), ((), ())),
            preferred_element_type=jnp.float32,
        )
        if k == 0:
            sums[0] = term
        else:
            sums[0] += term


def early_sums(slots, left_a, left_b, right_a, right_b, arrays):
    half, sec_dev, tile, _ = left_a.shape
    total = sum(a.shape[0] for a in arrays)
    ops = pl.BlockSpec((half, 1, tile, tile), lambda t, s: (0, t, 0, 0))
    return pl.pallas_call(
        early_kernel,
        grid_spec=pltpu.PrefetchScalarGridSpec(
            num_scalar_prefetch=1,
            grid=(sec_dev,),
            in_specs=[ops, ops, ops, ops] + [pl.BlockSpec(memory_space=pl.ANY)] * len(arrays),
            out_specs=pl.BlockSpec((1, tile, tile), lambda t, s: (t, 0, 0)),
            scratch_shapes=[
                pltpu.VMEM((total + 1, tile, tile), jnp.bfloat16),
                pltpu.SemaphoreType.DMA((len(arrays),)),
            ],
        ),
        out_shape=jax.ShapeDtypeStruct((sec_dev, tile, tile), jnp.float32),
        compiler_params=pltpu.CompilerParams(vmem_limit_bytes=48 * 2**20),
        cost_estimate=pl.CostEstimate(
            flops=2 * 2 * sec_dev * 2 * half * tile**3,
            bytes_accessed=2 * tile * tile * (total + 8 * half * sec_dev),
            transcendentals=0,
        ),
    )(slots, left_a, left_b, right_a, right_b, *arrays)


def late_kernel(skip, slots, own, early, left_a, left_b, right_a, right_b, *rest):
    arrays, scratch = rest[:-10], rest[-10:]
    out, vec, lefts, rights, acc, blocks, targets, sems, left_sems, right_sems = scratch
    half, sec_dev, tile, _ = left_a.shape
    size = 2 * half
    total = vec.shape[0] - 1
    block_copies = start_places(arrays, vec, sems)
    vec[total] = jnp.zeros(vec.shape[1:], vec.dtype)

    def enlist(pair, count):
        slot = slots[pair]
        mine = slot >= skip

        @pl.when(mine)
        def _():
            t, k = lax.div(pair, size), lax.rem(pair, size)
            blocks[count] = slot - skip
            targets[count] = t

            @pl.when(k < half)
            def _():
                pltpu.make_async_copy(left_a.at[k, t], lefts.at[count], left_sems.at[count]).start()
                pltpu.make_async_copy(right_a.at[k, t], rights.at[count], right_sems.at[count]).start()

            @pl.when(k >= half)
            def _():
                pltpu.make_async_copy(
                    left_b.at[k - half, t], lefts.at[count], left_sems.at[count]
                ).start()
                pltpu.make_async_copy(
                    right_b.at[k - half, t], rights.at[count], right_sems.at[count]
                ).start()

        return count + mine.astype(jnp.int32)

    count = lax.fori_loop(0, sec_dev * size, enlist, jnp.int32(0))
    for i in range(LATE_GROUP):
        blocks[count + i] = total
        targets[count + i] = 0
    acc[...] = early[...]
    for copy in block_copies:
        copy.wait()

    def group(i, carry):
        ats = [i * LATE_GROUP + j for j in range(LATE_GROUP)]
        for at in ats:

            @pl.when(at < count)
            def _():
                pltpu.make_async_copy(left_a.at[0, 0], lefts.at[at], left_sems.at[at]).wait()
                pltpu.make_async_copy(right_a.at[0, 0], rights.at[at], right_sems.at[at]).wait()

        terms = []
        for at in ats:
            place = jnp.where(at < count, at, 0)
            inner = jnp.dot(lefts[place], vec[blocks[at]], preferred_element_type=jnp.float32)
            terms.append(
                lax.dot_general(
                    inner.astype(jnp.bfloat16), rights[place], (((1,), (1,)), ((), ())),
                    preferred_element_type=jnp.float32,
                )
            )
        for at, term in zip(ats, terms):
            acc[targets[at]] += term
        return carry

    lax.fori_loop(0, lax.div(count + LATE_GROUP - 1, LATE_GROUP), group, 0)
    lay_out(acc, own, out)


def lay_out(acc, own, out):
    sec_dev, tile, _ = acc.shape
    op_count, _, lanes = out.shape
    share = tile // op_count
    cuts = tile // lanes
    dots = jnp.zeros((8, tile), jnp.float32)
    for t in range(sec_dev):
        total = acc[t]
        for cut in range(cuts):
            part = total[:, cut * lanes : (cut + 1) * lanes].reshape(op_count, share, lanes)
            row = (t * cuts + cut) * share
            out[:, row : row + share, :] = part.astype(out.dtype)
        mine = own[t].astype(jnp.float32) * total
        dots += jnp.sum(mine.reshape(tile // 8, 8, tile), axis=0)
    row = jnp.sum(dots, axis=0, keepdims=True)
    row = sum(row[:, cut * lanes : (cut + 1) * lanes] for cut in range(cuts))
    high = row.astype(jnp.bfloat16).astype(jnp.float32)
    mid = (row - high).astype(jnp.bfloat16).astype(jnp.float32)
    low = row - high - mid
    at = lax.broadcasted_iota(jnp.int32, (share, lanes), 0)
    slab = jnp.where(at == 0, high, jnp.where(at == 1, mid, jnp.where(at == 2, low, 0.0)))
    slab = slab.astype(out.dtype)
    out[:, sec_dev * cuts * share :, :] = jnp.broadcast_to(slab[None], (op_count, share, lanes))


def late_sums(slots, own, early, left_a, left_b, right_a, right_b, arrays, skip, op_count):
    half, sec_dev, tile, _ = left_a.shape
    size = 2 * half
    share = tile // op_count
    total = sum(a.shape[0] for a in arrays)
    out_shape = (op_count, (sec_dev * (tile // LANES) + 1) * share, LANES)
    whole = pl.BlockSpec(memory_space=pltpu.VMEM)
    return pl.pallas_call(
        functools.partial(late_kernel, skip),
        grid_spec=pltpu.PrefetchScalarGridSpec(
            num_scalar_prefetch=1,
            grid=(),
            in_specs=[whole, whole] + [pl.BlockSpec(memory_space=pl.ANY)] * (4 + len(arrays)),
            out_specs=whole,
            scratch_shapes=[
                pltpu.VMEM((total + 1, tile, tile), jnp.bfloat16),
                pltpu.VMEM((sec_dev * size, tile, tile), jnp.bfloat16),
                pltpu.VMEM((sec_dev * size, tile, tile), jnp.bfloat16),
                pltpu.VMEM((sec_dev, tile, tile), jnp.float32),
                pltpu.SMEM((sec_dev * size + LATE_GROUP,), jnp.int32),
                pltpu.SMEM((sec_dev * size + LATE_GROUP,), jnp.int32),
                pltpu.SemaphoreType.DMA((len(arrays),)),
                pltpu.SemaphoreType.DMA((sec_dev * size,)),
                pltpu.SemaphoreType.DMA((sec_dev * size,)),
            ],
        ),
        out_shape=jax.ShapeDtypeStruct(out_shape, jnp.bfloat16),
        compiler_params=pltpu.CompilerParams(vmem_limit_bytes=48 * 2**20),
        cost_estimate=pl.CostEstimate(
            flops=2 * sec_dev * half * tile**3,
            bytes_accessed=2 * tile * tile * (total + 2 * half * sec_dev),
            transcendentals=0,
        ),
    )(slots, own, early, left_a, left_b, right_a, right_b, *arrays)


def swap(x, axis, mask):
    count = lax.axis_size(axis)
    return lax.ppermute(x, axis, [(i, i ^ mask) for i in range(count)])


def step(x, side, ring, way):
    perm = []
    for op in range(lax.axis_size("op")):
        for at in range(side * side):
            y, x_ = at // side, at % side
            if (op + ring) % 2 == 0:
                x_ = (x_ + way) % side
            else:
                y = (y + way) % side
            perm.append((op * side * side + at, op * side * side + y * side + x_))
    return lax.ppermute(x, ("op", "sec"), perm)


def gather_blocks(own, side, left_ops, right_ops):
    first = lambda b, way: step(b, side, 0, way)
    second = lambda b, way: step(b, side, 1, way)
    left_other = swap(left_ops, "op", 1)
    behind, ahead = first(own, 1), first(own, -1)
    own, behind, ahead, left_other, right = lax.optimization_barrier(
        (own, behind, ahead, left_other, right_ops)
    )
    right_other = swap(right, "op", 1)
    far = first(behind, 1)
    own_a, behind_a, ahead_a = second(own, -1), second(behind, -1), second(ahead, -1)
    own, behind, ahead, far, right_other = lax.optimization_barrier(
        (own, behind, ahead, far, right_other)
    )
    far_a, far_b = second(far, -1), second(far, 1)
    own_b, behind_b, ahead_b = second(own, 1), second(behind, 1), second(ahead, 1)
    own_f, behind_f = second(own_b, 1), second(behind_a, -1)
    ahead_f, far_f = second(ahead_a, -1), second(far_a, -1)
    early = [
        own, behind, ahead, far, own_b, behind_b, ahead_b, own_a, behind_a, ahead_a, far_a,
    ]
    late = [far_b, own_f, behind_f, ahead_f, far_f]
    return early, late, left_other, right_other


def array_place(place):
    return jnp.where(place == 7, 11, jnp.where((place > 7) & (place < 12), place - 1, place))


def ring_place(source, mine, side):
    away = (source - mine) % side
    return jnp.where(away == 0, 0, jnp.where(away == side - 1, 1, away + 1))


def body(wavefunction, left_ops, right_ops, sources, block_dims, energies):
    op_count = lax.axis_size("op")
    sec_count = lax.axis_size("sec")
    my_sec = lax.axis_index("sec")
    my_op = lax.axis_index("op")
    sec_dev, vectors, tile, _ = wavefunction.shape
    share = tile // op_count
    chips = op_count // vectors
    core = my_op % vectors
    side = 4

    own = lax.dynamic_index_in_dim(wavefunction, core, 1, keepdims=False)
    row = lax.broadcasted_iota(jnp.int32, own.shape, 1)
    column = lax.broadcasted_iota(jnp.int32, own.shape, 2)
    inside = jnp.maximum(row, column) < block_dims[:, None, None]
    own = jnp.where(inside, own, jnp.zeros_like(own))

    early, late, left_other, right_other = gather_blocks(own, side, left_ops, right_ops)
    skip = sum(a.shape[0] for a in early)

    table = lax.dynamic_slice_in_dim(sources, my_sec * sec_dev, sec_dev, 1)
    table = jnp.concatenate([table, swap(table, "op", 1)], axis=0)
    table = jnp.transpose(table).reshape(-1)
    device, local = table // sec_dev, table % sec_dev
    in_y = ring_place(device // side, my_sec // side, side)
    in_x = ring_place(device % side, my_sec % side, side)
    place = jnp.where(core == 0, in_y * side + in_x, in_x * side + in_y)
    slots = array_place(place) * sec_dev + local

    live = jnp.arange(tile, dtype=jnp.int32)[None, :] < block_dims[:, None]
    window = live[:, :, None] & live[:, None, :]
    wide = jnp.where(window[:, None], wavefunction, 0).astype(jnp.float32)
    norms = jnp.sum(wide * wide, axis=(2, 3))

    ops = (left_ops, left_other, right_ops, right_other)
    sums = early_sums(slots, *ops, early)
    partial = late_sums(slots, own, sums, *ops, late, skip, op_count)
    parts = lax.all_to_all(partial, "op", split_axis=0, concat_axis=0, tiled=True)
    lanes = LANES
    parts = parts.reshape(chips, vectors, -1, share, lanes)
    numer = jnp.sum(parts[:, :, -1].astype(jnp.float32), axis=(0, 2, 3))
    numer = numer + jnp.sum(energies[:, None] * norms, axis=0)
    scalars = jnp.concatenate([numer, jnp.sum(norms, axis=0)])
    scalars = jnp.pad(scalars[None, None, :], ((0, 0), (0, 7), (0, 128 - 2 * vectors)))
    scalars = jnp.broadcast_to(scalars, (sec_count, 8, 128))
    scalars = lax.all_to_all(scalars, "sec", split_axis=0, concat_axis=0, tiled=True)
    scalars = jnp.sum(scalars[:, 0, : 2 * vectors], axis=0)
    rayleigh = scalars[:vectors] / scalars[vectors:]

    parts = parts[:, :, :-1].reshape(chips, vectors, sec_dev, tile // lanes, share, lanes)
    summed = jnp.sum(parts.astype(jnp.float32), axis=0)
    summed = jnp.concatenate([summed[:, :, cut] for cut in range(tile // lanes)], axis=3)
    summed = jnp.transpose(summed, (2, 1, 0, 3))
    rows = lax.dynamic_slice_in_dim(wavefunction, my_op * share, share, 2)
    live_rows = lax.dynamic_slice_in_dim(live, my_op * share, share, 1)
    row_window = jnp.transpose(live_rows)[:, :, None, None] & live[None, :, None, :]
    rows = jnp.where(row_window, jnp.transpose(rows, (2, 0, 1, 3)).astype(jnp.float32), 0.0)
    sigma = jnp.where(row_window, summed + energies[None, :, None, None] * rows, 0.0)
    residual = sigma - rayleigh[None, None, :, None] * rows
    return (residual, rayleigh)


def solution(mesh):
    in_specs = (
        P("sec", None, None, None),
        P("op", "sec", None, None),
        P("op", "sec", None, None),
        P("op", None),
        P("sec"),
        P("sec"),
    )
    out_specs = (P("op", "sec", None, None), P())
    return jax.shard_map(body, mesh=mesh, in_specs=in_specs, out_specs=out_specs, check_vma=False)
```

```python
import functools

import jax
import jax.numpy as jnp
from jax import lax
from jax.experimental import pallas as pl
from jax.experimental.pallas import tpu as pltpu
from jax.sharding import PartitionSpec as P

LATE_GROUP = 8
LANES = 128


def start_places(arrays, vec, sems):
    copies = []
    at = 0
    for i, array in enumerate(arrays):
        count = array.shape[0]
        copies.append(pltpu.make_async_copy(array, vec.at[pl.ds(at, count)], sems.at[i]))
        at += count
    for copy in copies:
        copy.start()
    return copies


def early_kernel(slots, left_a, left_b, right_a, right_b, *rest):
    arrays, (sums, vec, sems) = rest[:-3], rest[-3:]
    t = pl.program_id(0)
    half = left_a.shape[0]
    zero = vec.shape[0] - 1

    @pl.when(t == 0)
    def _():
        copies = start_places(arrays, vec, sems)
        vec[zero] = jnp.zeros(vec.shape[1:], vec.dtype)
        for copy in copies:
            copy.wait()

    for k in range(2 * half):
        left, right = (left_a, right_a) if k < half else (left_b, right_b)
        block = vec[jnp.minimum(slots[t * 2 * half + k], zero)]
        inner = jnp.dot(left[k % half, 0], block, preferred_element_type=jnp.float32)
        term = lax.dot_general(
            inner.astype(jnp.bfloat16), right[k % half, 0], (((1,), (1,)), ((), ())),
            preferred_element_type=jnp.float32,
        )
        if k == 0:
            sums[0] = term
        else:
            sums[0] += term


def early_sums(slots, left_a, left_b, right_a, right_b, arrays):
    half, sec_dev, tile, _ = left_a.shape
    total = sum(a.shape[0] for a in arrays)
    ops = pl.BlockSpec((half, 1, tile, tile), lambda t, s: (0, t, 0, 0))
    return pl.pallas_call(
        early_kernel,
        grid_spec=pltpu.PrefetchScalarGridSpec(
            num_scalar_prefetch=1,
            grid=(sec_dev,),
            in_specs=[ops, ops, ops, ops] + [pl.BlockSpec(memory_space=pl.ANY)] * len(arrays),
            out_specs=pl.BlockSpec((1, tile, tile), lambda t, s: (t, 0, 0)),
            scratch_shapes=[
                pltpu.VMEM((total + 1, tile, tile), jnp.bfloat16),
                pltpu.SemaphoreType.DMA((len(arrays),)),
            ],
        ),
        out_shape=jax.ShapeDtypeStruct((sec_dev, tile, tile), jnp.float32),
        compiler_params=pltpu.CompilerParams(vmem_limit_bytes=48 * 2**20),
        cost_estimate=pl.CostEstimate(
            flops=2 * 2 * sec_dev * 2 * half * tile**3,
            bytes_accessed=2 * tile * tile * (total + 8 * half * sec_dev),
            transcendentals=0,
        ),
    )(slots, left_a, left_b, right_a, right_b, *arrays)


def late_kernel(skip, slots, own, early, left_a, left_b, right_a, right_b, *rest):
    arrays, scratch = rest[:-10], rest[-10:]
    out, vec, lefts, rights, acc, blocks, targets, sems, left_sems, right_sems = scratch
    half, sec_dev, tile, _ = left_a.shape
    size = 2 * half
    total = vec.shape[0] - 1
    block_copies = start_places(arrays, vec, sems)
    vec[total] = jnp.zeros(vec.shape[1:], vec.dtype)

    def enlist(pair, count):
        slot = slots[pair]
        mine = slot >= skip

        @pl.when(mine)
        def _():
            t, k = lax.div(pair, size), lax.rem(pair, size)
            blocks[count] = slot - skip
            targets[count] = t

            @pl.when(k < half)
            def _():
                pltpu.make_async_copy(left_a.at[k, t], lefts.at[count], left_sems.at[count]).start()
                pltpu.make_async_copy(right_a.at[k, t], rights.at[count], right_sems.at[count]).start()

            @pl.when(k >= half)
            def _():
                pltpu.make_async_copy(
                    left_b.at[k - half, t], lefts.at[count], left_sems.at[count]
                ).start()
                pltpu.make_async_copy(
                    right_b.at[k - half, t], rights.at[count], right_sems.at[count]
                ).start()

        return count + mine.astype(jnp.int32)

    count = lax.fori_loop(0, sec_dev * size, enlist, jnp.int32(0))
    for i in range(LATE_GROUP):
        blocks[count + i] = total
        targets[count + i] = 0
    acc[...] = early[...]
    for copy in block_copies:
        copy.wait()

    def group(i, carry):
        ats = [i * LATE_GROUP + j for j in range(LATE_GROUP)]
        for at in ats:

            @pl.when(at < count)
            def _():
                pltpu.make_async_copy(left_a.at[0, 0], lefts.at[at], left_sems.at[at]).wait()
                pltpu.make_async_copy(right_a.at[0, 0], rights.at[at], right_sems.at[at]).wait()

        terms = []
        for at in ats:
            place = jnp.where(at < count, at, 0)
            inner = jnp.dot(lefts[place], vec[blocks[at]], preferred_element_type=jnp.float32)
            terms.append(
                lax.dot_general(
                    inner.astype(jnp.bfloat16), rights[place], (((1,), (1,)), ((), ())),
                    preferred_element_type=jnp.float32,
                )
            )
        for at, term in zip(ats, terms):
            acc[targets[at]] += term
        return carry

    lax.fori_loop(0, lax.div(count + LATE_GROUP - 1, LATE_GROUP), group, 0)
    lay_out(acc, own, out)


def lay_out(acc, own, out):
    sec_dev, tile, _ = acc.shape
    op_count, _, lanes = out.shape
    share = tile // op_count
    cuts = tile // lanes
    dots = jnp.zeros((8, tile), jnp.float32)
    for t in range(sec_dev):
        total = acc[t]
        for cut in range(cuts):
            part = total[:, cut * lanes : (cut + 1) * lanes].reshape(op_count, share, lanes)
            row = (t * cuts + cut) * share
            out[:, row : row + share, :] = part.astype(out.dtype)
        mine = own[t].astype(jnp.float32) * total
        dots += jnp.sum(mine.reshape(tile // 8, 8, tile), axis=0)
    row = jnp.sum(dots, axis=0, keepdims=True)
    row = sum(row[:, cut * lanes : (cut + 1) * lanes] for cut in range(cuts))
    high = row.astype(jnp.bfloat16).astype(jnp.float32)
    mid = (row - high).astype(jnp.bfloat16).astype(jnp.float32)
    low = row - high - mid
    at = lax.broadcasted_iota(jnp.int32, (share, lanes), 0)
    slab = jnp.where(at == 0, high, jnp.where(at == 1, mid, jnp.where(at == 2, low, 0.0)))
    slab = slab.astype(out.dtype)
    out[:, sec_dev * cuts * share :, :] = jnp.broadcast_to(slab[None], (op_count, share, lanes))


def late_sums(slots, own, early, left_a, left_b, right_a, right_b, arrays, skip, op_count):
    half, sec_dev, tile, _ = left_a.shape
    size = 2 * half
    share = tile // op_count
    total = sum(a.shape[0] for a in arrays)
    out_shape = (op_count, (sec_dev * (tile // LANES) + 1) * share, LANES)
    whole = pl.BlockSpec(memory_space=pltpu.VMEM)
    return pl.pallas_call(
        functools.partial(late_kernel, skip),
        grid_spec=pltpu.PrefetchScalarGridSpec(
            num_scalar_prefetch=1,
            grid=(),
            in_specs=[whole, whole] + [pl.BlockSpec(memory_space=pl.ANY)] * (4 + len(arrays)),
            out_specs=whole,
            scratch_shapes=[
                pltpu.VMEM((total + 1, tile, tile), jnp.bfloat16),
                pltpu.VMEM((sec_dev * size, tile, tile), jnp.bfloat16),
                pltpu.VMEM((sec_dev * size, tile, tile), jnp.bfloat16),
                pltpu.VMEM((sec_dev, tile, tile), jnp.float32),
                pltpu.SMEM((sec_dev * size + LATE_GROUP,), jnp.int32),
                pltpu.SMEM((sec_dev * size + LATE_GROUP,), jnp.int32),
                pltpu.SemaphoreType.DMA((len(arrays),)),
                pltpu.SemaphoreType.DMA((sec_dev * size,)),
                pltpu.SemaphoreType.DMA((sec_dev * size,)),
            ],
        ),
        out_shape=jax.ShapeDtypeStruct(out_shape, jnp.bfloat16),
        compiler_params=pltpu.CompilerParams(vmem_limit_bytes=48 * 2**20),
        cost_estimate=pl.CostEstimate(
            flops=2 * sec_dev * half * tile**3,
            bytes_accessed=2 * tile * tile * (total + 2 * half * sec_dev),
            transcendentals=0,
        ),
    )(slots, own, early, left_a, left_b, right_a, right_b, *arrays)


def swap(x, axis, mask):
    count = lax.axis_size(axis)
    return lax.ppermute(x, axis, [(i, i ^ mask) for i in range(count)])


def step(x, side, ring, way):
    perm = []
    for op in range(lax.axis_size("op")):
        for at in range(side * side):
            y, x_ = at // side, at % side
            if (op + ring) % 2 == 0:
                x_ = (x_ + way) % side
            else:
                y = (y + way) % side
            perm.append((op * side * side + at, op * side * side + y * side + x_))
    return lax.ppermute(x, ("op", "sec"), perm)


def join_kernel(one, other, joined):
    count = one.shape[0]
    joined[:count] = one[...]
    joined[count:] = other[...]


def join(one, other):
    whole = pl.BlockSpec(memory_space=pltpu.VMEM)
    shape = (one.shape[0] + other.shape[0],) + one.shape[1:]
    return pl.pallas_call(
        join_kernel,
        in_specs=[whole] * 2,
        out_specs=whole,
        out_shape=jax.ShapeDtypeStruct(shape, one.dtype),
    )(one, other)


def gather_blocks(own, side, left_ops, right_ops):
    first = lambda b, way: step(b, side, 0, way)
    second = lambda b, way: step(b, side, 1, way)
    left_other = swap(left_ops, "op", 1)
    behind, ahead = first(own, 1), first(own, -1)
    own, behind, ahead, left_other, right = lax.optimization_barrier(
        (own, behind, ahead, left_other, right_ops)
    )
    right_other = swap(right, "op", 1)
    far = first(behind, 1)
    own_a = second(own, -1)
    pair = join(behind, ahead)
    pair_a = second(pair, -1)
    own, pair, far, right_other = lax.optimization_barrier((own, pair, far, right_other))
    far_a, far_b = second(far, -1), second(far, 1)
    own_b, pair_b = second(own, 1), second(pair, 1)
    own_f, pair_f, far_f = second(own_b, 1), second(pair_a, -1), second(far_a, -1)
    early = [own, pair, far, own_b, pair_b, own_a, pair_a, far_a]
    late = [far_b, own_f, pair_f, far_f]
    return early, late, left_other, right_other


def array_place(place):
    return jnp.where(place == 7, 11, jnp.where((place > 7) & (place < 12), place - 1, place))


def ring_place(source, mine, side):
    away = (source - mine) % side
    return jnp.where(away == 0, 0, jnp.where(away == side - 1, 1, away + 1))


def body(wavefunction, left_ops, right_ops, sources, block_dims, energies):
    op_count = lax.axis_size("op")
    sec_count = lax.axis_size("sec")
    my_sec = lax.axis_index("sec")
    my_op = lax.axis_index("op")
    sec_dev, vectors, tile, _ = wavefunction.shape
    share = tile // op_count
    chips = op_count // vectors
    core = my_op % vectors
    side = 4

    own = lax.dynamic_index_in_dim(wavefunction, core, 1, keepdims=False)
    row = lax.broadcasted_iota(jnp.int32, own.shape, 1)
    column = lax.broadcasted_iota(jnp.int32, own.shape, 2)
    inside = jnp.maximum(row, column) < block_dims[:, None, None]
    own = jnp.where(inside, own, jnp.zeros_like(own))

    early, late, left_other, right_other = gather_blocks(own, side, left_ops, right_ops)
    skip = sum(a.shape[0] for a in early)

    table = lax.dynamic_slice_in_dim(sources, my_sec * sec_dev, sec_dev, 1)
    table = jnp.concatenate([table, swap(table, "op", 1)], axis=0)
    table = jnp.transpose(table).reshape(-1)
    device, local = table // sec_dev, table % sec_dev
    in_y = ring_place(device // side, my_sec // side, side)
    in_x = ring_place(device % side, my_sec % side, side)
    place = jnp.where(core == 0, in_y * side + in_x, in_x * side + in_y)
    slots = array_place(place) * sec_dev + local

    live = jnp.arange(tile, dtype=jnp.int32)[None, :] < block_dims[:, None]
    window = live[:, :, None] & live[:, None, :]
    wide = jnp.where(window[:, None], wavefunction, 0).astype(jnp.float32)
    norms = jnp.sum(wide * wide, axis=(2, 3))

    ops = (left_ops, left_other, right_ops, right_other)
    sums = early_sums(slots, *ops, early)
    partial = late_sums(slots, own, sums, *ops, late, skip, op_count)
    parts = lax.all_to_all(partial, "op", split_axis=0, concat_axis=0, tiled=True)
    lanes = LANES
    parts = parts.reshape(chips, vectors, -1, share, lanes)
    numer = jnp.sum(parts[:, :, -1].astype(jnp.float32), axis=(0, 2, 3))
    numer = numer + jnp.sum(energies[:, None] * norms, axis=0)
    scalars = jnp.concatenate([numer, jnp.sum(norms, axis=0)])
    scalars = jnp.pad(scalars[None, None, :], ((0, 0), (0, 7), (0, 128 - 2 * vectors)))
    scalars = jnp.broadcast_to(scalars, (sec_count, 8, 128))
    scalars = lax.all_to_all(scalars, "sec", split_axis=0, concat_axis=0, tiled=True)
    scalars = jnp.sum(scalars[:, 0, : 2 * vectors], axis=0)
    rayleigh = scalars[:vectors] / scalars[vectors:]

    parts = parts[:, :, :-1].reshape(chips, vectors, sec_dev, tile // lanes, share, lanes)
    summed = jnp.sum(parts.astype(jnp.float32), axis=0)
    summed = jnp.concatenate([summed[:, :, cut] for cut in range(tile // lanes)], axis=3)
    summed = jnp.transpose(summed, (2, 1, 0, 3))
    rows = lax.dynamic_slice_in_dim(wavefunction, my_op * share, share, 2)
    live_rows = lax.dynamic_slice_in_dim(live, my_op * share, share, 1)
    row_window = jnp.transpose(live_rows)[:, :, None, None] & live[None, :, None, :]
    rows = jnp.where(row_window, jnp.transpose(rows, (2, 0, 1, 3)).astype(jnp.float32), 0.0)
    sigma = jnp.where(row_window, summed + energies[None, :, None, None] * rows, 0.0)
    residual = sigma - rayleigh[None, None, :, None] * rows
    return (residual, rayleigh)


def solution(mesh):
    in_specs = (
        P("sec", None, None, None),
        P("op", "sec", None, None),
        P("op", "sec", None, None),
        P("op", None),
        P("sec"),
        P("sec"),
    )
    out_specs = (P("op", "sec", None, None), P())
    return jax.shard_map(body, mesh=mesh, in_specs=in_specs, out_specs=out_specs, check_vma=False)
```

```python
import functools

import jax
import jax.numpy as jnp
from jax import lax
from jax.experimental import pallas as pl
from jax.experimental.pallas import tpu as pltpu
from jax.sharding import PartitionSpec as P

LATE_GROUP = 8
LANES = 128


def start_places(arrays, vec, sems):
    copies = []
    at = 0
    for i, array in enumerate(arrays):
        count = array.shape[0]
        copies.append(pltpu.make_async_copy(array, vec.at[pl.ds(at, count)], sems.at[i]))
        at += count
    for copy in copies:
        copy.start()
    return copies


def early_kernel(slots, left_a, left_b, right_a, right_b, *rest):
    arrays, (sums, vec, sems) = rest[:-3], rest[-3:]
    t = pl.program_id(0)
    half = left_a.shape[0]
    zero = vec.shape[0] - 1

    @pl.when(t == 0)
    def _():
        copies = start_places(arrays, vec, sems)
        vec[zero] = jnp.zeros(vec.shape[1:], vec.dtype)
        for copy in copies:
            copy.wait()

    for k in range(2 * half):
        left, right = (left_a, right_a) if k < half else (left_b, right_b)
        block = vec[jnp.minimum(slots[t * 2 * half + k], zero)]
        inner = jnp.dot(left[k % half, 0], block, preferred_element_type=jnp.float32)
        term = lax.dot_general(
            inner.astype(jnp.bfloat16), right[k % half, 0], (((1,), (1,)), ((), ())),
            preferred_element_type=jnp.float32,
        )
        if k == 0:
            sums[0] = term
        else:
            sums[0] += term


def early_sums(slots, left_a, left_b, right_a, right_b, arrays):
    half, sec_dev, tile, _ = left_a.shape
    total = sum(a.shape[0] for a in arrays)
    ops = pl.BlockSpec((half, 1, tile, tile), lambda t, s: (0, t, 0, 0))
    return pl.pallas_call(
        early_kernel,
        grid_spec=pltpu.PrefetchScalarGridSpec(
            num_scalar_prefetch=1,
            grid=(sec_dev,),
            in_specs=[ops, ops, ops, ops] + [pl.BlockSpec(memory_space=pl.ANY)] * len(arrays),
            out_specs=pl.BlockSpec((1, tile, tile), lambda t, s: (t, 0, 0)),
            scratch_shapes=[
                pltpu.VMEM((total + 1, tile, tile), jnp.bfloat16),
                pltpu.SemaphoreType.DMA((len(arrays),)),
            ],
        ),
        out_shape=jax.ShapeDtypeStruct((sec_dev, tile, tile), jnp.float32),
        compiler_params=pltpu.CompilerParams(vmem_limit_bytes=48 * 2**20),
        cost_estimate=pl.CostEstimate(
            flops=2 * 2 * sec_dev * 2 * half * tile**3,
            bytes_accessed=2 * tile * tile * (total + 8 * half * sec_dev),
            transcendentals=0,
        ),
    )(slots, left_a, left_b, right_a, right_b, *arrays)


def late_kernel(skip, slots, own, early, left_a, left_b, right_a, right_b, *rest):
    arrays, scratch = rest[:-10], rest[-10:]
    out, vec, lefts, rights, acc, blocks, targets, sems, left_sems, right_sems = scratch
    half, sec_dev, tile, _ = left_a.shape
    size = 2 * half
    total = vec.shape[0] - 1
    block_copies = start_places(arrays, vec, sems)
    vec[total] = jnp.zeros(vec.shape[1:], vec.dtype)

    def enlist(pair, count):
        slot = slots[pair]
        mine = slot >= skip

        @pl.when(mine)
        def _():
            t, k = lax.div(pair, size), lax.rem(pair, size)
            blocks[count] = slot - skip
            targets[count] = t

            @pl.when(k < half)
            def _():
                pltpu.make_async_copy(left_a.at[k, t], lefts.at[count], left_sems.at[count]).start()
                pltpu.make_async_copy(right_a.at[k, t], rights.at[count], right_sems.at[count]).start()

            @pl.when(k >= half)
            def _():
                pltpu.make_async_copy(
                    left_b.at[k - half, t], lefts.at[count], left_sems.at[count]
                ).start()
                pltpu.make_async_copy(
                    right_b.at[k - half, t], rights.at[count], right_sems.at[count]
                ).start()

        return count + mine.astype(jnp.int32)

    count = lax.fori_loop(0, sec_dev * size, enlist, jnp.int32(0))
    for i in range(LATE_GROUP):
        blocks[count + i] = total
        targets[count + i] = 0
    acc[...] = early[...]
    for copy in block_copies:
        copy.wait()

    def group(i, carry):
        ats = [i * LATE_GROUP + j for j in range(LATE_GROUP)]
        for at in ats:

            @pl.when(at < count)
            def _():
                pltpu.make_async_copy(left_a.at[0, 0], lefts.at[at], left_sems.at[at]).wait()
                pltpu.make_async_copy(right_a.at[0, 0], rights.at[at], right_sems.at[at]).wait()

        terms = []
        for at in ats:
            place = jnp.where(at < count, at, 0)
            inner = jnp.dot(lefts[place], vec[blocks[at]], preferred_element_type=jnp.float32)
            terms.append(
                lax.dot_general(
                    inner.astype(jnp.bfloat16), rights[place], (((1,), (1,)), ((), ())),
                    preferred_element_type=jnp.float32,
                )
            )
        for at, term in zip(ats, terms):
            acc[targets[at]] += term
        return carry

    lax.fori_loop(0, lax.div(count + LATE_GROUP - 1, LATE_GROUP), group, 0)
    lay_out(acc, own, out)


def lay_out(acc, own, out):
    sec_dev, tile, _ = acc.shape
    op_count, _, lanes = out.shape
    share = tile // op_count
    cuts = tile // lanes
    dots = jnp.zeros((8, tile), jnp.float32)
    for t in range(sec_dev):
        total = acc[t]
        for cut in range(cuts):
            part = total[:, cut * lanes : (cut + 1) * lanes].reshape(op_count, share, lanes)
            row = (t * cuts + cut) * share
            out[:, row : row + share, :] = part.astype(out.dtype)
        mine = own[t].astype(jnp.float32) * total
        dots += jnp.sum(mine.reshape(tile // 8, 8, tile), axis=0)
    row = jnp.sum(dots, axis=0, keepdims=True)
    row = sum(row[:, cut * lanes : (cut + 1) * lanes] for cut in range(cuts))
    high = row.astype(jnp.bfloat16).astype(jnp.float32)
    mid = (row - high).astype(jnp.bfloat16).astype(jnp.float32)
    low = row - high - mid
    at = lax.broadcasted_iota(jnp.int32, (share, lanes), 0)
    slab = jnp.where(at == 0, high, jnp.where(at == 1, mid, jnp.where(at == 2, low, 0.0)))
    slab = slab.astype(out.dtype)
    out[:, sec_dev * cuts * share :, :] = jnp.broadcast_to(slab[None], (op_count, share, lanes))


def late_sums(slots, own, early, left_a, left_b, right_a, right_b, arrays, skip, op_count):
    half, sec_dev, tile, _ = left_a.shape
    size = 2 * half
    share = tile // op_count
    total = sum(a.shape[0] for a in arrays)
    out_shape = (op_count, (sec_dev * (tile // LANES) + 1) * share, LANES)
    whole = pl.BlockSpec(memory_space=pltpu.VMEM)
    return pl.pallas_call(
        functools.partial(late_kernel, skip),
        grid_spec=pltpu.PrefetchScalarGridSpec(
            num_scalar_prefetch=1,
            grid=(),
            in_specs=[whole, whole] + [pl.BlockSpec(memory_space=pl.ANY)] * (4 + len(arrays)),
            out_specs=whole,
            scratch_shapes=[
                pltpu.VMEM((total + 1, tile, tile), jnp.bfloat16),
                pltpu.VMEM((sec_dev * size, tile, tile), jnp.bfloat16),
                pltpu.VMEM((sec_dev * size, tile, tile), jnp.bfloat16),
                pltpu.VMEM((sec_dev, tile, tile), jnp.float32),
                pltpu.SMEM((sec_dev * size + LATE_GROUP,), jnp.int32),
                pltpu.SMEM((sec_dev * size + LATE_GROUP,), jnp.int32),
                pltpu.SemaphoreType.DMA((len(arrays),)),
                pltpu.SemaphoreType.DMA((sec_dev * size,)),
                pltpu.SemaphoreType.DMA((sec_dev * size,)),
            ],
        ),
        out_shape=jax.ShapeDtypeStruct(out_shape, jnp.bfloat16),
        compiler_params=pltpu.CompilerParams(vmem_limit_bytes=48 * 2**20),
        cost_estimate=pl.CostEstimate(
            flops=2 * sec_dev * half * tile**3,
            bytes_accessed=2 * tile * tile * (total + 2 * half * sec_dev),
            transcendentals=0,
        ),
    )(slots, own, early, left_a, left_b, right_a, right_b, *arrays)


def swap(x, axis, mask):
    count = lax.axis_size(axis)
    return lax.ppermute(x, axis, [(i, i ^ mask) for i in range(count)])


def step(x, side, ring, way):
    perm = []
    for op in range(lax.axis_size("op")):
        for at in range(side * side):
            y, x_ = at // side, at % side
            if (op + ring) % 2 == 0:
                x_ = (x_ + way) % side
            else:
                y = (y + way) % side
            perm.append((op * side * side + at, op * side * side + y * side + x_))
    return lax.ppermute(x, ("op", "sec"), perm)


def join_kernel(one, other, joined):
    count = one.shape[0]
    joined[:count] = one[...]
    joined[count:] = other[...]


def join(one, other):
    whole = pl.BlockSpec(memory_space=pltpu.VMEM)
    shape = (one.shape[0] + other.shape[0],) + one.shape[1:]
    return pl.pallas_call(
        join_kernel,
        in_specs=[whole] * 2,
        out_specs=whole,
        out_shape=jax.ShapeDtypeStruct(shape, one.dtype),
    )(one, other)


def gather_blocks(own, side, left_ops, right_ops):
    first = lambda b, way: step(b, side, 0, way)
    second = lambda b, way: step(b, side, 1, way)
    left_other = swap(left_ops, "op", 1)
    behind, ahead = first(own, 1), first(own, -1)
    own, behind, ahead, left_other, right = lax.optimization_barrier(
        (own, behind, ahead, left_other, right_ops)
    )
    right_other = swap(right, "op", 1)
    far = first(behind, 1)
    own_a = second(own, -1)
    pair = join(behind, ahead)
    own, own_a, pair, far, right_other = lax.optimization_barrier(
        (own, own_a, pair, far, right_other)
    )
    far_a, far_b = second(far, -1), second(far, 1)
    own_b, pair_b, pair_a = second(own, 1), second(pair, 1), second(pair, -1)
    own_f, pair_f, far_f = second(own_b, 1), second(pair_a, -1), second(far_a, -1)
    early = [own, pair, far, own_b, pair_b, own_a, pair_a, far_a]
    late = [far_b, own_f, pair_f, far_f]
    return early, late, left_other, right_other


def array_place(place):
    return jnp.where(place == 7, 11, jnp.where((place > 7) & (place < 12), place - 1, place))


def ring_place(source, mine, side):
    away = (source - mine) % side
    return jnp.where(away == 0, 0, jnp.where(away == side - 1, 1, away + 1))


def body(wavefunction, left_ops, right_ops, sources, block_dims, energies):
    op_count = lax.axis_size("op")
    sec_count = lax.axis_size("sec")
    my_sec = lax.axis_index("sec")
    my_op = lax.axis_index("op")
    sec_dev, vectors, tile, _ = wavefunction.shape
    share = tile // op_count
    chips = op_count // vectors
    core = my_op % vectors
    side = 4

    own = lax.dynamic_index_in_dim(wavefunction, core, 1, keepdims=False)
    row = lax.broadcasted_iota(jnp.int32, own.shape, 1)
    column = lax.broadcasted_iota(jnp.int32, own.shape, 2)
    inside = jnp.maximum(row, column) < block_dims[:, None, None]
    own = jnp.where(inside, own, jnp.zeros_like(own))

    early, late, left_other, right_other = gather_blocks(own, side, left_ops, right_ops)
    skip = sum(a.shape[0] for a in early)

    table = lax.dynamic_slice_in_dim(sources, my_sec * sec_dev, sec_dev, 1)
    table = jnp.concatenate([table, swap(table, "op", 1)], axis=0)
    table = jnp.transpose(table).reshape(-1)
    device, local = table // sec_dev, table % sec_dev
    in_y = ring_place(device // side, my_sec // side, side)
    in_x = ring_place(device % side, my_sec % side, side)
    place = jnp.where(core == 0, in_y * side + in_x, in_x * side + in_y)
    slots = array_place(place) * sec_dev + local

    live = jnp.arange(tile, dtype=jnp.int32)[None, :] < block_dims[:, None]
    window = live[:, :, None] & live[:, None, :]
    wide = jnp.where(window[:, None], wavefunction, 0).astype(jnp.float32)
    norms = jnp.sum(wide * wide, axis=(2, 3))

    ops = (left_ops, left_other, right_ops, right_other)
    sums = early_sums(slots, *ops, early)
    partial = late_sums(slots, own, sums, *ops, late, skip, op_count)
    parts = lax.all_to_all(partial, "op", split_axis=0, concat_axis=0, tiled=True)
    lanes = LANES
    parts = parts.reshape(chips, vectors, -1, share, lanes)
    numer = jnp.sum(parts[:, :, -1].astype(jnp.float32), axis=(0, 2, 3))
    numer = numer + jnp.sum(energies[:, None] * norms, axis=0)
    scalars = jnp.concatenate([numer, jnp.sum(norms, axis=0)])
    scalars = jnp.pad(scalars[None, None, :], ((0, 0), (0, 7), (0, 128 - 2 * vectors)))
    scalars = jnp.broadcast_to(scalars, (sec_count, 8, 128))
    scalars = lax.all_to_all(scalars, "sec", split_axis=0, concat_axis=0, tiled=True)
    scalars = jnp.sum(scalars[:, 0, : 2 * vectors], axis=0)
    rayleigh = scalars[:vectors] / scalars[vectors:]

    parts = parts[:, :, :-1].reshape(chips, vectors, sec_dev, tile // lanes, share, lanes)
    summed = jnp.sum(parts.astype(jnp.float32), axis=0)
    summed = jnp.concatenate([summed[:, :, cut] for cut in range(tile // lanes)], axis=3)
    summed = jnp.transpose(summed, (2, 1, 0, 3))
    rows = lax.dynamic_slice_in_dim(wavefunction, my_op * share, share, 2)
    live_rows = lax.dynamic_slice_in_dim(live, my_op * share, share, 1)
    row_window = jnp.transpose(live_rows)[:, :, None, None] & live[None, :, None, :]
    rows = jnp.where(row_window, jnp.transpose(rows, (2, 0, 1, 3)).astype(jnp.float32), 0.0)
    sigma = jnp.where(row_window, summed + energies[None, :, None, None] * rows, 0.0)
    residual = sigma - rayleigh[None, None, :, None] * rows
    return (residual, rayleigh)


def solution(mesh):
    in_specs = (
        P("sec", None, None, None),
        P("op", "sec", None, None),
        P("op", "sec", None, None),
        P("op", None),
        P("sec"),
        P("sec"),
    )
    out_specs = (P("op", "sec", None, None), P())
    return jax.shard_map(body, mesh=mesh, in_specs=in_specs, out_specs=out_specs, check_vma=False)
```

```python
import functools

import jax
import jax.numpy as jnp
from jax import lax
from jax.experimental import pallas as pl
from jax.experimental.pallas import tpu as pltpu
from jax.sharding import PartitionSpec as P

LATE_GROUP = 8
LANES = 128


def start_places(arrays, vec, sems):
    copies = []
    at = 0
    for i, array in enumerate(arrays):
        count = array.shape[0]
        copies.append(pltpu.make_async_copy(array, vec.at[pl.ds(at, count)], sems.at[i]))
        at += count
    for copy in copies:
        copy.start()
    return copies


def early_kernel(slots, left_a, left_b, right_a, right_b, *rest):
    arrays, (sums, vec, sems) = rest[:-3], rest[-3:]
    t = pl.program_id(0)
    half = left_a.shape[0]
    zero = vec.shape[0] - 1

    @pl.when(t == 0)
    def _():
        copies = start_places(arrays, vec, sems)
        vec[zero] = jnp.zeros(vec.shape[1:], vec.dtype)
        for copy in copies:
            copy.wait()

    for k in range(2 * half):
        left, right = (left_a, right_a) if k < half else (left_b, right_b)
        block = vec[jnp.minimum(slots[t * 2 * half + k], zero)]
        inner = jnp.dot(left[k % half, 0], block, preferred_element_type=jnp.float32)
        term = lax.dot_general(
            inner.astype(jnp.bfloat16), right[k % half, 0], (((1,), (1,)), ((), ())),
            preferred_element_type=jnp.float32,
        )
        if k == 0:
            sums[0] = term
        else:
            sums[0] += term


def early_sums(slots, left_a, left_b, right_a, right_b, arrays):
    half, sec_dev, tile, _ = left_a.shape
    total = sum(a.shape[0] for a in arrays)
    ops = pl.BlockSpec((half, 1, tile, tile), lambda t, s: (0, t, 0, 0))
    return pl.pallas_call(
        early_kernel,
        grid_spec=pltpu.PrefetchScalarGridSpec(
            num_scalar_prefetch=1,
            grid=(sec_dev,),
            in_specs=[ops, ops, ops, ops] + [pl.BlockSpec(memory_space=pl.ANY)] * len(arrays),
            out_specs=pl.BlockSpec((1, tile, tile), lambda t, s: (t, 0, 0)),
            scratch_shapes=[
                pltpu.VMEM((total + 1, tile, tile), jnp.bfloat16),
                pltpu.SemaphoreType.DMA((len(arrays),)),
            ],
        ),
        out_shape=jax.ShapeDtypeStruct((sec_dev, tile, tile), jnp.float32),
        compiler_params=pltpu.CompilerParams(vmem_limit_bytes=46 * 2**20),
        cost_estimate=pl.CostEstimate(
            flops=2 * 2 * sec_dev * 2 * half * tile**3,
            bytes_accessed=2 * tile * tile * (total + 8 * half * sec_dev),
            transcendentals=0,
        ),
    )(slots, left_a, left_b, right_a, right_b, *arrays)


def late_kernel(skip, slots, own, early, left_a, left_b, right_a, right_b, *rest):
    arrays, scratch = rest[:-10], rest[-10:]
    out, vec, lefts, rights, acc, blocks, targets, sems, left_sems, right_sems = scratch
    half, sec_dev, tile, _ = left_a.shape
    size = 2 * half
    total = vec.shape[0] - 1
    block_copies = start_places(arrays, vec, sems)
    vec[total] = jnp.zeros(vec.shape[1:], vec.dtype)

    def enlist(pair, count):
        slot = slots[pair]
        mine = slot >= skip

        @pl.when(mine)
        def _():
            t, k = lax.div(pair, size), lax.rem(pair, size)
            blocks[count] = slot - skip
            targets[count] = t

            @pl.when(k < half)
            def _():
                pltpu.make_async_copy(left_a.at[k, t], lefts.at[count], left_sems.at[count]).start()
                pltpu.make_async_copy(right_a.at[k, t], rights.at[count], right_sems.at[count]).start()

            @pl.when(k >= half)
            def _():
                pltpu.make_async_copy(
                    left_b.at[k - half, t], lefts.at[count], left_sems.at[count]
                ).start()
                pltpu.make_async_copy(
                    right_b.at[k - half, t], rights.at[count], right_sems.at[count]
                ).start()

        return count + mine.astype(jnp.int32)

    count = lax.fori_loop(0, sec_dev * size, enlist, jnp.int32(0))
    for i in range(LATE_GROUP):
        blocks[count + i] = total
        targets[count + i] = 0
    acc[...] = early[...]
    for copy in block_copies:
        copy.wait()

    def group(i, carry):
        ats = [i * LATE_GROUP + j for j in range(LATE_GROUP)]
        for at in ats:

            @pl.when(at < count)
            def _():
                pltpu.make_async_copy(left_a.at[0, 0], lefts.at[at], left_sems.at[at]).wait()
                pltpu.make_async_copy(right_a.at[0, 0], rights.at[at], right_sems.at[at]).wait()

        terms = []
        for at in ats:
            place = jnp.where(at < count, at, 0)
            inner = jnp.dot(lefts[place], vec[blocks[at]], preferred_element_type=jnp.float32)
            terms.append(
                lax.dot_general(
                    inner.astype(jnp.bfloat16), rights[place], (((1,), (1,)), ((), ())),
                    preferred_element_type=jnp.float32,
                )
            )
        for at, term in zip(ats, terms):
            acc[targets[at]] += term
        return carry

    lax.fori_loop(0, lax.div(count + LATE_GROUP - 1, LATE_GROUP), group, 0)
    lay_out(acc, own, out)


def lay_out(acc, own, out):
    sec_dev, tile, _ = acc.shape
    op_count, _, lanes = out.shape
    share = tile // op_count
    cuts = tile // lanes
    dots = jnp.zeros((8, tile), jnp.float32)
    for t in range(sec_dev):
        total = acc[t]
        for cut in range(cuts):
            part = total[:, cut * lanes : (cut + 1) * lanes].reshape(op_count, share, lanes)
            row = (t * cuts + cut) * share
            out[:, row : row + share, :] = part.astype(out.dtype)
        mine = own[t].astype(jnp.float32) * total
        dots += jnp.sum(mine.reshape(tile // 8, 8, tile), axis=0)
    row = jnp.sum(dots, axis=0, keepdims=True)
    row = sum(row[:, cut * lanes : (cut + 1) * lanes] for cut in range(cuts))
    high = row.astype(jnp.bfloat16).astype(jnp.float32)
    mid = (row - high).astype(jnp.bfloat16).astype(jnp.float32)
    low = row - high - mid
    at = lax.broadcasted_iota(jnp.int32, (share, lanes), 0)
    slab = jnp.where(at == 0, high, jnp.where(at == 1, mid, jnp.where(at == 2, low, 0.0)))
    slab = slab.astype(out.dtype)
    out[:, sec_dev * cuts * share :, :] = jnp.broadcast_to(slab[None], (op_count, share, lanes))


def late_sums(slots, own, early, left_a, left_b, right_a, right_b, arrays, skip, op_count):
    half, sec_dev, tile, _ = left_a.shape
    size = 2 * half
    share = tile // op_count
    total = sum(a.shape[0] for a in arrays)
    out_shape = (op_count, (sec_dev * (tile // LANES) + 1) * share, LANES)
    whole = pl.BlockSpec(memory_space=pltpu.VMEM)
    return pl.pallas_call(
        functools.partial(late_kernel, skip),
        grid_spec=pltpu.PrefetchScalarGridSpec(
            num_scalar_prefetch=1,
            grid=(),
            in_specs=[whole, whole] + [pl.BlockSpec(memory_space=pl.ANY)] * (4 + len(arrays)),
            out_specs=whole,
            scratch_shapes=[
                pltpu.VMEM((total + 1, tile, tile), jnp.bfloat16),
                pltpu.VMEM((sec_dev * size, tile, tile), jnp.bfloat16),
                pltpu.VMEM((sec_dev * size, tile, tile), jnp.bfloat16),
                pltpu.VMEM((sec_dev, tile, tile), jnp.float32),
                pltpu.SMEM((sec_dev * size + LATE_GROUP,), jnp.int32),
                pltpu.SMEM((sec_dev * size + LATE_GROUP,), jnp.int32),
                pltpu.SemaphoreType.DMA((len(arrays),)),
                pltpu.SemaphoreType.DMA((sec_dev * size,)),
                pltpu.SemaphoreType.DMA((sec_dev * size,)),
            ],
        ),
        out_shape=jax.ShapeDtypeStruct(out_shape, jnp.bfloat16),
        compiler_params=pltpu.CompilerParams(vmem_limit_bytes=46 * 2**20),
        cost_estimate=pl.CostEstimate(
            flops=2 * sec_dev * half * tile**3,
            bytes_accessed=2 * tile * tile * (total + 2 * half * sec_dev),
            transcendentals=0,
        ),
    )(slots, own, early, left_a, left_b, right_a, right_b, *arrays)


def swap(x, axis, mask):
    count = lax.axis_size(axis)
    return lax.ppermute(x, axis, [(i, i ^ mask) for i in range(count)])


def step(x, side, ring, way):
    perm = []
    for op in range(lax.axis_size("op")):
        for at in range(side * side):
            y, x_ = at // side, at % side
            if (op + ring) % 2 == 0:
                x_ = (x_ + way) % side
            else:
                y = (y + way) % side
            perm.append((op * side * side + at, op * side * side + y * side + x_))
    return lax.ppermute(x, ("op", "sec"), perm)


def gather_blocks(own, side, left_ops, right_ops):
    first = lambda b, way: step(b, side, 0, way)
    second = lambda b, way: step(b, side, 1, way)
    left_other = swap(left_ops, "op", 1)
    behind, ahead = first(own, 1), first(own, -1)
    own, behind, ahead, left_other, right = lax.optimization_barrier(
        (own, behind, ahead, left_other, right_ops)
    )
    right_other = swap(right, "op", 1)
    far = first(behind, 1)
    own_a, behind_a, ahead_a = second(own, -1), second(behind, -1), second(ahead, -1)
    own, behind, ahead, far, right_other = lax.optimization_barrier(
        (own, behind, ahead, far, right_other)
    )
    far_a, far_b = second(far, -1), second(far, 1)
    own_b, behind_b, ahead_b = second(own, 1), second(behind, 1), second(ahead, 1)
    own_f, behind_f = second(own_b, 1), second(behind_a, -1)
    ahead_f, far_f = second(ahead_a, -1), second(far_a, -1)
    early = [
        own, behind, ahead, far, own_b, behind_b, ahead_b, own_a, behind_a, ahead_a, far_a,
    ]
    late = [far_b, own_f, behind_f, ahead_f, far_f]
    return early, late, left_other, right_other


def array_place(place):
    return jnp.where(place == 7, 11, jnp.where((place > 7) & (place < 12), place - 1, place))


def ring_place(source, mine, side):
    away = (source - mine) % side
    return jnp.where(away == 0, 0, jnp.where(away == side - 1, 1, away + 1))


def body(wavefunction, left_ops, right_ops, sources, block_dims, energies):
    op_count = lax.axis_size("op")
    sec_count = lax.axis_size("sec")
    my_sec = lax.axis_index("sec")
    my_op = lax.axis_index("op")
    sec_dev, vectors, tile, _ = wavefunction.shape
    share = tile // op_count
    chips = op_count // vectors
    core = my_op % vectors
    side = 4

    own = lax.dynamic_index_in_dim(wavefunction, core, 1, keepdims=False)
    row = lax.broadcasted_iota(jnp.int32, own.shape, 1)
    column = lax.broadcasted_iota(jnp.int32, own.shape, 2)
    inside = jnp.maximum(row, column) < block_dims[:, None, None]
    own = jnp.where(inside, own, jnp.zeros_like(own))

    early, late, left_other, right_other = gather_blocks(own, side, left_ops, right_ops)
    skip = sum(a.shape[0] for a in early)

    table = lax.dynamic_slice_in_dim(sources, my_sec * sec_dev, sec_dev, 1)
    table = jnp.concatenate([table, swap(table, "op", 1)], axis=0)
    table = jnp.transpose(table).reshape(-1)
    device, local = table // sec_dev, table % sec_dev
    in_y = ring_place(device // side, my_sec // side, side)
    in_x = ring_place(device % side, my_sec % side, side)
    place = jnp.where(core == 0, in_y * side + in_x, in_x * side + in_y)
    slots = array_place(place) * sec_dev + local

    live = jnp.arange(tile, dtype=jnp.int32)[None, :] < block_dims[:, None]
    window = live[:, :, None] & live[:, None, :]
    wide = jnp.where(window[:, None], wavefunction, 0).astype(jnp.float32)
    norms = jnp.sum(wide * wide, axis=(2, 3))

    ops = (left_ops, left_other, right_ops, right_other)
    sums = early_sums(slots, *ops, early)
    partial = late_sums(slots, own, sums, *ops, late, skip, op_count)
    parts = lax.all_to_all(partial, "op", split_axis=0, concat_axis=0, tiled=True)
    lanes = LANES
    parts = parts.reshape(chips, vectors, -1, share, lanes)
    numer = jnp.sum(parts[:, :, -1].astype(jnp.float32), axis=(0, 2, 3))
    numer = numer + jnp.sum(energies[:, None] * norms, axis=0)
    scalars = jnp.concatenate([numer, jnp.sum(norms, axis=0)])
    scalars = jnp.pad(scalars[None, None, :], ((0, 0), (0, 7), (0, 128 - 2 * vectors)))
    scalars = jnp.broadcast_to(scalars, (sec_count, 8, 128))
    scalars = lax.all_to_all(scalars, "sec", split_axis=0, concat_axis=0, tiled=True)
    scalars = jnp.sum(scalars[:, 0, : 2 * vectors], axis=0)
    rayleigh = scalars[:vectors] / scalars[vectors:]

    parts = parts[:, :, :-1].reshape(chips, vectors, sec_dev, tile // lanes, share, lanes)
    summed = jnp.sum(parts.astype(jnp.float32), axis=0)
    summed = jnp.concatenate([summed[:, :, cut] for cut in range(tile // lanes)], axis=3)
    summed = jnp.transpose(summed, (2, 1, 0, 3))
    rows = lax.dynamic_slice_in_dim(wavefunction, my_op * share, share, 2)
    live_rows = lax.dynamic_slice_in_dim(live, my_op * share, share, 1)
    row_window = jnp.transpose(live_rows)[:, :, None, None] & live[None, :, None, :]
    rows = jnp.where(row_window, jnp.transpose(rows, (2, 0, 1, 3)).astype(jnp.float32), 0.0)
    sigma = jnp.where(row_window, summed + energies[None, :, None, None] * rows, 0.0)
    residual = sigma - rayleigh[None, None, :, None] * rows
    return (residual, rayleigh)


def solution(mesh):
    in_specs = (
        P("sec", None, None, None),
        P("op", "sec", None, None),
        P("op", "sec", None, None),
        P("op", None),
        P("sec"),
        P("sec"),
    )
    out_specs = (P("op", "sec", None, None), P())
    return jax.shard_map(body, mesh=mesh, in_specs=in_specs, out_specs=out_specs, check_vma=False)
```
